32 devices in a mesh: kern: 2 (over core), ty: 8 (over z, x), tx: 2 (over y).
Axes of the slice: x: 2, y: 2, z: 4, core: 2. Of those that a mesh axis runs over, the one named last changes fastest.
Arguments:
- mask: float32 [2048, 512], P('ty', 'tx'), may hold values from -1 to 1
- target: int32 [2048, 512], P('ty', 'tx'), may hold values 0 or 1
- spectra: float32 [2, 24, 128, 128], P(None, 'kern'), may hold values from -4.5 to 4.5
Outputs:
- resist: float32 [2048, 512], P('ty', 'tx')
- mask_grad: float32 [2048, 512], P('ty', 'tx')
The draws below stay inside these ranges and needn't reach their ends.
All inputs are finite; a program needn't handle non-finite values. No bound on the sum of `target` on one device may be relied on, other than what follows from the above.
Results may differ from the reference program's by a relative error of at most 0.0003.
Values sent between devices are 32-bit elements; how exact they have to be, the bound alone decides.
No kernel may reach another device: no remote copies, remote signals or barrier semaphores. Data moves between devices by JAX's collectives and lax.ppermute only.
A program may use at most 64 MiB of HBM per device.

```python
import math
import jax
import jax.numpy as jnp
from jax import lax

TILE = 256
HALO = 64
BAND = 128
KERNELS = 24
NY = 2048
NX = 512


def with_ends(drawn, rng, low, largest):
    spot = [jax.random.randint(jax.random.fold_in(rng, axis), (), 0, length) for axis, length in enumerate(drawn.shape)]
    longest = drawn.shape.index(max(drawn.shape))
    beside = spot[:longest] + [(spot[longest] + 1) % drawn.shape[longest]] + spot[longest + 1:]
    return drawn.at[tuple(spot)].set(low).at[tuple(beside)].set(largest)


def steps_of(stream_key, dims, pieces, low, top_value):
    level = 1.0
    for position, parts in pieces:
        heights = jax.random.uniform(jax.random.fold_in(jax.random.fold_in(stream_key, 6), position), (parts,), jnp.float32, low / len(pieces), top_value / len(pieces))
        level = level * jnp.repeat(jnp.exp(heights), dims[position] // parts).reshape((-1,) + (1,) * (len(dims) - 1 - position))
    return level


def normal_values(stream_key, dims, spread, most, pieces=(), kind=jnp.bfloat16):
    gain = steps_of(stream_key, dims, pieces, -0.22, 0.18) if pieces else 1.0
    array = jax.random.normal(stream_key, dims, jnp.float32) * spread * gain
    return jnp.minimum(jnp.maximum(array, -most), most).astype(kind)


def setup_inputs(seed: int = 0) -> dict:
    seeds = jax.random.split(jax.random.key(seed), 4)
    mask = jnp.clip(jax.random.uniform(seeds[0], (NY, NX), jnp.float32, -1.0, 1.0) * steps_of(seeds[0], (NY, NX), ((0, 8), (1, 2)), -0.4, 0.0), -1.0, 1.0)
    target = with_ends((jax.random.randint(seeds[1], (NY, NX), 0, 2) < 1).astype(jnp.int32), jax.random.fold_in(seeds[1], 1), 0, 1)
    spectra = normal_values(seeds[2], (2, KERNELS, BAND, BAND), 0.75, 4.5, ((1, 2),), jnp.float32)
    return dict(mask=mask, target=target, spectra=spectra)


STEEP = 8.0
LEVEL = 1.0


def matmul(pattern, first, second):
    return jnp.einsum(pattern, first.astype(jnp.float32), second.astype(jnp.float32), precision=lax.Precision.HIGHEST, preferred_element_type=jnp.float32)


def make_tables(band_size, window_size, tile_size, margin):
    frequency = jnp.arange(band_size, dtype=jnp.int32) - band_size // 2
    positions = jnp.arange(window_size, dtype=jnp.int32)
    centred = jnp.arange(tile_size, dtype=jnp.int32) + margin
    angle_unit = 2.0 * math.pi / window_size
    outer_angle = jnp.mod(frequency[:, None] * positions[None, :], window_size).astype(jnp.float32) * angle_unit
    inner_angle = jnp.mod(centred[:, None] * frequency[None, :], window_size).astype(jnp.float32) * angle_unit
    return jnp.cos(outer_angle), -jnp.sin(outer_angle), jnp.cos(inner_angle), jnp.sin(inner_angle)


def window_spectrum(windows, tables):
    fwd_re, fwd_im, inv_re, inv_im = tables
    half_re = matmul("uy,tyx->tux", fwd_re, windows)
    half_im = matmul("uy,tyx->tux", fwd_im, windows)
    spec_re = matmul("tux,vx->tuv", half_re, fwd_re) - matmul("tux,vx->tuv", half_im, fwd_im)
    spec_im = matmul("tux,vx->tuv", half_re, fwd_im) + matmul("tux,vx->tuv", half_im, fwd_re)
    return spec_re, spec_im


def kernel_fields(spec_re, spec_im, kern_re, kern_im, tables, scale):
    fwd_re, fwd_im, inv_re, inv_im = tables
    prod_re = spec_re[:, None] * kern_re[None] - spec_im[:, None] * kern_im[None]
    prod_im = spec_re[:, None] * kern_im[None] + spec_im[:, None] * kern_re[None]
    rows_re = matmul("yu,tkuv->tkyv", inv_re, prod_re) - matmul("yu,tkuv->tkyv", inv_im, prod_im)
    rows_im = matmul("yu,tkuv->tkyv", inv_re, prod_im) + matmul("yu,tkuv->tkyv", inv_im, prod_re)
    field_re = (matmul("tkyv,xv->tkyx", rows_re, inv_re) - matmul("tkyv,xv->tkyx", rows_im, inv_im)) * scale
    field_im = (matmul("tkyv,xv->tkyx", rows_re, inv_im) + matmul("tkyv,xv->tkyx", rows_im, inv_re)) * scale
    return field_re, field_im


def resist_terms(intensity, goal):
    resist = jax.nn.sigmoid(STEEP * (intensity - LEVEL))
    weight = 2.0 * (resist - goal.astype(jnp.float32)) * STEEP * resist * (1.0 - resist)
    return resist, weight


def back_spectrum(weight, field_re, field_im, kern_re, kern_im, tables, scale):
    fwd_re, fwd_im, inv_re, inv_im = tables
    load_re = weight[:, None] * field_re
    load_im = weight[:, None] * field_im
    cols_re = matmul("tkyx,xv->tkyv", load_re, inv_re) + matmul("tkyx,xv->tkyv", load_im, inv_im)
    cols_im = matmul("tkyx,xv->tkyv", load_im, inv_re) - matmul("tkyx,xv->tkyv", load_re, inv_im)
    spread_re = matmul("yu,tkyv->tkuv", inv_re, cols_re) + matmul("yu,tkyv->tkuv", inv_im, cols_im)
    spread_im = matmul("yu,tkyv->tkuv", inv_re, cols_im) - matmul("yu,tkyv->tkuv", inv_im, cols_re)
    back_re = jnp.sum(kern_re[None] * spread_re + kern_im[None] * spread_im, axis=1) * scale
    back_im = jnp.sum(kern_re[None] * spread_im - kern_im[None] * spread_re, axis=1) * scale
    return back_re, back_im


def window_gradient(back_re, back_im, tables):
    fwd_re, fwd_im, inv_re, inv_im = tables
    lift_re = matmul("uy,tuv->tyv", fwd_re, back_re) + matmul("uy,tuv->tyv", fwd_im, back_im)
    lift_im = matmul("uy,tuv->tyv", fwd_re, back_im) - matmul("uy,tuv->tyv", fwd_im, back_re)
    return 2.0 * (matmul("tyv,vx->tyx", lift_re, fwd_re) + matmul("tyv,vx->tyx", lift_im, fwd_im))


def reference(mask, target, spectra):
    window_size = TILE + 2 * HALO
    tables = make_tables(BAND, window_size, TILE, HALO)
    scale = 1.0 / (window_size * window_size)
    widened = jnp.pad(mask, HALO)
    tile_rows = NY // TILE
    tile_cols = NX // TILE
    kern_re = spectra[0]
    kern_im = spectra[1]

    def one_tile(number):
        number = number.astype(jnp.int32)
        row_at = ((number // tile_cols) * TILE).astype(jnp.int32)
        col_at = ((number % tile_cols) * TILE).astype(jnp.int32)
        window = lax.dynamic_slice(widened, (row_at, col_at), (window_size, window_size))[None]
        goal = lax.dynamic_slice(target, (row_at, col_at), (TILE, TILE))[None]
        spec_re, spec_im = window_spectrum(window, tables)
        field_re, field_im = kernel_fields(spec_re, spec_im, kern_re, kern_im, tables, scale)
        intensity = jnp.sum(field_re * field_re + field_im * field_im, axis=1)
        resist, weight = resist_terms(intensity, goal)
        back_re, back_im = back_spectrum(weight, field_re, field_im, kern_re, kern_im, tables, scale)
        return resist[0], window_gradient(back_re, back_im, tables)[0]

    numbers = jnp.arange(tile_rows * tile_cols, dtype=jnp.int32)
    resist_tiles, grad_tiles = lax.map(one_tile, numbers)
    resist = resist_tiles.reshape(tile_rows, tile_cols, TILE, TILE).transpose(0, 2, 1, 3).reshape(NY, NX)

    def place(number, total):
        number = jnp.asarray(number).astype(jnp.int32)
        row_at = ((number // tile_cols) * TILE).astype(jnp.int32)
        col_at = ((number % tile_cols) * TILE).astype(jnp.int32)
        current = lax.dynamic_slice(total, (row_at, col_at), (window_size, window_size))
        return lax.dynamic_update_slice(total, current + grad_tiles[number], (row_at, col_at))

    total = lax.fori_loop(0, tile_rows * tile_cols, place, jnp.zeros(widened.shape, jnp.float32))
    return resist, total[HALO:HALO + NY, HALO:HALO + NX]
```

```python
import functools
import math

import jax
import jax.numpy as jnp
import ml_dtypes
import numpy as np
from jax import lax
from jax.experimental import pallas as pl
from jax.experimental.pallas import tpu as pltpu
from jax.sharding import PartitionSpec as P

HALO = 64
STEEP = 8.0
LEVEL = 1.0
F32 = jnp.float32
BF16 = jnp.bfloat16
VMEM_LIMIT = 52 * 1024 * 1024


def table_parts(table):
    high = table.astype(np.float32).astype(ml_dtypes.bfloat16)
    low = (table - high.astype(np.float64)).astype(np.float32).astype(ml_dtypes.bfloat16)
    return (high, low)


def make_tables(band, tile):
    window = tile + 2 * HALO
    frequency = np.arange(band) - band // 2
    positions = np.concatenate([np.arange(HALO, window), np.arange(HALO)])
    angle = ((positions[:, None] * frequency[None, :]) % window) * (2.0 * math.pi / window)
    cosine, sine = (np.cos(angle), np.sin(angle))
    table = np.block([[cosine, -sine], [sine, cosine]])
    return table_parts(table) + table_parts(np.ascontiguousarray(table.T))


def split(value):
    high = value.astype(BF16)
    return (high, (value - high.astype(F32)).astype(BF16))


def dot(first, second):
    def product(a, b):
        return jnp.dot(a, b, preferred_element_type=F32)

    return product(first[0], second[0]) + (
        product(first[1], second[0]) + product(first[0], second[1])
    )


def own_rows(refs, window, tile):
    return tuple(jnp.concatenate([r[:tile], r[window : window + tile]], axis=0) for r in refs)


def own_columns(refs, window, tile):
    return tuple(jnp.concatenate([r[:, :tile], r[:, window : window + tile]], axis=1) for r in refs)


class Place:
    def __init__(self):
        core, ty, tx = (lax.axis_index(name) for name in ("kern", "ty", "tx"))
        self.down = lax.rem(ty + core, 2) == 0
        self.has_below = ty < lax.axis_size("ty") - 1
        self.has_above = ty > 0
        self.has_right = tx < lax.axis_size("tx") - 1
        self.has_left = tx > 0
        self.tx = tx

    def rightward(self, turn):
        return lax.rem(self.tx + turn, 2) == 0


def side_turns():
    count = lax.axis_size("tx")
    return 0 if count == 1 else 1 if count == 2 else 2


def partners(count, turn):
    found = [((i - turn) ^ 1) + turn for i in range(count)]
    return [j if 0 <= j < count else i for i, j in enumerate(found)]


def row_pairs(side_turn):
    rows, columns = (lax.axis_size("ty"), lax.axis_size("tx"))
    beside = partners(columns, 0)
    moved = list(range(columns)) if side_turn is None else partners(columns, side_turn)
    pairs = []
    for core in range(2):
        met = partners(rows, core)
        for ty in range(rows):
            for tx in range(columns):
                to = (met[ty], moved[tx]) if met[ty] != ty else (ty, beside[tx])
                base = core * rows * columns
                pairs.append((base + ty * columns + tx, base + to[0] * columns + to[1]))
    return pairs


def swap_cores(value):
    return lax.ppermute(value, "kern", [(0, 1), (1, 0)])


def swap_rows(value, side_turn=None):
    return lax.ppermute(value, ("kern", "ty", "tx"), row_pairs(side_turn))


def swap_side(value, turn):
    return lax.ppermute(value, "tx", list(enumerate(partners(lax.axis_size("tx"), turn))))


def merge_sides(place, pieces, lanes_of_right):
    width = pieces[0].shape[1]
    lane = lax.broadcasted_iota(jnp.int32, pieces[0].shape, 1)
    from_right = lane < HALO if lanes_of_right == 0 else lane >= width - HALO
    total = jnp.zeros(pieces[0].shape, F32)
    for turn, piece in enumerate(pieces):
        right = place.rightward(turn)
        there = jnp.where(right, place.has_right, place.has_left)
        mine = jnp.logical_and(from_right == right, there)
        total = total + jnp.where(mine, piece, 0.0)
    return total


def forward_kernel(turns, tile, band, scale, *refs):
    mask_ref, row_mine, row_other = refs[:3]
    sides = refs[3 : 3 + turns]
    corners_mine = refs[3 + turns : 3 + 2 * turns]
    corners_other = refs[3 + 2 * turns : 3 + 3 * turns]
    spectra_ref, g_high, g_low, t_high, t_low, intensity_ref, field_ref = refs[3 + 3 * turns :]
    place = Place()
    window = tile + 2 * HALO
    kernels = spectra_ref.shape[1]

    def rows_of(own, mine, other):
        below = jnp.where(jnp.logical_and(place.down, place.has_below), mine, 0.0) + jnp.where(
            jnp.logical_and(jnp.logical_not(place.down), place.has_below), other, 0.0
        )
        above = jnp.where(jnp.logical_and(place.down, place.has_above), other, 0.0) + jnp.where(
            jnp.logical_and(jnp.logical_not(place.down), place.has_above), mine, 0.0
        )
        return jnp.concatenate([own, below, above], axis=0)

    image = rows_of(mask_ref[...], row_mine[...], row_other[...])
    if turns:
        side = rows_of(
            merge_sides(place, [r[...] for r in sides], 0),
            merge_sides(place, [r[...] for r in corners_mine], 0),
            merge_sides(place, [r[...] for r in corners_other], 0),
        )
    else:
        side = jnp.zeros((window, 2 * HALO), F32)
    image = jnp.concatenate([image, side], axis=1)
    half = dot((t_high[:, :window], t_low[:, :window]), split(image))
    half = jnp.concatenate([half[:band], half[band:]], axis=1)
    spectrum = dot(split(half), (g_high[...], g_low[...])) * scale
    spec_re, spec_im = (spectrum[:, :band], spectrum[:, band:])

    first = own_rows((g_high, g_low), window, tile)
    second = own_columns((t_high, t_low), window, tile)
    total = None
    for start in range(0, kernels, 2):
        group = range(start, min(start + 2, kernels))
        shifted = []
        for k in group:
            kern_re, kern_im = (spectra_ref[0, k], spectra_ref[1, k])
            shifted.append(
                jnp.concatenate(
                    [spec_re * kern_re - spec_im * kern_im, spec_re * kern_im + spec_im * kern_re],
                    axis=0,
                )
            )
        rows = dot(first, split(jnp.concatenate(shifted, axis=1)))
        for place_in, k in enumerate(group):
            part = rows[:, place_in * band : (place_in + 1) * band]
            part = jnp.concatenate([part[:tile], part[tile:]], axis=1)
            field = dot(split(part), second)
            field_ref[k] = field
            power = field[:, :tile] * field[:, :tile] + field[:, tile:] * field[:, tile:]
            total = power if total is None else total + power
    intensity_ref[...] = total


def backward_kernel(tile, band, scale, *refs):
    (part_mine, part_other, target_ref, spectra_ref, field_ref) = refs[:5]
    g_high, g_low, t_high, t_low, resist_ref, back_ref = refs[5:]
    window = tile + 2 * HALO
    kernels = spectra_ref.shape[1]
    intensity = part_mine[...] + part_other[...]
    resist = 1.0 / (1.0 + jnp.exp(-STEEP * (intensity - LEVEL)))
    resist_ref[...] = resist
    weight = 2.0 * (resist - target_ref[...].astype(F32)) * STEEP * resist * (1.0 - resist)
    first = own_rows((g_high, g_low), window, tile)
    second = own_columns((t_high, t_low), window, tile)
    weight = jnp.concatenate([weight, weight], axis=1)
    back_re = jnp.zeros((band, band), F32)
    back_im = jnp.zeros((band, band), F32)
    for start in range(0, kernels, 2):
        group = range(start, min(start + 2, kernels))
        columns = []
        for k in group:
            column = dot(split(field_ref[k] * weight), first)
            columns.append(jnp.concatenate([column[:, :band], column[:, band:]], axis=0))
        spread = dot(second, split(jnp.concatenate(columns, axis=1)))
        for place_in, k in enumerate(group):
            part = spread[:, place_in * band : (place_in + 1) * band]
            part_re, part_im = (part[:band], part[band:])
            kern_re, kern_im = (spectra_ref[0, k], spectra_ref[1, k])
            back_re = back_re + (kern_re * part_re + kern_im * part_im)
            back_im = back_im + (kern_re * part_im - kern_im * part_re)
    back_ref[...] = jnp.concatenate([back_re, back_im], axis=1) * scale


def gradient_kernel(tile, band, *refs):
    back_mine, back_other, g_high, g_low, t_high, t_low = refs[:6]
    core_ref, row_ref, side_ref, corner_ref = refs[6:]
    place = Place()
    window = tile + 2 * HALO
    back = 2.0 * (back_mine[...] + back_other[...])
    back = jnp.concatenate([back[:, :band], back[:, band:]], axis=0)
    lift = dot((g_high[...], g_low[...]), split(back))
    lift = jnp.concatenate([lift[:window], lift[window:]], axis=1)
    grad = dot(split(lift), (t_high[:, :window], t_low[:, :window]))
    after, before = (grad[tile : tile + HALO], grad[tile + HALO :])
    strip = jnp.where(place.down, after, before)
    row_ref[...] = strip[:, :tile]
    corner_ref[...] = strip[:, tile:]
    side_ref[...] = grad[:tile, tile:]
    core_ref[...] = grad[:tile, :tile]


def merge_kernel(turns, tile, *refs):
    core_ref, row_mine, row_other = refs[:3]
    sides = refs[3 : 3 + turns]
    corners_mine = refs[3 + turns : 3 + 2 * turns]
    corners_other = refs[3 + 2 * turns : 3 + 3 * turns]
    out_ref = refs[3 + 3 * turns]
    place = Place()

    def spread(pieces):
        merged = merge_sides(place, pieces, 1)
        lane = lax.broadcasted_iota(jnp.int32, merged.shape, 1)
        first = jnp.where(lane < HALO, merged, 0.0)
        last = jnp.where(lane >= HALO, merged, 0.0)
        middle = jnp.zeros((merged.shape[0], tile - 2 * merged.shape[1]), F32)
        return jnp.concatenate([first, middle, last] if middle.shape[1] else [first, last], axis=1)

    total = core_ref[...]
    mine, other = (row_mine[...], row_other[...])
    if turns:
        total = total + spread([r[...] for r in sides])
        mine = mine + spread([r[...] for r in corners_mine])
        other = other + spread([r[...] for r in corners_other])
    bottom = jnp.where(place.has_below, jnp.where(place.down, mine, other), 0.0)
    top = jnp.where(place.has_above, jnp.where(place.down, other, mine), 0.0)
    out_ref[:HALO] = total[:HALO] + top
    out_ref[HALO : tile - HALO] = total[HALO : tile - HALO]
    out_ref[tile - HALO :] = total[tile - HALO :] + bottom


def call(kernel, out_shape, operands):
    spec = pl.BlockSpec(memory_space=pltpu.VMEM)
    return pl.pallas_call(
        kernel,
        out_shape=out_shape,
        in_specs=[spec] * len(operands),
        out_specs=jax.tree.map(lambda _: spec, out_shape),
        compiler_params=pltpu.CompilerParams(vmem_limit_bytes=VMEM_LIMIT),
    )(*operands)


def exchange(row, sides, corners):
    turns = side_turns()
    row_mine = swap_rows(row)
    corners_mine = [swap_rows(corners[turn], turn) for turn in range(turns)]
    side = [swap_side(sides[turn], turn) for turn in range(turns)]
    row_other = swap_cores(row_mine)
    corners_other = [swap_cores(corner) for corner in corners_mine]
    return [row_mine, row_other, *side, *corners_mine, *corners_other]


def on_device(mask, target, spectra):
    tile = mask.shape[0]
    band = spectra.shape[-1]
    window = tile + 2 * HALO
    scale = 1.0 / (window * window)
    tables = [jnp.asarray(t) for t in make_tables(band, tile)]
    place = Place()
    turns = side_turns()

    row_start = jnp.where(place.down, tile - HALO, 0)
    row = lax.dynamic_slice(mask, (row_start, 0), (HALO, tile))
    starts = [jnp.where(place.rightward(turn), tile - 2 * HALO, 0) for turn in range(turns)]
    sides = [lax.dynamic_slice(mask, (0, start), (tile, 2 * HALO)) for start in starts]
    corners = [lax.dynamic_slice(mask, (row_start, start), (HALO, 2 * HALO)) for start in starts]
    received = exchange(row, sides, corners)

    image = jax.ShapeDtypeStruct((tile, tile), F32)
    intensity, field = call(
        functools.partial(forward_kernel, turns, tile, band, scale),
        (image, pltpu.VMEM((spectra.shape[1], tile, 2 * tile), F32)),
        [mask, *received, spectra, *tables],
    )
    resist, back = call(
        functools.partial(backward_kernel, tile, band, scale),
        (image, jax.ShapeDtypeStruct((band, 2 * band), F32)),
        [intensity, swap_cores(intensity), target, spectra, field, *tables],
    )
    core, row, side, corner = call(
        functools.partial(gradient_kernel, tile, band),
        (
            image,
            jax.ShapeDtypeStruct((HALO, tile), F32),
            jax.ShapeDtypeStruct((tile, 2 * HALO), F32),
            jax.ShapeDtypeStruct((HALO, 2 * HALO), F32),
        ),
        [back, swap_cores(back), *tables],
    )
    received = exchange(row, [side] * turns, [corner] * turns)
    grad = call(functools.partial(merge_kernel, turns, tile), image, [core, *received])
    return (resist, grad)


def solution(mesh):
    return jax.shard_map(
        on_device,
        mesh=mesh,
        in_specs=(P("ty", "tx"), P("ty", "tx"), P(None, "kern", None, None)),
        out_specs=(P("ty", "tx"), P("ty", "tx")),
        check_vma=False,
    )
```

```python
import functools
import math

import jax
import jax.numpy as jnp
import ml_dtypes
import numpy as np
from jax import lax
from jax.experimental import pallas as pl
from jax.experimental.pallas import tpu as pltpu
from jax.sharding import PartitionSpec as P

HALO = 64
STEEP = 8.0
LEVEL = 1.0
F32 = jnp.float32
BF16 = jnp.bfloat16
VMEM_LIMIT = 24 * 1024 * 1024


def table_parts(table):
    high = table.astype(np.float32).astype(ml_dtypes.bfloat16)
    low = (table - high.astype(np.float64)).astype(np.float32).astype(ml_dtypes.bfloat16)
    return (high, low)


def make_tables(band, tile):
    window = tile + 2 * HALO
    frequency = np.arange(band) - band // 2
    positions = np.concatenate([np.arange(HALO, window), np.arange(HALO)])
    angle = ((positions[:, None] * frequency[None, :]) % window) * (2.0 * math.pi / window)
    cosine, sine = (np.cos(angle), np.sin(angle))
    table = np.block([[cosine, -sine], [sine, cosine]])
    return table_parts(np.ascontiguousarray(table.T)) + table_parts(table)


def split(value):
    high = value.astype(BF16)
    return (high, (value - high.astype(F32)).astype(BF16))


def dot(first, second):
    def product(a, b):
        return jnp.dot(a, b, preferred_element_type=F32)

    return product(first[0], second[0]) + (
        product(first[1], second[0]) + product(first[0], second[1])
    )


def own_rows(refs, window, tile):
    return tuple(jnp.concatenate([r[:tile], r[window : window + tile]], axis=0) for r in refs)


def own_columns(refs, window, tile):
    return tuple(jnp.concatenate([r[:, :tile], r[:, window : window + tile]], axis=1) for r in refs)


class Place:
    def __init__(self):
        core, ty, tx = (lax.axis_index(name) for name in ("kern", "ty", "tx"))
        self.down = lax.rem(ty + core, 2) == 0
        self.has_below = ty < lax.axis_size("ty") - 1
        self.has_above = ty > 0
        self.has_right = tx < lax.axis_size("tx") - 1
        self.has_left = tx > 0
        self.tx = tx

    def rightward(self, turn):
        return lax.rem(self.tx + turn, 2) == 0


def side_turns():
    count = lax.axis_size("tx")
    return 0 if count == 1 else 1 if count == 2 else 2


def partners(count, turn):
    found = [((i - turn) ^ 1) + turn for i in range(count)]
    return [j if 0 <= j < count else i for i, j in enumerate(found)]


def row_pairs(side_turn):
    rows, columns = (lax.axis_size("ty"), lax.axis_size("tx"))
    beside = partners(columns, 0)
    moved = list(range(columns)) if side_turn is None else partners(columns, side_turn)
    pairs = []
    for core in range(2):
        met = partners(rows, core)
        for ty in range(rows):
            for tx in range(columns):
                to = (met[ty], moved[tx]) if met[ty] != ty else (ty, beside[tx])
                base = core * rows * columns
                pairs.append((base + ty * columns + tx, base + to[0] * columns + to[1]))
    return pairs


def swap_cores(value):
    return lax.ppermute(value, "kern", [(0, 1), (1, 0)])


def swap_rows(value, side_turn=None):
    return lax.ppermute(value, ("kern", "ty", "tx"), row_pairs(side_turn))


def swap_side(value, turn):
    return lax.ppermute(value, "tx", list(enumerate(partners(lax.axis_size("tx"), turn))))


def half_turn(value):
    return pltpu.roll(value, HALO, 1)


def pack(block, upper):
    rows = block.shape[0] // 2
    first, last = (block[:rows], block[rows:])
    lane = lax.broadcasted_iota(jnp.int32, first.shape, 1)
    return jnp.where(
        lane < HALO,
        jnp.where(upper, half_turn(first), first),
        jnp.where(upper, last, half_turn(last)),
    )


def unpack(packed, upper):
    turned = half_turn(packed)
    return jnp.concatenate(
        [jnp.where(upper, turned, packed), jnp.where(upper, packed, turned)], axis=0
    )


def merge_sides(place, refs, right_is_upper):
    total = None
    for turn, ref in enumerate(refs):
        right = place.rightward(turn)
        there = jnp.where(right, place.has_right, place.has_left)
        upper = right if right_is_upper else jnp.logical_not(right)
        block = unpack(ref[...], upper)
        lane = lax.broadcasted_iota(jnp.int32, block.shape, 1)
        mine = jnp.logical_and((lane >= HALO) == upper, there)
        block = jnp.where(mine, block, 0.0)
        total = block if total is None else total + block
    return total


def prepare_kernel(turns, tile, mask_ref, kept_ref, row_ref, *refs):
    place = Place()
    block = mask_ref[...]
    kept_ref[...] = block
    strip = jnp.where(place.down, block[tile - HALO :], block[:HALO])
    row_ref[...] = strip
    for turn in range(turns):
        right = place.rightward(turn)
        for source, ref in ((block, refs[turn]), (strip, refs[turns + turn])):
            ref[...] = pack(
                jnp.where(right, source[:, tile - 2 * HALO :], source[:, : 2 * HALO]), right
            )


def own_kernel(tile, kept_ref, *refs):
    count = (len(refs) - 2) // 2
    sources, half_ref, copies, sems = (refs[:count], refs[count], refs[count + 1 : -1], refs[-1])
    moves = [
        pltpu.make_async_copy(source, copy, sems.at[i])
        for i, (source, copy) in enumerate(zip(sources, copies))
    ]
    for move in moves:
        move.start()
    moves[0].wait()
    moves[1].wait()
    half_ref[...] = dot((copies[0][:, :tile], copies[1][:, :tile]), split(kept_ref[...]))
    for move in moves[2:]:
        move.wait()


def forward_kernel(turns, tile, band, scale, *refs):
    half_ref, row_mine, row_other = refs[:3]
    sides = refs[3 : 3 + turns]
    corners_mine = refs[3 + turns : 3 + 2 * turns]
    corners_other = refs[3 + 2 * turns : 3 + 3 * turns]
    t_high, t_low, g_high, g_low, spectra_ref, intensity_ref, field_ref = refs[3 + 3 * turns :]
    place = Place()
    window = tile + 2 * HALO
    kernels = spectra_ref.shape[1]

    def margins(mine, other):
        below = jnp.where(place.has_below, jnp.where(place.down, mine, other), 0.0)
        above = jnp.where(place.has_above, jnp.where(place.down, other, mine), 0.0)
        return jnp.concatenate([below, above], axis=0)

    near = dot(
        (t_high[:, tile:window], t_low[:, tile:window]),
        split(margins(row_mine[...], row_other[...])),
    )
    near = half_ref[...] + near
    if turns:
        side = jnp.concatenate(
            [
                merge_sides(place, sides, False),
                margins(
                    merge_sides(place, corners_mine, False),
                    merge_sides(place, corners_other, False),
                ),
            ],
            axis=0,
        )
        far = dot((t_high[:, :window], t_low[:, :window]), split(side))
    else:
        far = jnp.zeros((near.shape[0], 2 * HALO), F32)
    half = jnp.concatenate([near[:band], far[:band], near[band:], far[band:]], axis=1)
    spectrum = dot(split(half), (g_high[...], g_low[...])) * scale
    spec_re, spec_im = (spectrum[:, :band], spectrum[:, band:])

    first = own_rows((g_high, g_low), window, tile)
    second = own_columns((t_high, t_low), window, tile)
    total = None
    for start in range(0, kernels, 2):
        group = range(start, min(start + 2, kernels))
        shifted = []
        for k in group:
            kern_re, kern_im = (spectra_ref[0, k], spectra_ref[1, k])
            shifted.append(
                jnp.concatenate(
                    [spec_re * kern_re - spec_im * kern_im, spec_re * kern_im + spec_im * kern_re],
                    axis=0,
                )
            )
        rows = dot(first, split(jnp.concatenate(shifted, axis=1)))
        for place_in, k in enumerate(group):
            part = rows[:, place_in * band : (place_in + 1) * band]
            part = jnp.concatenate([part[:tile], part[tile:]], axis=1)
            field = dot(split(part), second)
            field_ref[k] = field
            power = field[:, :tile] * field[:, :tile] + field[:, tile:] * field[:, tile:]
            total = power if total is None else total + power
    intensity_ref[...] = total


def backward_kernel(tile, band, scale, *refs):
    (part_mine, part_other, target_ref, field_ref) = refs[:4]
    t_high, t_low, g_high, g_low, spectra_ref, resist_ref, back_ref = refs[4:]
    window = tile + 2 * HALO
    kernels = spectra_ref.shape[1]
    intensity = part_mine[...] + part_other[...]
    resist = 1.0 / (1.0 + jnp.exp(-STEEP * (intensity - LEVEL)))
    resist_ref[...] = resist
    weight = 2.0 * (resist - target_ref[...].astype(F32)) * STEEP * resist * (1.0 - resist)
    first = own_rows((g_high, g_low), window, tile)
    second = own_columns((t_high, t_low), window, tile)
    weight = jnp.concatenate([weight, weight], axis=1)
    back_re = jnp.zeros((band, band), F32)
    back_im = jnp.zeros((band, band), F32)
    for start in range(0, kernels, 2):
        group = range(start, min(start + 2, kernels))
        columns = []
        for k in group:
            column = dot(split(field_ref[k] * weight), first)
            columns.append(jnp.concatenate([column[:, :band], column[:, band:]], axis=0))
        spread = dot(second, split(jnp.concatenate(columns, axis=1)))
        for place_in, k in enumerate(group):
            part = spread[:, place_in * band : (place_in + 1) * band]
            part_re, part_im = (part[:band], part[band:])
            kern_re, kern_im = (spectra_ref[0, k], spectra_ref[1, k])
            back_re = back_re + (kern_re * part_re + kern_im * part_im)
            back_im = back_im + (kern_re * part_im - kern_im * part_re)
    back_ref[...] = jnp.concatenate([back_re, back_im], axis=1) * scale


def margin_kernel(turns, tile, band, *refs):
    back_mine, back_other, t_high, t_low, g_high, g_low, lift_ref, row_ref = refs[:8]
    place = Place()
    window = tile + 2 * HALO
    back = 2.0 * (back_mine[...] + back_other[...])
    back = jnp.concatenate([back[:, :band], back[:, band:]], axis=0)
    lift = dot((g_high[...], g_low[...]), split(back))
    lift = jnp.concatenate([lift[:window], lift[window:]], axis=1)
    lift_ref[...] = lift[:tile]
    strip = jnp.where(place.down, lift[tile : tile + HALO], lift[tile + HALO :])
    strip = dot(split(strip), (t_high[:, :window], t_low[:, :window]))
    row_ref[...] = strip[:, :tile]
    if turns:
        side = dot(split(lift[:tile]), (t_high[:, tile:window], t_low[:, tile:window]))
        for turn in range(turns):
            upper = jnp.logical_not(place.rightward(turn))
            refs[8 + turn][...] = pack(side, upper)
            refs[8 + turns + turn][...] = pack(strip[:, tile:], upper)


def core_kernel(tile, lift_ref, t_high, t_low, core_ref):
    core_ref[...] = dot(split(lift_ref[...]), (t_high[:, :tile], t_low[:, :tile]))


def merge_kernel(turns, tile, *refs):
    core_ref, row_mine, row_other = refs[:3]
    sides = refs[3 : 3 + turns]
    corners_mine = refs[3 + turns : 3 + 2 * turns]
    corners_other = refs[3 + 2 * turns : 3 + 3 * turns]
    out_ref = refs[3 + 3 * turns]
    place = Place()

    def spread(refs):
        merged = merge_sides(place, refs, True)
        lane = lax.broadcasted_iota(jnp.int32, merged.shape, 1)
        first = jnp.where(lane < HALO, merged, 0.0)
        last = jnp.where(lane >= HALO, merged, 0.0)
        middle = jnp.zeros((merged.shape[0], tile - 2 * merged.shape[1]), F32)
        return jnp.concatenate([first, middle, last] if middle.shape[1] else [first, last], axis=1)

    total = core_ref[...]
    mine, other = (row_mine[...], row_other[...])
    if turns:
        total = total + spread(sides)
        mine = mine + spread(corners_mine)
        other = other + spread(corners_other)
    bottom = jnp.where(place.has_below, jnp.where(place.down, mine, other), 0.0)
    top = jnp.where(place.has_above, jnp.where(place.down, other, mine), 0.0)
    out_ref[:HALO] = total[:HALO] + top
    out_ref[HALO : tile - HALO] = total[HALO : tile - HALO]
    out_ref[tile - HALO :] = total[tile - HALO :] + bottom


def call(kernel, out_shape, operands, in_hbm=(), **options):
    in_vmem = pl.BlockSpec(memory_space=pltpu.VMEM)
    anywhere = pl.BlockSpec(memory_space=pltpu.HBM)
    operands = [
        pltpu.with_memory_space_constraint(operand, pltpu.HBM) if i in in_hbm else operand
        for i, operand in enumerate(operands)
    ]
    return pl.pallas_call(
        kernel,
        out_shape=out_shape,
        in_specs=[anywhere if i in in_hbm else in_vmem for i in range(len(operands))],
        out_specs=jax.tree.map(lambda _: in_vmem, out_shape),
        compiler_params=pltpu.CompilerParams(vmem_limit_bytes=VMEM_LIMIT),
        **options,
    )(*operands)


def exchange(row, sides, corners, beside):
    turns = side_turns()
    row_mine = swap_rows(row)
    corners_mine = [swap_rows(corners[turn], turn) for turn in range(turns)]
    side = [swap_side(sides[turn], turn) for turn in range(turns)]
    row_mine, corners_mine, beside = lax.optimization_barrier((row_mine, corners_mine, beside))
    row_other = swap_cores(row_mine)
    corners_other = [swap_cores(corner) for corner in corners_mine]
    return ([row_mine, row_other, *side, *corners_mine, *corners_other], beside)


def on_device(mask, target, spectra):
    tile = mask.shape[0]
    band = spectra.shape[-1]
    window = tile + 2 * HALO
    scale = 1.0 / (window * window)
    turns = side_turns()
    image = pltpu.VMEM((tile, tile), F32)
    strips = (
        pltpu.VMEM((HALO, tile), F32),
        *[pltpu.VMEM((tile // 2, 2 * HALO), F32)] * turns,
        *[pltpu.VMEM((HALO // 2, 2 * HALO), F32)] * turns,
    )

    kept, row, *packed = call(
        functools.partial(prepare_kernel, turns, tile), (image, *strips), [mask]
    )
    sources = [jnp.asarray(t) for t in make_tables(band, tile)] + [spectra]
    half, *shared = call(
        functools.partial(own_kernel, tile),
        (
            pltpu.VMEM((2 * band, tile), F32),
            *[pltpu.VMEM(source.shape, source.dtype) for source in sources],
        ),
        [kept, *sources],
        in_hbm=range(1, 1 + len(sources)),
        scratch_shapes=[pltpu.SemaphoreType.DMA((len(sources),))],
    )
    received, half = exchange(row, packed[:turns], packed[turns:], half)
    intensity, field = call(
        functools.partial(forward_kernel, turns, tile, band, scale),
        (image, pltpu.VMEM((spectra.shape[1], tile, 2 * tile), F32)),
        [half, *received, *shared],
    )
    resist, back = call(
        functools.partial(backward_kernel, tile, band, scale),
        (jax.ShapeDtypeStruct((tile, tile), F32), pltpu.VMEM((band, 2 * band), F32)),
        [intensity, swap_cores(intensity), target, field, *shared],
    )
    lift, row, *packed = call(
        functools.partial(margin_kernel, turns, tile, band),
        (pltpu.VMEM((tile, 2 * band), F32), *strips),
        [back, swap_cores(back), *shared[:4]],
    )
    core = call(functools.partial(core_kernel, tile), image, [lift, *shared[:2]])
    received, core = exchange(row, packed[:turns], packed[turns:], core)
    grad = call(
        functools.partial(merge_kernel, turns, tile),
        jax.ShapeDtypeStruct((tile, tile), F32),
        [core, *received],
    )
    return (resist, grad)


def solution(mesh):
    return jax.shard_map(
        on_device,
        mesh=mesh,
        in_specs=(P("ty", "tx"), P("ty", "tx"), P(None, "kern", None, None)),
        out_specs=(P("ty", "tx"), P("ty", "tx")),
        check_vma=False,
    )
```

```python
import functools
import math

import jax
import jax.numpy as jnp
import ml_dtypes
import numpy as np
from jax import lax
from jax.experimental import pallas as pl
from jax.experimental.pallas import tpu as pltpu
from jax.sharding import PartitionSpec as P

HALO = 64
STEEP = 8.0
LEVEL = 1.0
F32 = jnp.float32
BF16 = jnp.bfloat16
VMEM_LIMIT = 24 * 1024 * 1024


def table_parts(table):
    high = table.astype(np.float32).astype(ml_dtypes.bfloat16)
    low = (table - high.astype(np.float64)).astype(np.float32).astype(ml_dtypes.bfloat16)
    return (high, low)


def signed_order(count):
    return np.concatenate([np.arange(count // 2, count), np.arange(count // 2)[::-1]])


def permutation(count):
    return np.eye(count)[signed_order(count)].astype(ml_dtypes.bfloat16)


def make_tables(band, tile):
    window = tile + 2 * HALO
    unit = 2.0 * math.pi / window
    natural = np.arange(band) - band // 2
    signed = signed_order(band) - band // 2
    places = np.concatenate([np.arange(HALO, window), np.arange(HALO)]) - (window - 1) / 2

    def blocks(frequency):
        angle = places[:, None] * frequency[None, :] * unit
        cosine, sine = (np.cos(angle), np.sin(angle))
        return np.block([[cosine, -sine], [sine, cosine]])

    rows = blocks(natural)
    columns = np.ascontiguousarray(blocks(signed).T)
    spectrum_rows = np.ascontiguousarray(rows.T[:, :window])

    pixel = np.arange(tile // 2) + 0.5
    angle = (natural + 0.5)[:, None] * pixel[None, :] * unit
    lift = np.concatenate([np.cos(angle), np.sin(angle)], axis=1)
    both = np.concatenate([pixel, -pixel])[:, None] * (natural + 0.5)[None, :] * unit
    drop = np.concatenate([np.cos(both), np.sin(both)], axis=1)
    half = pixel[:, None] * (np.arange(band // 2) + 0.5)[None, :] * unit
    cosine, sine = (np.cos(half), np.sin(half))
    fold = np.block([[cosine.T, sine.T], [cosine.T, -sine.T]])

    def first(table):
        high, low = table_parts(table)
        return np.concatenate([high, low, high], axis=1)

    def second(table):
        high, low = table_parts(table)
        return np.concatenate([high, high, low], axis=0)

    return {
        "window": table_parts(spectrum_rows) + table_parts(columns) + table_parts(rows),
        "forward": (second(lift), first(cosine), first(sine)),
        "backward": (np.concatenate(table_parts(fold), axis=0), second(drop)),
        "order": (permutation(band), permutation(tile), np.ascontiguousarray(permutation(tile).T)),
    }


def split(value):
    high = value.astype(BF16)
    return (high, (value - high.astype(F32)).astype(BF16))


def product(a, b):
    return jnp.dot(a, b, preferred_element_type=F32)


def product_turned(a, b):
    return lax.dot_general(a, b, (((1,), (1,)), ((), ())), preferred_element_type=F32)


def dot(first, second, multiply=product):
    return multiply(first[0], second[0]) + (
        multiply(first[1], second[0]) + multiply(first[0], second[1])
    )


def as_first(value):
    high, low = split(value)
    return jnp.concatenate([high, low, high], axis=1)


def as_second(value):
    high, low = split(value)
    return jnp.concatenate([high, high, low], axis=0)


class Place:
    def __init__(self):
        core, ty, tx = (lax.axis_index(name) for name in ("kern", "ty", "tx"))
        self.down = lax.rem(ty + core, 2) == 0
        self.has_below = ty < lax.axis_size("ty") - 1
        self.has_above = ty > 0
        self.has_right = tx < lax.axis_size("tx") - 1
        self.has_left = tx > 0
        self.tx = tx

    def rightward(self, turn):
        return lax.rem(self.tx + turn, 2) == 0


def side_turns():
    count = lax.axis_size("tx")
    return 0 if count == 1 else 1 if count == 2 else 2


def partners(count, turn):
    found = [((i - turn) ^ 1) + turn for i in range(count)]
    return [j if 0 <= j < count else i for i, j in enumerate(found)]


def row_pairs(side_turn):
    rows, columns = (lax.axis_size("ty"), lax.axis_size("tx"))
    beside = partners(columns, 0)
    moved = list(range(columns)) if side_turn is None else partners(columns, side_turn)
    pairs = []
    for core in range(2):
        met = partners(rows, core)
        for ty in range(rows):
            for tx in range(columns):
                to = (met[ty], moved[tx]) if met[ty] != ty else (ty, beside[tx])
                base = core * rows * columns
                pairs.append((base + ty * columns + tx, base + to[0] * columns + to[1]))
    return pairs


def swap_cores(value):
    return lax.ppermute(value, "kern", [(0, 1), (1, 0)])


def swap_rows(value, side_turn=None):
    return lax.ppermute(value, ("kern", "ty", "tx"), row_pairs(side_turn))


def swap_side(value, turn):
    return lax.ppermute(value, "tx", list(enumerate(partners(lax.axis_size("tx"), turn))))


def half_turn(value):
    return pltpu.roll(value, HALO, 1)


def pack(block, upper):
    rows = block.shape[0] // 2
    first, last = (block[:rows], block[rows:])
    lane = lax.broadcasted_iota(jnp.int32, first.shape, 1)
    return jnp.where(
        lane < HALO,
        jnp.where(upper, half_turn(first), first),
        jnp.where(upper, last, half_turn(last)),
    )


def unpack(packed, upper):
    turned = half_turn(packed)
    return jnp.concatenate(
        [jnp.where(upper, turned, packed), jnp.where(upper, packed, turned)], axis=0
    )


def merge_sides(place, refs, right_is_upper):
    total = None
    for turn, ref in enumerate(refs):
        right = place.rightward(turn)
        there = jnp.where(right, place.has_right, place.has_left)
        upper = right if right_is_upper else jnp.logical_not(right)
        block = unpack(ref[...], upper)
        lane = lax.broadcasted_iota(jnp.int32, block.shape, 1)
        mine = jnp.logical_and((lane >= HALO) == upper, there)
        block = jnp.where(mine, block, 0.0)
        total = block if total is None else total + block
    return total


def prepare_kernel(turns, tile, mask_ref, kept_ref, row_ref, *refs):
    place = Place()
    block = mask_ref[...]
    kept_ref[...] = block
    strip = jnp.where(place.down, block[tile - HALO :], block[:HALO])
    row_ref[...] = strip
    for turn in range(turns):
        right = place.rightward(turn)
        for source, ref in ((block, refs[turn]), (strip, refs[turns + turn])):
            ref[...] = pack(
                jnp.where(right, source[:, tile - 2 * HALO :], source[:, : 2 * HALO]), right
            )


def own_kernel(tile, kept_ref, *refs):
    count = (len(refs) - 2) // 2
    sources, half_ref, copies, sems = (refs[:count], refs[count], refs[count + 1 : -1], refs[-1])
    moves = [
        pltpu.make_async_copy(source, copy, sems.at[i])
        for i, (source, copy) in enumerate(zip(sources, copies))
    ]
    for move in moves:
        move.start()
    moves[0].wait()
    moves[1].wait()
    half_ref[...] = dot((copies[0][:, :tile], copies[1][:, :tile]), split(kept_ref[...]))
    for move in moves[2:]:
        move.wait()


def order_kernel(spectra_ref, target_ref, band_order, tile_order, ordered_ref, goal_ref):
    band = band_order.shape[0]
    order = band_order[...]
    for part in range(spectra_ref.shape[0]):
        for start in range(0, spectra_ref.shape[1], 2):
            group = range(start, min(start + 2, spectra_ref.shape[1]))
            high, low = split(jnp.concatenate([spectra_ref[part, k] for k in group], axis=0))
            turned = product_turned(order, high) + product_turned(order, low)
            for place_in, k in enumerate(group):
                ordered_ref[part, k] = turned[:, place_in * band : (place_in + 1) * band]
    goal = product_turned(tile_order[...], target_ref[...].astype(F32).astype(BF16))
    goal_ref[...] = product_turned(goal.astype(BF16), tile_order[...])


def forward_kernel(turns, tile, band, scale, *refs):
    half_ref, row_mine, row_other = refs[:3]
    sides = refs[3 : 3 + turns]
    corners_mine = refs[3 + turns : 3 + 2 * turns]
    corners_other = refs[3 + 2 * turns : 3 + 3 * turns]
    (a_high, a_low, c_high, c_low, lift, cosine, sine, spectra_ref) = refs[3 + 3 * turns : -2]
    intensity_ref, field_ref = refs[-2:]
    place = Place()
    window = tile + 2 * HALO

    def margins(mine, other):
        below = jnp.where(place.has_below, jnp.where(place.down, mine, other), 0.0)
        above = jnp.where(place.has_above, jnp.where(place.down, other, mine), 0.0)
        return jnp.concatenate([below, above], axis=0)

    near = dot(
        (a_high[:, tile:window], a_low[:, tile:window]),
        split(margins(row_mine[...], row_other[...])),
    )
    near = half_ref[...] + near
    if turns:
        side = jnp.concatenate(
            [
                merge_sides(place, sides, False),
                margins(
                    merge_sides(place, corners_mine, False),
                    merge_sides(place, corners_other, False),
                ),
            ],
            axis=0,
        )
        far = dot((a_high[...], a_low[...]), split(side))
    else:
        far = jnp.zeros((near.shape[0], 2 * HALO), F32)
    half = jnp.concatenate([near[:band], far[:band], near[band:], far[band:]], axis=1)
    spectrum = dot((c_high[...], c_low[...]), split(half), product_turned) * scale
    spec_re, spec_im = (spectrum[:band], spectrum[band:])

    middle = tile // 2
    plain = cross = None
    for k in range(spectra_ref.shape[1]):
        kern_re, kern_im = (spectra_ref[0, k], spectra_ref[1, k])
        shifted = jnp.concatenate(
            [spec_re * kern_re - spec_im * kern_im, spec_re * kern_im + spec_im * kern_re], axis=0
        )
        rows = product(as_first(shifted), lift[...])
        even_re, odd_re = (rows[:band, :middle], rows[:band, middle:])
        even_im, odd_im = (rows[band:, :middle], rows[band:, middle:])
        parts = []
        for value in (
            jnp.concatenate([even_re - odd_im, even_re + odd_im], axis=1),
            jnp.concatenate([even_im + odd_re, even_im - odd_re], axis=1),
        ):
            ahead, behind = (value[: band // 2], value[band // 2 :])
            parts.append(product(cosine[...], as_second(ahead + behind)))
            parts.append(product(sine[...], as_second(ahead - behind)))
        for i, part in enumerate(parts):
            field_ref[k, i] = part
        even_re, odd_re, even_im, odd_im = parts
        power = (even_re * even_re + even_im * even_im) + (odd_re * odd_re + odd_im * odd_im)
        turn = even_im * odd_re - even_re * odd_im
        plain = power if plain is None else plain + power
        cross = turn if cross is None else cross + turn
    intensity_ref[:middle] = plain + 2.0 * cross
    intensity_ref[middle:] = plain - 2.0 * cross


def backward_kernel(tile, band, scale, *refs):
    (part_mine, part_other, goal_ref, field_ref, fold, drop, spectra_ref) = refs[:7]
    resist_ref, back_ref = refs[7:]
    middle = tile // 2
    intensity = part_mine[...] + part_other[...]
    resist = 1.0 / (1.0 + jnp.exp(-STEEP * (intensity - LEVEL)))
    resist_ref[...] = resist
    weight = 2.0 * (resist - goal_ref[...]) * STEEP * resist * (1.0 - resist)
    both, differ = (weight[:middle] + weight[middle:], weight[:middle] - weight[middle:])
    back_re = jnp.zeros((band, band), F32)
    back_im = jnp.zeros((band, band), F32)
    for k in range(spectra_ref.shape[1]):
        even_re, odd_re, even_im, odd_im = (field_ref[k, i] for i in range(4))
        columns = []
        for even, odd in (
            (both * even_re - differ * odd_im, both * odd_re + differ * even_im),
            (both * even_im + differ * odd_re, both * odd_im - differ * even_re),
        ):
            high, low = split(jnp.concatenate([even, odd], axis=0))
            wide = product(fold[...], high)
            columns.append(wide[:band] + wide[band:] + product(fold[:band], low))
        rows = product(as_first(jnp.concatenate(columns, axis=0)), drop[...])
        part_re = rows[:band, :band] + rows[band:, band:]
        part_im = rows[band:, :band] - rows[:band, band:]
        kern_re, kern_im = (spectra_ref[0, k], spectra_ref[1, k])
        back_re = back_re + (kern_re * part_re + kern_im * part_im)
        back_im = back_im + (kern_re * part_im - kern_im * part_re)
    back_ref[...] = jnp.concatenate([back_re, back_im], axis=1) * scale


def margin_kernel(turns, tile, band, *refs):
    back_mine, back_other, c_high, c_low, r_high, r_low, back_ref, row_ref = refs[:8]
    place = Place()
    window = tile + 2 * HALO
    back = 2.0 * (back_mine[...] + back_other[...])
    back_ref[...] = back

    def strip_rows(ref):
        picked = [
            jnp.where(
                place.down,
                ref[base + tile : base + tile + HALO],
                ref[base + tile + HALO : base + window],
            )
            for base in (0, window)
        ]
        return jnp.concatenate(picked, axis=0)

    lift = dot((strip_rows(r_high), strip_rows(r_low)), split(back), product_turned)
    lift = jnp.concatenate([lift[:HALO], lift[HALO:]], axis=1)
    strip = dot(split(lift), (c_high[:, :window], c_low[:, :window]))
    row_ref[...] = strip[:, :tile]
    for turn in range(turns):
        upper = jnp.logical_not(place.rightward(turn))
        refs[8 + turn][...] = pack(strip[:, tile:], upper)


def side_kernel(turns, tile, band, *refs):
    back_ref, c_high, c_low, r_high, r_low, lift_ref = refs[:6]
    place = Place()
    window = tile + 2 * HALO
    own = tuple(
        jnp.concatenate([r[:tile], r[window : window + tile]], axis=0) for r in (r_high, r_low)
    )
    lift = dot(own, split(back_ref[...]), product_turned)
    lift = jnp.concatenate([lift[:tile], lift[tile:]], axis=1)
    lift_ref[...] = lift
    if turns:
        side = dot(split(lift), (c_high[:, tile:window], c_low[:, tile:window]))
        for turn in range(turns):
            refs[6 + turn][...] = pack(side, jnp.logical_not(place.rightward(turn)))


def core_kernel(tile, lift_ref, c_high, c_low, core_ref):
    core_ref[...] = dot(split(lift_ref[...]), (c_high[:, :tile], c_low[:, :tile]))


def resist_kernel(resist_ref, order, order_back, out_ref):
    high, low = split(resist_ref[...])
    turned = product_turned(order_back[...], high) + product_turned(order_back[...], low)
    high, low = split(turned)
    out_ref[...] = product(high, order[...]) + product(low, order[...])


def merge_kernel(turns, tile, *refs):
    core_ref, row_mine, row_other = refs[:3]
    sides = refs[3 : 3 + turns]
    corners_mine = refs[3 + turns : 3 + 2 * turns]
    corners_other = refs[3 + 2 * turns : 3 + 3 * turns]
    out_ref = refs[3 + 3 * turns]
    place = Place()

    def spread(refs):
        merged = merge_sides(place, refs, True)
        lane = lax.broadcasted_iota(jnp.int32, merged.shape, 1)
        first = jnp.where(lane < HALO, merged, 0.0)
        last = jnp.where(lane >= HALO, merged, 0.0)
        middle = jnp.zeros((merged.shape[0], tile - 2 * merged.shape[1]), F32)
        return jnp.concatenate([first, middle, last] if middle.shape[1] else [first, last], axis=1)

    total = core_ref[...]
    mine, other = (row_mine[...], row_other[...])
    if turns:
        total = total + spread(sides)
        mine = mine + spread(corners_mine)
        other = other + spread(corners_other)
    bottom = jnp.where(place.has_below, jnp.where(place.down, mine, other), 0.0)
    top = jnp.where(place.has_above, jnp.where(place.down, other, mine), 0.0)
    out_ref[:HALO] = total[:HALO] + top
    out_ref[HALO : tile - HALO] = total[HALO : tile - HALO]
    out_ref[tile - HALO :] = total[tile - HALO :] + bottom


def call(kernel, out_shape, operands, in_hbm=(), **options):
    in_vmem = pl.BlockSpec(memory_space=pltpu.VMEM)
    anywhere = pl.BlockSpec(memory_space=pltpu.HBM)
    operands = [
        pltpu.with_memory_space_constraint(operand, pltpu.HBM) if i in in_hbm else operand
        for i, operand in enumerate(operands)
    ]
    return pl.pallas_call(
        kernel,
        out_shape=out_shape,
        in_specs=[anywhere if i in in_hbm else in_vmem for i in range(len(operands))],
        out_specs=jax.tree.map(lambda _: in_vmem, out_shape),
        compiler_params=pltpu.CompilerParams(vmem_limit_bytes=VMEM_LIMIT),
        **options,
    )(*operands)


def exchange(row, sides, corners, beside):
    turns = side_turns()
    row_mine = swap_rows(row)
    corners_mine = [swap_rows(corners[turn], turn) for turn in range(turns)]
    side = [swap_side(sides[turn], turn) for turn in range(turns)]
    row_mine, corners_mine, beside = lax.optimization_barrier((row_mine, corners_mine, beside))
    row_other = swap_cores(row_mine)
    corners_other = [swap_cores(corner) for corner in corners_mine]
    return ([row_mine, row_other, *side, *corners_mine, *corners_other], beside)


def on_device(mask, target, spectra):
    tile = mask.shape[0]
    band = spectra.shape[-1]
    window = tile + 2 * HALO
    scale = 1.0 / (window * window)
    turns = side_turns()
    image = pltpu.VMEM((tile, tile), F32)
    row_strip = pltpu.VMEM((HALO, tile), F32)
    side_strips = [pltpu.VMEM((tile // 2, 2 * HALO), F32)] * turns
    corner_strips = [pltpu.VMEM((HALO // 2, 2 * HALO), F32)] * turns

    kept, row, *packed = call(
        functools.partial(prepare_kernel, turns, tile),
        (image, row_strip, *side_strips, *corner_strips),
        [mask],
    )
    tables = make_tables(band, tile)
    sizes = [len(group) for group in tables.values()]
    sources = [jnp.asarray(t) for group in tables.values() for t in group] + [spectra, target]
    half, *shared = call(
        functools.partial(own_kernel, tile),
        (
            pltpu.VMEM((2 * band, tile), F32),
            *[pltpu.VMEM(source.shape, source.dtype) for source in sources],
        ),
        [kept, *sources],
        in_hbm=range(1, 1 + len(sources)),
        scratch_shapes=[pltpu.SemaphoreType.DMA((len(sources),))],
    )
    groups = iter(shared)
    window_tables, forward, backward, order = ([next(groups) for _ in range(n)] for n in sizes)
    received, (half, spectra, target) = exchange(
        row, packed[:turns], packed[turns:], (half, *shared[-2:])
    )
    ordered, goal = call(
        order_kernel,
        (pltpu.VMEM(spectra.shape, F32), image),
        [spectra, target, *order[:2]],
    )
    intensity, field = call(
        functools.partial(forward_kernel, turns, tile, band, scale),
        (image, pltpu.VMEM((spectra.shape[1], 4, tile // 2, tile), F32)),
        [half, *received, *window_tables[:4], *forward, ordered],
    )
    resist, back = call(
        functools.partial(backward_kernel, tile, band, scale),
        (image, pltpu.VMEM((band, 2 * band), F32)),
        [intensity, swap_cores(intensity), goal, field, *backward, ordered],
    )
    back, row, *corners = call(
        functools.partial(margin_kernel, turns, tile, band),
        (pltpu.VMEM((band, 2 * band), F32), row_strip, *corner_strips),
        [back, swap_cores(back), *window_tables[2:]],
    )
    lift, *sides = call(
        functools.partial(side_kernel, turns, tile, band),
        (pltpu.VMEM((tile, 2 * band), F32), *side_strips),
        [back, *window_tables[2:]],
    )
    sides, resist = lax.optimization_barrier((sides, resist))
    resist = call(resist_kernel, jax.ShapeDtypeStruct((tile, tile), F32), [resist, *order[1:]])
    received, (lift, resist) = exchange(row, sides, corners, (lift, resist))
    core = call(functools.partial(core_kernel, tile), image, [lift, *window_tables[2:4]])
    grad = call(
        functools.partial(merge_kernel, turns, tile),
        jax.ShapeDtypeStruct((tile, tile), F32),
        [core, *received],
    )
    return (resist, grad)


def solution(mesh):
    return jax.shard_map(
        on_device,
        mesh=mesh,
        in_specs=(P("ty", "tx"), P("ty", "tx"), P(None, "kern", None, None)),
        out_specs=(P("ty", "tx"), P("ty", "tx")),
        check_vma=False,
    )
```

```python
import functools
import math

import jax
import jax.numpy as jnp
import ml_dtypes
import numpy as np
from jax import lax
from jax.experimental import pallas as pl
from jax.experimental.pallas import tpu as pltpu
from jax.sharding import PartitionSpec as P

HALO = 64
STEEP = 8.0
LEVEL = 1.0
F32 = jnp.float32
BF16 = jnp.bfloat16


def cost(flops):
    return pl.CostEstimate(flops=flops, bytes_accessed=1 << 20, transcendentals=0)


VMEM_LIMIT = 24 * 1024 * 1024


def table_parts(table):
    high = table.astype(np.float32).astype(ml_dtypes.bfloat16)
    low = (table - high.astype(np.float64)).astype(np.float32).astype(ml_dtypes.bfloat16)
    return (high, low)


def signed_order(count):
    return np.concatenate([np.arange(count // 2, count), np.arange(count // 2)[::-1]])


def permutation(count):
    return np.eye(count)[signed_order(count)].astype(ml_dtypes.bfloat16)


def make_tables(band, tile):
    window = tile + 2 * HALO
    unit = 2.0 * math.pi / window
    natural = np.arange(band) - band // 2
    signed = signed_order(band) - band // 2
    places = np.concatenate([np.arange(HALO, window), np.arange(HALO)]) - (window - 1) / 2

    def blocks(frequency):
        angle = places[:, None] * frequency[None, :] * unit
        cosine, sine = (np.cos(angle), np.sin(angle))
        return np.block([[cosine, -sine], [sine, cosine]])

    rows = blocks(natural)
    own = np.r_[0:tile, window : window + tile]
    margin = np.r_[tile:window, window + tile : 2 * window]
    columns = np.ascontiguousarray(blocks(signed).T[:, :window])

    pixel = np.arange(tile // 2) + 0.5
    angle = (natural + 0.5)[:, None] * pixel[None, :] * unit
    lift = np.concatenate([np.cos(angle), np.sin(angle)], axis=1)
    both = np.concatenate([pixel, -pixel])[:, None] * (natural + 0.5)[None, :] * unit
    drop = np.concatenate([np.cos(both), np.sin(both)], axis=1)
    half = pixel[:, None] * (np.arange(band // 2) + 0.5)[None, :] * unit
    cosine, sine = (np.cos(half), np.sin(half))
    fold = np.block([[cosine.T, sine.T], [cosine.T, -sine.T]])

    def first(table):
        high, low = table_parts(table)
        return np.concatenate([high, low, high], axis=1)

    def second(table):
        high, low = table_parts(table)
        return np.concatenate([high, high, low], axis=0)

    return {
        "window": (
            *table_parts(columns),
            permutation(band),
            *table_parts(rows[own]),
            *table_parts(rows[margin]),
        ),
        "forward": (second(lift), first(cosine), first(sine)),
        "backward": (np.concatenate(table_parts(fold), axis=0), second(drop)),
        "order": (permutation(tile),),
    }


def split(value):
    high = value.astype(BF16)
    return (high, (value - high.astype(F32)).astype(BF16))


def product(a, b):
    return jnp.dot(a, b, preferred_element_type=F32)


def product_turned(a, b):
    return lax.dot_general(a, b, (((1,), (1,)), ((), ())), preferred_element_type=F32)


def dot(first, second, multiply=product):
    return multiply(first[0], second[0]) + (
        multiply(first[1], second[0]) + multiply(first[0], second[1])
    )


def as_first(value):
    high, low = split(value)
    return jnp.concatenate([high, low, high], axis=1)


def as_second(value):
    high, low = split(value)
    return jnp.concatenate([high, high, low], axis=0)


class Place:
    def __init__(self):
        core, ty, tx = (lax.axis_index(name) for name in ("kern", "ty", "tx"))
        self.down = lax.rem(ty + core, 2) == 0
        self.has_below = ty < lax.axis_size("ty") - 1
        self.has_above = ty > 0
        self.has_right = tx < lax.axis_size("tx") - 1
        self.has_left = tx > 0
        self.tx = tx

    def rightward(self, turn):
        return lax.rem(self.tx + turn, 2) == 0


def side_turns():
    count = lax.axis_size("tx")
    return 0 if count == 1 else 1 if count == 2 else 2


def partners(count, turn):
    found = [((i - turn) ^ 1) + turn for i in range(count)]
    return [j if 0 <= j < count else i for i, j in enumerate(found)]


def row_pairs(side_turn):
    rows, columns = (lax.axis_size("ty"), lax.axis_size("tx"))
    beside = partners(columns, 0)
    moved = list(range(columns)) if side_turn is None else partners(columns, side_turn)
    pairs = []
    for core in range(2):
        met = partners(rows, core)
        for ty in range(rows):
            for tx in range(columns):
                to = (met[ty], moved[tx]) if met[ty] != ty else (ty, beside[tx])
                base = core * rows * columns
                pairs.append((base + ty * columns + tx, base + to[0] * columns + to[1]))
    return pairs


def swap_cores(value):
    return lax.ppermute(value, "kern", [(0, 1), (1, 0)])


def swap_rows(value, side_turn=None):
    return lax.ppermute(value, ("kern", "ty", "tx"), row_pairs(side_turn))


def swap_side(value, turn):
    return lax.ppermute(value, "tx", list(enumerate(partners(lax.axis_size("tx"), turn))))


def half_turn(value):
    return pltpu.roll(value, HALO, 1)


def pack(block, upper):
    rows = block.shape[0] // 2
    first, last = (block[:rows], block[rows:])
    lane = lax.broadcasted_iota(jnp.int32, first.shape, 1)
    return jnp.where(
        lane < HALO,
        jnp.where(upper, half_turn(first), first),
        jnp.where(upper, last, half_turn(last)),
    )


def unpack(packed, upper):
    turned = half_turn(packed)
    return jnp.concatenate(
        [jnp.where(upper, turned, packed), jnp.where(upper, packed, turned)], axis=0
    )


def merge_sides(place, refs, right_is_upper):
    total = None
    for turn, ref in enumerate(refs):
        right = place.rightward(turn)
        there = jnp.where(right, place.has_right, place.has_left)
        upper = right if right_is_upper else jnp.logical_not(right)
        block = unpack(ref[...], upper)
        lane = lax.broadcasted_iota(jnp.int32, block.shape, 1)
        mine = jnp.logical_and((lane >= HALO) == upper, there)
        block = jnp.where(mine, block, 0.0)
        total = block if total is None else total + block
    return total


def start_copies(pairs, sems):
    moves = [pltpu.make_async_copy(a, b, sems.at[i]) for i, (a, b) in enumerate(pairs)]
    for move in moves:
        move.start()
    return moves


def prepare_kernel(turns, tile, mask_ref, row_ref, *refs):
    packed, blocks, sems = (refs[: 2 * turns], refs[2 * turns : -1], refs[-1])
    place = Place()
    rows = pl.ds(pl.multiple_of(jnp.where(place.down, tile - HALO, 0), HALO), HALO)
    pairs = [(mask_ref.at[rows, :], row_ref)]
    for turn in range(turns):
        start = jnp.where(place.rightward(turn), tile - 2 * HALO, 0)
        columns = pl.ds(pl.multiple_of(start, 2 * HALO), 2 * HALO)
        pairs.append((mask_ref.at[:, columns], blocks[turn]))
        pairs.append((mask_ref.at[rows, columns], blocks[turns + turn]))
    for move in start_copies(pairs, sems):
        move.wait()
    for i in range(2 * turns):
        packed[i][...] = pack(blocks[i][...], place.rightward(i % turns))


def own_kernel(tile, sources_count, *refs):
    sources, outs = (refs[:sources_count], refs[sources_count:])
    part_ref, *copies, mask_ref, sems = outs
    moves = start_copies(zip(sources, [mask_ref, *copies]), sems)
    for move in moves[:3]:
        move.wait()
    part_ref[...] = dot(
        (copies[0][:, :tile], copies[1][:, :tile]), split(mask_ref[...]), product_turned
    )
    for move in moves[3:]:
        move.wait()


def order_kernel(spectra_ref, order_ref, ordered_ref):
    order = order_ref[...]
    band = order.shape[0]
    for part in range(spectra_ref.shape[0]):
        for start in range(0, spectra_ref.shape[1], 2):
            group = range(start, min(start + 2, spectra_ref.shape[1]))
            high, low = split(jnp.concatenate([spectra_ref[part, k] for k in group], axis=0))
            turned = product_turned(order, high) + product_turned(order, low)
            for place_in, k in enumerate(group):
                ordered_ref[part, k] = turned[:, place_in * band : (place_in + 1) * band]


def late_kernel(sources_count, *refs):
    sources, outs = (refs[:sources_count], refs[sources_count:])
    goal_ref, *copies, target_ref, sems = outs
    moves = start_copies(zip(sources, [target_ref, *copies]), sems)
    for move in moves[:2]:
        move.wait()
    order = copies[0][...]
    goal = product_turned(order, target_ref[...].astype(F32).astype(BF16))
    goal_ref[...] = product_turned(goal.astype(BF16), order)
    for move in moves[2:]:
        move.wait()


def beside_kernel(turns, tile, band, *refs):
    part_ref, *sides = refs[: 1 + turns]
    c_high, c_low, r_high, r_low, spectrum_ref = refs[1 + turns :]
    place = Place()
    part = part_ref[...]
    if turns:
        side = merge_sides(place, sides, False)
        part = part + dot(
            (c_high[:, tile:], c_low[:, tile:]), split(side), product_turned
        )
    part = jnp.concatenate([part[:band], part[band:]], axis=1)
    spectrum_ref[...] = dot(split(part), (r_high[...], r_low[...]))


def join_kernel(turns, row_ref, *refs):
    corners, out_ref = (refs[:turns], refs[turns])
    rows = row_ref.shape[0]
    out_ref[:rows] = row_ref[...]
    for turn in range(turns):
        corner = corners[turn][...]
        half = corner.shape[0] // 2
        start = rows + turn * half
        out_ref[start : start + half] = jnp.concatenate([corner[:half], corner[half:]], axis=1)


def split_joined(joined, turns):
    half = HALO // 4
    corners = []
    for turn in range(turns):
        corner = joined[HALO + turn * half : HALO + (turn + 1) * half]
        lanes = 2 * HALO
        corners.append(jnp.concatenate([corner[:, :lanes], corner[:, lanes:]], axis=0))
    return (joined[:HALO], corners)


def forward_kernel(turns, tile, band, scale, *refs):
    spectrum_ref, joined_mine, joined_other = refs[:3]
    (c_high, c_low, m_high, m_low, lift, cosine, sine, spectra_ref) = refs[3:-2]
    row_mine, corners_mine = split_joined(joined_mine[...], turns)
    row_other, corners_other = split_joined(joined_other[...], turns)
    intensity_ref, field_ref = refs[-2:]
    place = Place()

    def margins(mine, other):
        below = jnp.where(place.has_below, jnp.where(place.down, mine, other), 0.0)
        above = jnp.where(place.has_above, jnp.where(place.down, other, mine), 0.0)
        return jnp.concatenate([below, above], axis=0)

    strips = margins(row_mine, row_other)
    if turns:
        corners = margins(
            merge_sides(place, corners_mine, False), merge_sides(place, corners_other, False)
        )
    else:
        corners = jnp.zeros((strips.shape[0], 2 * HALO), F32)
    strips = jnp.concatenate([strips, corners], axis=1)
    part = dot((c_high[...], c_low[...]), split(strips), product_turned)
    part = jnp.concatenate([part[:band], part[band:]], axis=1)
    spectrum = spectrum_ref[...] + dot(split(part), (m_high[...], m_low[...]))
    spectrum = spectrum * scale
    spec_re, spec_im = (spectrum[:, :band], spectrum[:, band:])

    middle = tile // 2
    plain = cross = None
    for k in range(spectra_ref.shape[1]):
        kern_re, kern_im = (spectra_ref[0, k], spectra_ref[1, k])
        shifted = jnp.concatenate(
            [spec_re * kern_re - spec_im * kern_im, spec_re * kern_im + spec_im * kern_re], axis=0
        )
        rows = product(as_first(shifted), lift[...])
        even_re, odd_re = (rows[:band, :middle], rows[:band, middle:])
        even_im, odd_im = (rows[band:, :middle], rows[band:, middle:])
        parts = []
        for value in (
            jnp.concatenate([even_re - odd_im, even_re + odd_im], axis=1),
            jnp.concatenate([even_im + odd_re, even_im - odd_re], axis=1),
        ):
            ahead, behind = (value[: band // 2], value[band // 2 :])
            parts.append(product(cosine[...], as_second(ahead + behind)))
            parts.append(product(sine[...], as_second(ahead - behind)))
        for i, part in enumerate(parts):
            field_ref[k, i] = part
        even_re, odd_re, even_im, odd_im = parts
        power = (even_re * even_re + even_im * even_im) + (odd_re * odd_re + odd_im * odd_im)
        turn = even_im * odd_re - even_re * odd_im
        plain = power if plain is None else plain + power
        cross = turn if cross is None else cross + turn
    intensity_ref[:middle] = plain + 2.0 * cross
    intensity_ref[middle:] = plain - 2.0 * cross


def backward_kernel(tile, band, scale, *refs):
    (part_mine, part_other, goal_ref, field_ref, fold, drop, spectra_ref) = refs[:7]
    resist_ref, back_ref = refs[7:]
    middle = tile // 2
    intensity = part_mine[...] + part_other[...]
    resist = 1.0 / (1.0 + jnp.exp(-STEEP * (intensity - LEVEL)))
    resist_ref[...] = resist
    weight = 2.0 * (resist - goal_ref[...]) * STEEP * resist * (1.0 - resist)
    both, differ = (weight[:middle] + weight[middle:], weight[:middle] - weight[middle:])
    back_re = jnp.zeros((band, band), F32)
    back_im = jnp.zeros((band, band), F32)
    for k in range(spectra_ref.shape[1]):
        even_re, odd_re, even_im, odd_im = (field_ref[k, i] for i in range(4))
        columns = []
        for even, odd in (
            (both * even_re - differ * odd_im, both * odd_re + differ * even_im),
            (both * even_im + differ * odd_re, both * odd_im - differ * even_re),
        ):
            high, low = split(jnp.concatenate([even, odd], axis=0))
            wide = product(fold[...], high)
            columns.append(wide[:band] + wide[band:] + product(fold[:band], low))
        rows = product(as_first(jnp.concatenate(columns, axis=0)), drop[...])
        part_re = rows[:band, :band] + rows[band:, band:]
        part_im = rows[band:, :band] - rows[:band, band:]
        kern_re, kern_im = (spectra_ref[0, k], spectra_ref[1, k])
        back_re = back_re + (kern_re * part_re + kern_im * part_im)
        back_im = back_im + (kern_re * part_im - kern_im * part_re)
    back_ref[...] = jnp.concatenate([back_re, back_im], axis=1) * scale


def margin_kernel(turns, tile, band, *refs):
    back_mine, back_other, c_high, c_low, m_high, m_low, back_ref, row_ref = refs[:8]
    place = Place()
    back = 2.0 * (back_mine[...] + back_other[...])
    back_ref[...] = back

    def strip_rows(ref):
        picked = [
            jnp.where(place.down, ref[base : base + HALO], ref[base + HALO : base + 2 * HALO])
            for base in (0, 2 * HALO)
        ]
        return jnp.concatenate(picked, axis=0)

    lift = dot((strip_rows(m_high), strip_rows(m_low)), split(back), product_turned)
    lift = jnp.concatenate([lift[:HALO], lift[HALO:]], axis=1)
    strip = dot(split(lift), (c_high[...], c_low[...]))
    row_ref[...] = strip[:, :tile]
    for turn in range(turns):
        upper = jnp.logical_not(place.rightward(turn))
        refs[8 + turn][...] = pack(strip[:, tile:], upper)


def side_kernel(turns, tile, band, *refs):
    back_ref, c_high, c_low, r_high, r_low, lift_ref = refs[:6]
    place = Place()
    lift = dot((r_high[...], r_low[...]), split(back_ref[...]), product_turned)
    lift = jnp.concatenate([lift[:tile], lift[tile:]], axis=1)
    lift_ref[...] = lift
    if turns:
        side = dot(split(lift), (c_high[:, tile:], c_low[:, tile:]))
        for turn in range(turns):
            refs[6 + turn][...] = pack(side, jnp.logical_not(place.rightward(turn)))


def core_kernel(tile, lift_ref, c_high, c_low, core_ref):
    core_ref[...] = dot(split(lift_ref[...]), (c_high[:, :tile], c_low[:, :tile]))


def resist_kernel(resist_ref, order, out_ref):
    high, low = split(resist_ref[...])
    turned = product(high, order[...]) + product(low, order[...])
    high, low = split(turned.T)
    out_ref[...] = product(high, order[...]) + product(low, order[...])


def spread_sides(place, refs, tile):
    merged = merge_sides(place, refs, True)
    lane = lax.broadcasted_iota(jnp.int32, merged.shape, 1)
    first = jnp.where(lane < HALO, merged, 0.0)
    last = jnp.where(lane >= HALO, merged, 0.0)
    middle = jnp.zeros((merged.shape[0], tile - 2 * merged.shape[1]), F32)
    return jnp.concatenate([first, middle, last] if middle.shape[1] else [first, last], axis=1)


def add_corners_kernel(turns, row_ref, *refs):
    place = Place()
    refs[turns][...] = row_ref[...] + spread_sides(place, refs[:turns], row_ref.shape[1])


def merge_kernel(turns, tile, core_ref, row_mine, row_other, *refs):
    place = Place()
    total = core_ref[...]
    if turns:
        total = total + spread_sides(place, refs[:turns], tile)
    mine, other = (row_mine[...], row_other[...])
    out_ref = refs[turns]
    bottom = jnp.where(place.has_below, jnp.where(place.down, mine, other), 0.0)
    top = jnp.where(place.has_above, jnp.where(place.down, other, mine), 0.0)
    out_ref[:HALO] = total[:HALO] + top
    out_ref[HALO : tile - HALO] = total[HALO : tile - HALO]
    out_ref[tile - HALO :] = total[tile - HALO :] + bottom


def call(kernel, out_shape, operands, in_hbm=(), **options):
    in_vmem = pl.BlockSpec(memory_space=pltpu.VMEM)
    anywhere = pl.BlockSpec(memory_space=pltpu.HBM)
    operands = [
        pltpu.with_memory_space_constraint(operand, pltpu.HBM) if i in in_hbm else operand
        for i, operand in enumerate(operands)
    ]
    return pl.pallas_call(
        kernel,
        out_shape=out_shape,
        in_specs=[anywhere if i in in_hbm else in_vmem for i in range(len(operands))],
        out_specs=jax.tree.map(lambda _: in_vmem, out_shape),
        compiler_params=pltpu.CompilerParams(vmem_limit_bytes=VMEM_LIMIT),
        **options,
    )(*operands)


def exchange(row, sides, corners, beside, join, joined_rows):
    turns = side_turns()
    row = swap_rows(row)
    corners = [swap_rows(corners[turn], turn) for turn in range(turns)]
    sides = [swap_side(sides[turn], turn) for turn in range(turns)]
    row, corners, beside = lax.optimization_barrier((row, corners, beside))
    if turns:
        joined = pltpu.VMEM((joined_rows, row.shape[1]), F32)
        row = call(
            functools.partial(join, turns), joined, [row, *corners], cost_estimate=cost(4 << 30)
        )
    return ([row, swap_cores(row), *sides], beside)


def on_device(mask, target, spectra):
    tile = mask.shape[0]
    band = spectra.shape[-1]
    window = tile + 2 * HALO
    scale = 1.0 / (window * window)
    turns = side_turns()
    image = pltpu.VMEM((tile, tile), F32)
    row_strip = pltpu.VMEM((HALO, tile), F32)
    side_strips = [pltpu.VMEM((tile // 2, 2 * HALO), F32)] * turns
    corner_strips = [pltpu.VMEM((HALO // 2, 2 * HALO), F32)] * turns
    wide = pltpu.VMEM((band, 2 * band), F32)

    row, *packed = call(
        functools.partial(prepare_kernel, turns, tile),
        (row_strip, *side_strips, *corner_strips),
        [mask],
        in_hbm=[0],
        scratch_shapes=[
            *[pltpu.VMEM((tile, 2 * HALO), F32)] * turns,
            *[pltpu.VMEM((HALO, 2 * HALO), F32)] * turns,
            pltpu.SemaphoreType.DMA((1 + 2 * turns,)),
        ],
    )
    tables = {
        name: [jnp.asarray(t) for t in group] for name, group in make_tables(band, tile).items()
    }
    row, mask = lax.optimization_barrier((row, mask))
    sources = [mask, *tables["window"], spectra, *tables["forward"]]
    part, *shared = call(
        functools.partial(own_kernel, tile, len(sources)),
        (
            pltpu.VMEM((2 * band, tile), F32),
            *[pltpu.VMEM(source.shape, source.dtype) for source in sources[1:]],
        ),
        sources,
        in_hbm=range(len(sources)),
        scratch_shapes=[
            pltpu.VMEM(mask.shape, F32),
            pltpu.SemaphoreType.DMA((len(sources),)),
        ],
    )
    columns, order, own_rows, margin_rows = (shared[0:2], shared[2], shared[3:5], shared[5:7])
    (mine, other, *sides), (part, spectra) = exchange(
        row,
        packed[:turns],
        packed[turns:],
        (part, shared[7]),
        join_kernel,
        HALO + turns * HALO // 4,
    )
    ordered = call(order_kernel, pltpu.VMEM(spectra.shape, F32), [spectra, order])
    part, ordered = lax.optimization_barrier((part, ordered))
    spectrum = call(
        functools.partial(beside_kernel, turns, tile, band),
        wide,
        [part, *sides, *columns, *own_rows],
        cost_estimate=cost(3 << 30),
    )
    intensity, field = call(
        functools.partial(forward_kernel, turns, tile, band, scale),
        (image, pltpu.VMEM((spectra.shape[1], 4, tile // 2, tile), F32)),
        [
            spectrum,
            mine,
            other,
            *columns,
            *margin_rows,
            *shared[8:],
            ordered,
        ],
    )
    intensity, target = lax.optimization_barrier((intensity, target))
    sources = tables["order"] + tables["backward"]
    goal, *late = call(
        functools.partial(late_kernel, len(sources) + 1),
        (image, *[pltpu.VMEM(source.shape, source.dtype) for source in sources]),
        [target, *sources],
        in_hbm=range(len(sources) + 1),
        scratch_shapes=[
            pltpu.VMEM(target.shape, target.dtype),
            pltpu.SemaphoreType.DMA((len(sources) + 1,)),
        ],
    )
    order, backward = (late[:1], late[1:])
    resist, back = call(
        functools.partial(backward_kernel, tile, band, scale),
        (image, wide),
        [intensity, swap_cores(intensity), goal, field, *backward, ordered],
    )
    resist = call(resist_kernel, jax.ShapeDtypeStruct((tile, tile), F32), [resist, *order])
    back_other, resist = lax.optimization_barrier((swap_cores(back), resist))
    back, row, *corners = call(
        functools.partial(margin_kernel, turns, tile, band),
        (wide, row_strip, *corner_strips),
        [back, back_other, *columns, *margin_rows],
    )
    lift, *sides = call(
        functools.partial(side_kernel, turns, tile, band),
        (pltpu.VMEM((tile, 2 * band), F32), *side_strips),
        [back, *columns, *own_rows],
    )
    received, lift = exchange(row, sides, corners, lift, add_corners_kernel, HALO)
    core = call(functools.partial(core_kernel, tile), image, [lift, *columns])
    grad = call(
        functools.partial(merge_kernel, turns, tile),
        jax.ShapeDtypeStruct((tile, tile), F32),
        [core, *received],
    )
    return (resist, grad)


def solution(mesh):
    return jax.shard_map(
        on_device,
        mesh=mesh,
        in_specs=(P("ty", "tx"), P("ty", "tx"), P(None, "kern", None, None)),
        out_specs=(P("ty", "tx"), P("ty", "tx")),
        check_vma=False,
    )
```

```python
import functools
import math

import jax
import jax.numpy as jnp
import ml_dtypes
import numpy as np
from jax import lax
from jax.experimental import pallas as pl
from jax.experimental.pallas import tpu as pltpu
from jax.sharding import PartitionSpec as P

HALO = 64
STEEP = 8.0
LEVEL = 1.0
F32 = jnp.float32
BF16 = jnp.bfloat16
AHEAD = 4


def cost(flops):
    return pl.CostEstimate(flops=flops, bytes_accessed=1 << 20, transcendentals=0)


VMEM_LIMIT = 24 * 1024 * 1024


def table_parts(table):
    high = table.astype(np.float32).astype(ml_dtypes.bfloat16)
    low = (table - high.astype(np.float64)).astype(np.float32).astype(ml_dtypes.bfloat16)
    return (high, low)


def signed_order(count):
    return np.concatenate([np.arange(count // 2, count), np.arange(count // 2)[::-1]])


def permutation(count):
    return np.eye(count)[signed_order(count)].astype(ml_dtypes.bfloat16)


def make_tables(band, tile):
    window = tile + 2 * HALO
    unit = 2.0 * math.pi / window
    natural = np.arange(band) - band // 2
    signed = signed_order(band) - band // 2
    places = np.concatenate([np.arange(HALO, window), np.arange(HALO)]) - (window - 1) / 2

    def blocks(frequency):
        angle = places[:, None] * frequency[None, :] * unit
        cosine, sine = (np.cos(angle), np.sin(angle))
        return np.block([[cosine, -sine], [sine, cosine]])

    rows = blocks(natural)
    own = np.r_[0:tile, window : window + tile]
    margin = np.r_[tile:window, window + tile : 2 * window]
    columns = np.ascontiguousarray(blocks(signed).T[:, :window])

    pixel = np.arange(tile // 2) + 0.5
    angle = (natural + 0.5)[:, None] * pixel[None, :] * unit
    lift = np.concatenate([np.cos(angle), np.sin(angle)], axis=1)
    drops = (np.cos(angle.T), np.sin(angle.T))
    half = pixel[:, None] * (np.arange(band // 2) + 0.5)[None, :] * unit
    cosine, sine = (np.cos(half), np.sin(half))
    fold = np.block([[cosine.T, sine.T], [cosine.T, -sine.T]])

    def first(table):
        high, low = table_parts(table)
        return np.concatenate([high, low, high], axis=1)

    def second(table):
        high, low = table_parts(table)
        return np.concatenate([high, high, low], axis=0)

    def paired(table):
        high, low = table_parts(table)
        return np.block([[high, low], [high, np.zeros_like(low)]])

    return {
        "window": (*table_parts(columns), permutation(tile)),
        "forward": (
            permutation(band),
            *table_parts(rows[own]),
            *table_parts(rows[margin]),
            second(lift),
            first(cosine),
            first(sine),
        ),
        "backward": (
            np.concatenate(table_parts(fold), axis=0),
            *[paired(table) for table in drops],
        ),
    }


def split(value):
    high = value.astype(BF16)
    return (high, (value - high.astype(F32)).astype(BF16))


def product(a, b):
    return jnp.dot(a, b, preferred_element_type=F32)


def product_turned(a, b):
    return lax.dot_general(a, b, (((1,), (1,)), ((), ())), preferred_element_type=F32)


def dot(first, second, multiply=product):
    return multiply(first[0], second[0]) + (
        multiply(first[1], second[0]) + multiply(first[0], second[1])
    )


def as_first(value):
    high, low = split(value)
    return jnp.concatenate([high, low, high], axis=1)


def as_second(value):
    high, low = split(value)
    return jnp.concatenate([high, high, low], axis=0)


class Place:
    def __init__(self):
        core, ty, tx = (lax.axis_index(name) for name in ("kern", "ty", "tx"))
        self.down = lax.rem(ty + core, 2) == 0
        self.has_below = ty < lax.axis_size("ty") - 1
        self.has_above = ty > 0
        self.has_right = tx < lax.axis_size("tx") - 1
        self.has_left = tx > 0
        self.tx = tx

    def rightward(self, turn):
        return lax.rem(self.tx + turn, 2) == 0


def side_turns():
    count = lax.axis_size("tx")
    return 0 if count == 1 else 1 if count == 2 else 2


def partners(count, turn):
    found = [((i - turn) ^ 1) + turn for i in range(count)]
    return [j if 0 <= j < count else i for i, j in enumerate(found)]


def row_pairs(side_turn):
    rows, columns = (lax.axis_size("ty"), lax.axis_size("tx"))
    beside = partners(columns, 0)
    moved = list(range(columns)) if side_turn is None else partners(columns, side_turn)
    pairs = []
    for core in range(2):
        met = partners(rows, core)
        for ty in range(rows):
            for tx in range(columns):
                to = (met[ty], moved[tx]) if met[ty] != ty else (ty, beside[tx])
                base = core * rows * columns
                pairs.append((base + ty * columns + tx, base + to[0] * columns + to[1]))
    return pairs


def swap_cores(value):
    return lax.ppermute(value, "kern", [(0, 1), (1, 0)])


def swap_rows(value, side_turn=None):
    return lax.ppermute(value, ("kern", "ty", "tx"), row_pairs(side_turn))


def swap_side(value, turn):
    return lax.ppermute(value, "tx", list(enumerate(partners(lax.axis_size("tx"), turn))))


def half_turn(value):
    return pltpu.roll(value, HALO, 1)


def pack(block, upper):
    rows = block.shape[0] // 2
    first, last = (block[:rows], block[rows:])
    lane = lax.broadcasted_iota(jnp.int32, first.shape, 1)
    return jnp.where(
        lane < HALO,
        jnp.where(upper, half_turn(first), first),
        jnp.where(upper, last, half_turn(last)),
    )


def unpack(packed, upper):
    turned = half_turn(packed)
    return jnp.concatenate(
        [jnp.where(upper, turned, packed), jnp.where(upper, packed, turned)], axis=0
    )


def merge_sides(place, refs, right_is_upper):
    total = None
    for turn, ref in enumerate(refs):
        right = place.rightward(turn)
        there = jnp.where(right, place.has_right, place.has_left)
        upper = right if right_is_upper else jnp.logical_not(right)
        block = unpack(ref[...], upper)
        lane = lax.broadcasted_iota(jnp.int32, block.shape, 1)
        mine = jnp.logical_and((lane >= HALO) == upper, there)
        block = jnp.where(mine, block, 0.0)
        total = block if total is None else total + block
    return total


def start_copies(pairs, sems):
    moves = [pltpu.make_async_copy(a, b, sems.at[i]) for i, (a, b) in enumerate(pairs)]
    for move in moves:
        move.start()
    return moves


def prepare_kernel(turns, tile, mask_ref, row_ref, *refs):
    place = Place()
    block = mask_ref[...]
    strip = jnp.where(place.down, block[tile - HALO :], block[:HALO])
    row_ref[...] = strip
    for turn in range(turns):
        right = place.rightward(turn)
        for source, ref in ((block, refs[turn]), (strip, refs[turns + turn])):
            ref[...] = pack(
                jnp.where(right, source[:, tile - 2 * HALO :], source[:, : 2 * HALO]), right
            )


def own_kernel(tile, sources_count, mask_ref, *refs):
    sources, outs = (refs[:sources_count], refs[sources_count:])
    part_ref, goal_ref, *copies, target_ref, sems = outs
    moves = start_copies(zip(sources, [*copies[:3], target_ref, *copies[3:]]), sems)
    for move in moves[:2]:
        move.wait()
    part_ref[...] = dot(
        (copies[0][:, :tile], copies[1][:, :tile]), split(mask_ref[...]), product_turned
    )
    for move in moves[2:4]:
        move.wait()
    order = copies[2][...]
    goal = product_turned(order, target_ref[...].astype(F32).astype(BF16))
    goal_ref[...] = product_turned(goal.astype(BF16), order)
    for move in moves[4:]:
        move.wait()


def order_kernel(spectra_ref, order_ref, ordered_ref):
    order = order_ref[...]
    band = order.shape[0]
    for part in range(spectra_ref.shape[0]):
        for start in range(0, spectra_ref.shape[1], 2):
            group = range(start, min(start + 2, spectra_ref.shape[1]))
            high, low = split(jnp.concatenate([spectra_ref[part, k] for k in group], axis=0))
            turned = product_turned(order, high) + product_turned(order, low)
            for place_in, k in enumerate(group):
                ordered_ref[part, k] = turned[:, place_in * band : (place_in + 1) * band]


def late_kernel(sources_count, after_ref, *refs):
    sources, copies, sems = (refs[:sources_count], refs[sources_count:-1], refs[-1])
    for move in start_copies(zip(sources, copies), sems):
        move.wait()


def beside_kernel(turns, tile, band, *refs):
    part_ref, *sides = refs[: 1 + turns]
    c_high, c_low, r_high, r_low, spectrum_ref = refs[1 + turns :]
    place = Place()
    part = part_ref[...]
    if turns:
        side = merge_sides(place, sides, False)
        part = part + dot(
            (c_high[:, tile:], c_low[:, tile:]), split(side), product_turned
        )
    part = jnp.concatenate([part[:band], part[band:]], axis=1)
    spectrum_ref[...] = dot(split(part), (r_high[...], r_low[...]))


def join_kernel(turns, row_ref, *refs):
    corners, out_ref = (refs[:turns], refs[turns])
    rows = row_ref.shape[0]
    out_ref[:rows] = row_ref[...]
    for turn in range(turns):
        corner = corners[turn][...]
        half = corner.shape[0] // 2
        start = rows + turn * half
        out_ref[start : start + half] = jnp.concatenate([corner[:half], corner[half:]], axis=1)


def split_joined(joined, turns):
    half = HALO // 4
    corners = []
    for turn in range(turns):
        corner = joined[HALO + turn * half : HALO + (turn + 1) * half]
        lanes = 2 * HALO
        corners.append(jnp.concatenate([corner[:, :lanes], corner[:, lanes:]], axis=0))
    return (joined[:HALO], corners)


def forward_kernel(turns, tile, band, scale, *refs):
    spectrum_ref, joined_mine, joined_other = refs[:3]
    (c_high, c_low, m_high, m_low, lift, cosine, sine, spectra_ref) = refs[3:-2]
    row_mine, corners_mine = split_joined(joined_mine[...], turns)
    row_other, corners_other = split_joined(joined_other[...], turns)
    intensity_ref, field_ref = refs[-2:]
    place = Place()

    def margins(mine, other):
        below = jnp.where(place.has_below, jnp.where(place.down, mine, other), 0.0)
        above = jnp.where(place.has_above, jnp.where(place.down, other, mine), 0.0)
        return jnp.concatenate([below, above], axis=0)

    strips = margins(row_mine, row_other)
    if turns:
        corners = margins(
            merge_sides(place, corners_mine, False), merge_sides(place, corners_other, False)
        )
    else:
        corners = jnp.zeros((strips.shape[0], 2 * HALO), F32)
    strips = jnp.concatenate([strips, corners], axis=1)
    part = dot((c_high[...], c_low[...]), split(strips), product_turned)
    part = jnp.concatenate([part[:band], part[band:]], axis=1)
    spectrum = spectrum_ref[...] + dot(split(part), (m_high[...], m_low[...]))
    spectrum = spectrum * scale
    spec_re, spec_im = (spectrum[:, :band], spectrum[:, band:])

    middle = tile // 2
    kernels = spectra_ref.shape[1]

    def lifted(k):
        kern_re, kern_im = (spectra_ref[0, k], spectra_ref[1, k])
        shifted = jnp.concatenate(
            [spec_re * kern_re - spec_im * kern_im, spec_re * kern_im + spec_im * kern_re], axis=0
        )
        return product(as_first(shifted), lift[...])

    ahead = [lifted(k) for k in range(min(AHEAD, kernels))]
    plain = cross = None
    for k in range(kernels):
        if k + AHEAD < kernels:
            ahead.append(lifted(k + AHEAD))
        rows = ahead.pop(0)
        even_re, odd_re = (rows[:band, :middle], rows[:band, middle:])
        even_im, odd_im = (rows[band:, :middle], rows[band:, middle:])
        parts = []
        for value in (
            jnp.concatenate([even_re - odd_im, even_re + odd_im], axis=1),
            jnp.concatenate([even_im + odd_re, even_im - odd_re], axis=1),
        ):
            up, down = (value[: band // 2], value[band // 2 :])
            parts.append(product(cosine[...], as_second(up + down)))
            parts.append(product(sine[...], as_second(up - down)))
        for i, part in enumerate(parts):
            field_ref[k, i] = part
        even_re, odd_re, even_im, odd_im = parts
        power = (even_re * even_re + even_im * even_im) + (odd_re * odd_re + odd_im * odd_im)
        turn = even_im * odd_re - even_re * odd_im
        plain = power if plain is None else plain + power
        cross = turn if cross is None else cross + turn
    intensity_ref[:middle] = plain + 2.0 * cross
    intensity_ref[middle:] = plain - 2.0 * cross


def backward_kernel(tile, band, scale, *refs):
    part_mine, part_other, goal_ref, field_ref = refs[:4]
    fold, drop_even, drop_odd, spectra_ref, resist_ref, back_ref = refs[4:]
    middle = tile // 2
    intensity = part_mine[...] + part_other[...]
    resist = 1.0 / (1.0 + jnp.exp(-STEEP * (intensity - LEVEL)))
    resist_ref[...] = resist
    weight = 2.0 * (resist - goal_ref[...]) * STEEP * resist * (1.0 - resist)
    both, differ = (weight[:middle] + weight[middle:], weight[:middle] - weight[middle:])
    back_re = jnp.zeros((band, band), F32)
    back_im = jnp.zeros((band, band), F32)
    kernels = spectra_ref.shape[1]

    def folded(k):
        even_re, odd_re, even_im, odd_im = (field_ref[k, i] for i in range(4))
        columns = []
        for even, odd in (
            (both * even_re - differ * odd_im, both * odd_re + differ * even_im),
            (both * even_im + differ * odd_re, both * odd_im - differ * even_re),
        ):
            high, low = split(jnp.concatenate([even, odd], axis=0))
            wide = product(fold[...], high)
            columns.append(wide[:band] + wide[band:] + product(fold[:band], low))
        return jnp.concatenate(columns, axis=0)

    def dropped(value, table):
        pair = product(jnp.concatenate(split(value), axis=1), table[...])
        return pair[:, :band] + pair[:, band:]

    ahead = folded(0)
    for k in range(kernels):
        rows = ahead
        if k + 1 < kernels:
            ahead = folded(k + 1)
        even = dropped(rows[:, :middle] + rows[:, middle:], drop_even)
        odd = dropped(rows[:, :middle] - rows[:, middle:], drop_odd)
        part_re = even[:band] + odd[band:]
        part_im = even[band:] - odd[:band]
        kern_re, kern_im = (spectra_ref[0, k], spectra_ref[1, k])
        back_re = back_re + (kern_re * part_re + kern_im * part_im)
        back_im = back_im + (kern_re * part_im - kern_im * part_re)
    back_ref[...] = jnp.concatenate([back_re, back_im], axis=1) * scale


def margin_kernel(turns, tile, band, *refs):
    back_mine, back_other, c_high, c_low, m_high, m_low, back_ref, row_ref = refs[:8]
    place = Place()
    back = 2.0 * (back_mine[...] + back_other[...])
    back_ref[...] = back

    def strip_rows(ref):
        picked = [
            jnp.where(place.down, ref[base : base + HALO], ref[base + HALO : base + 2 * HALO])
            for base in (0, 2 * HALO)
        ]
        return jnp.concatenate(picked, axis=0)

    lift = dot((strip_rows(m_high), strip_rows(m_low)), split(back), product_turned)
    lift = jnp.concatenate([lift[:HALO], lift[HALO:]], axis=1)
    strip = dot(split(lift), (c_high[...], c_low[...]))
    row_ref[...] = strip[:, :tile]
    for turn in range(turns):
        upper = jnp.logical_not(place.rightward(turn))
        refs[8 + turn][...] = pack(strip[:, tile:], upper)


def side_kernel(turns, tile, band, *refs):
    back_ref, c_high, c_low, r_high, r_low, lift_ref = refs[:6]
    place = Place()
    lift = dot((r_high[...], r_low[...]), split(back_ref[...]), product_turned)
    lift = jnp.concatenate([lift[:tile], lift[tile:]], axis=1)
    lift_ref[...] = lift
    if turns:
        side = dot(split(lift), (c_high[:, tile:], c_low[:, tile:]))
        for turn in range(turns):
            refs[6 + turn][...] = pack(side, jnp.logical_not(place.rightward(turn)))


def core_kernel(tile, lift_ref, c_high, c_low, core_ref):
    core_ref[...] = dot(split(lift_ref[...]), (c_high[:, :tile], c_low[:, :tile]))


def resist_kernel(resist_ref, order, out_ref):
    high, low = split(resist_ref[...])
    turned = product(high, order[...]) + product(low, order[...])
    high, low = split(turned.T)
    out_ref[...] = product(high, order[...]) + product(low, order[...])


def spread_sides(place, refs, tile):
    merged = merge_sides(place, refs, True)
    lane = lax.broadcasted_iota(jnp.int32, merged.shape, 1)
    first = jnp.where(lane < HALO, merged, 0.0)
    last = jnp.where(lane >= HALO, merged, 0.0)
    middle = jnp.zeros((merged.shape[0], tile - 2 * merged.shape[1]), F32)
    return jnp.concatenate([first, middle, last] if middle.shape[1] else [first, last], axis=1)


def add_corners_kernel(turns, row_ref, *refs):
    place = Place()
    refs[turns][...] = row_ref[...] + spread_sides(place, refs[:turns], row_ref.shape[1])


def merge_kernel(turns, tile, core_ref, row_mine, row_other, *refs):
    place = Place()
    total = core_ref[...]
    if turns:
        total = total + spread_sides(place, refs[:turns], tile)
    mine, other = (row_mine[...], row_other[...])
    out_ref = refs[turns]
    bottom = jnp.where(place.has_below, jnp.where(place.down, mine, other), 0.0)
    top = jnp.where(place.has_above, jnp.where(place.down, other, mine), 0.0)
    out_ref[:HALO] = total[:HALO] + top
    out_ref[HALO : tile - HALO] = total[HALO : tile - HALO]
    out_ref[tile - HALO :] = total[tile - HALO :] + bottom


def call(kernel, out_shape, operands, in_hbm=(), **options):
    in_vmem = pl.BlockSpec(memory_space=pltpu.VMEM)
    anywhere = pl.BlockSpec(memory_space=pltpu.HBM)
    operands = [
        pltpu.with_memory_space_constraint(operand, pltpu.HBM) if i in in_hbm else operand
        for i, operand in enumerate(operands)
    ]
    return pl.pallas_call(
        kernel,
        out_shape=out_shape,
        in_specs=[anywhere if i in in_hbm else in_vmem for i in range(len(operands))],
        out_specs=jax.tree.map(lambda _: in_vmem, out_shape),
        compiler_params=pltpu.CompilerParams(vmem_limit_bytes=VMEM_LIMIT),
        **options,
    )(*operands)


def exchange(row, sides, corners, beside, join, joined_rows):
    turns = side_turns()
    row = swap_rows(row)
    corners = [swap_rows(corners[turn], turn) for turn in range(turns)]
    sides = [swap_side(sides[turn], turn) for turn in range(turns)]
    row, corners, beside = lax.optimization_barrier((row, corners, beside))
    if turns:
        joined = pltpu.VMEM((joined_rows, row.shape[1]), F32)
        row = call(
            functools.partial(join, turns), joined, [row, *corners], cost_estimate=cost(4 << 30)
        )
    return ([row, swap_cores(row), *sides], beside)


def on_device(mask, target, spectra):
    tile = mask.shape[0]
    band = spectra.shape[-1]
    window = tile + 2 * HALO
    scale = 1.0 / (window * window)
    turns = side_turns()
    image = pltpu.VMEM((tile, tile), F32)
    row_strip = pltpu.VMEM((HALO, tile), F32)
    side_strips = [pltpu.VMEM((tile // 2, 2 * HALO), F32)] * turns
    corner_strips = [pltpu.VMEM((HALO // 2, 2 * HALO), F32)] * turns
    wide = pltpu.VMEM((band, 2 * band), F32)

    row, *packed = call(
        functools.partial(prepare_kernel, turns, tile),
        (row_strip, *side_strips, *corner_strips),
        [mask],
    )
    tables = {
        name: [jnp.asarray(t) for t in group] for name, group in make_tables(band, tile).items()
    }
    row, mask = lax.optimization_barrier((row, mask))
    sources = [*tables["window"], target, spectra, *tables["forward"]]
    kept = sources[:3] + sources[4:]
    part, goal, *shared = call(
        functools.partial(own_kernel, tile, len(sources)),
        (
            pltpu.VMEM((2 * band, tile), F32),
            image,
            *[pltpu.VMEM(source.shape, source.dtype) for source in kept],
        ),
        [mask, *sources],
        in_hbm=range(1, 1 + len(sources)),
        scratch_shapes=[
            pltpu.VMEM(target.shape, target.dtype),
            pltpu.SemaphoreType.DMA((len(sources),)),
        ],
    )
    columns, tile_order, order = (shared[0:2], shared[2], shared[4])
    own_rows, margin_rows = (shared[5:7], shared[7:9])
    (mine, other, *sides), (part, spectra) = exchange(
        row,
        packed[:turns],
        packed[turns:],
        (part, shared[3]),
        join_kernel,
        HALO + turns * HALO // 4,
    )
    ordered = call(order_kernel, pltpu.VMEM(spectra.shape, F32), [spectra, order])
    part, ordered = lax.optimization_barrier((part, ordered))
    spectrum = call(
        functools.partial(beside_kernel, turns, tile, band),
        wide,
        [part, *sides, *columns, *own_rows],
        cost_estimate=cost(3 << 30),
    )
    intensity, field = call(
        functools.partial(forward_kernel, turns, tile, band, scale),
        (image, pltpu.VMEM((spectra.shape[1], 4, tile // 2, tile), F32)),
        [
            spectrum,
            mine,
            other,
            *columns,
            *margin_rows,
            *shared[9:],
            ordered,
        ],
    )
    sources = tables["backward"]
    backward = call(
        functools.partial(late_kernel, len(sources)),
        tuple(pltpu.VMEM(source.shape, source.dtype) for source in sources),
        [intensity, *sources],
        in_hbm=range(1, 1 + len(sources)),
        scratch_shapes=[pltpu.SemaphoreType.DMA((len(sources),))],
    )
    resist, back = call(
        functools.partial(backward_kernel, tile, band, scale),
        (image, wide),
        [intensity, swap_cores(intensity), goal, field, *backward, ordered],
    )
    back, row, *corners = call(
        functools.partial(margin_kernel, turns, tile, band),
        (wide, row_strip, *corner_strips),
        [back, swap_cores(back), *columns, *margin_rows],
    )
    lift, *sides = call(
        functools.partial(side_kernel, turns, tile, band),
        (pltpu.VMEM((tile, 2 * band), F32), *side_strips),
        [back, *columns, *own_rows],
    )
    sides, resist = lax.optimization_barrier((sides, resist))
    resist = call(resist_kernel, jax.ShapeDtypeStruct((tile, tile), F32), [resist, tile_order])
    received, (lift, resist) = exchange(
        row, sides, corners, (lift, resist), add_corners_kernel, HALO
    )
    core = call(functools.partial(core_kernel, tile), image, [lift, *columns])
    grad = call(
        functools.partial(merge_kernel, turns, tile),
        jax.ShapeDtypeStruct((tile, tile), F32),
        [core, *received],
    )
    return (resist, grad)


def solution(mesh):
    return jax.shard_map(
        on_device,
        mesh=mesh,
        in_specs=(P("ty", "tx"), P("ty", "tx"), P(None, "kern", None, None)),
        out_specs=(P("ty", "tx"), P("ty", "tx")),
        check_vma=False,
    )
```

```python
import functools
import math

import jax
import jax.numpy as jnp
import ml_dtypes
import numpy as np
from jax import lax
from jax.experimental import pallas as pl
from jax.experimental.pallas import tpu as pltpu
from jax.sharding import PartitionSpec as P

HALO = 64
STEEP = 8.0
LEVEL = 1.0
F32 = jnp.float32
BF16 = jnp.bfloat16
AHEAD = 4


def cost(flops):
    return pl.CostEstimate(flops=flops, bytes_accessed=1 << 20, transcendentals=0)


VMEM_LIMIT = 24 * 1024 * 1024


def table_parts(table):
    high = table.astype(np.float32).astype(ml_dtypes.bfloat16)
    low = (table - high.astype(np.float64)).astype(np.float32).astype(ml_dtypes.bfloat16)
    return (high, low)


def signed_order(count):
    return np.concatenate([np.arange(count // 2, count), np.arange(count // 2)[::-1]])


def permutation(count):
    return np.eye(count)[signed_order(count)].astype(ml_dtypes.bfloat16)


def make_tables(band, tile):
    window = tile + 2 * HALO
    unit = 2.0 * math.pi / window
    natural = np.arange(band) - band // 2
    signed = signed_order(band) - band // 2
    places = np.concatenate([np.arange(HALO, window), np.arange(HALO)]) - (window - 1) / 2

    def blocks(frequency):
        angle = places[:, None] * frequency[None, :] * unit
        cosine, sine = (np.cos(angle), np.sin(angle))
        return np.block([[cosine, -sine], [sine, cosine]])

    rows = blocks(natural)
    own = np.r_[0:tile, window : window + tile]
    margin = np.r_[tile:window, window + tile : 2 * window]
    columns = np.ascontiguousarray(blocks(signed).T[:, :window])

    pixel = np.arange(tile // 2) + 0.5
    angle = (natural + 0.5)[:, None] * pixel[None, :] * unit
    lift = np.concatenate([np.cos(angle), np.sin(angle)], axis=1)
    drops = (np.cos(angle.T), np.sin(angle.T))
    half = pixel[:, None] * (np.arange(band // 2) + 0.5)[None, :] * unit
    cosine, sine = (np.cos(half), np.sin(half))

    def first(table):
        high, low = table_parts(table)
        return np.concatenate([high, low, high], axis=1)

    def second(table):
        high, low = table_parts(table)
        return np.concatenate([high, high, low], axis=0)

    def paired(table):
        high, low = table_parts(table)
        return np.block([[high, low], [high, np.zeros_like(low)]])

    return {
        "window": (*table_parts(columns), permutation(tile)),
        "forward": (
            permutation(band),
            *table_parts(rows[own]),
            *table_parts(rows[margin]),
            second(lift),
            first(cosine),
            first(sine),
        ),
        "backward": (
            *[np.ascontiguousarray(paired(table).T) for table in (cosine, sine)],
            *[paired(table) for table in drops],
        ),
    }


def split(value):
    high = value.astype(BF16)
    return (high, (value - high.astype(F32)).astype(BF16))


def product(a, b):
    return jnp.dot(a, b, preferred_element_type=F32)


def product_turned(a, b):
    return lax.dot_general(a, b, (((1,), (1,)), ((), ())), preferred_element_type=F32)


def dot(first, second, multiply=product):
    return multiply(first[0], second[0]) + (
        multiply(first[1], second[0]) + multiply(first[0], second[1])
    )


def as_first(value):
    high, low = split(value)
    return jnp.concatenate([high, low, high], axis=1)


def as_second(value):
    high, low = split(value)
    return jnp.concatenate([high, high, low], axis=0)


class Place:
    def __init__(self):
        core, ty, tx = (lax.axis_index(name) for name in ("kern", "ty", "tx"))
        self.down = lax.rem(ty + core, 2) == 0
        self.has_below = ty < lax.axis_size("ty") - 1
        self.has_above = ty > 0
        self.has_right = tx < lax.axis_size("tx") - 1
        self.has_left = tx > 0
        self.tx = tx

    def rightward(self, turn):
        return lax.rem(self.tx + turn, 2) == 0


def side_turns():
    count = lax.axis_size("tx")
    return 0 if count == 1 else 1 if count == 2 else 2


def partners(count, turn):
    found = [((i - turn) ^ 1) + turn for i in range(count)]
    return [j if 0 <= j < count else i for i, j in enumerate(found)]


def row_pairs(side_turn):
    rows, columns = (lax.axis_size("ty"), lax.axis_size("tx"))
    beside = partners(columns, 0)
    moved = list(range(columns)) if side_turn is None else partners(columns, side_turn)
    pairs = []
    for core in range(2):
        met = partners(rows, core)
        for ty in range(rows):
            for tx in range(columns):
                to = (met[ty], moved[tx]) if met[ty] != ty else (ty, beside[tx])
                base = core * rows * columns
                pairs.append((base + ty * columns + tx, base + to[0] * columns + to[1]))
    return pairs


def swap_cores(value):
    return lax.ppermute(value, "kern", [(0, 1), (1, 0)])


def swap_rows(value, side_turn=None):
    return lax.ppermute(value, ("kern", "ty", "tx"), row_pairs(side_turn))


def swap_side(value, turn):
    return lax.ppermute(value, "tx", list(enumerate(partners(lax.axis_size("tx"), turn))))


def half_turn(value):
    return pltpu.roll(value, HALO, 1)


def pack(block, upper):
    rows = block.shape[0] // 2
    first, last = (block[:rows], block[rows:])
    lane = lax.broadcasted_iota(jnp.int32, first.shape, 1)
    return jnp.where(
        lane < HALO,
        jnp.where(upper, half_turn(first), first),
        jnp.where(upper, last, half_turn(last)),
    )


def unpack(packed, upper):
    turned = half_turn(packed)
    return jnp.concatenate(
        [jnp.where(upper, turned, packed), jnp.where(upper, packed, turned)], axis=0
    )


def merge_sides(place, refs, right_is_upper):
    total = None
    for turn, ref in enumerate(refs):
        right = place.rightward(turn)
        there = jnp.where(right, place.has_right, place.has_left)
        upper = right if right_is_upper else jnp.logical_not(right)
        block = unpack(ref[...], upper)
        lane = lax.broadcasted_iota(jnp.int32, block.shape, 1)
        mine = jnp.logical_and((lane >= HALO) == upper, there)
        block = jnp.where(mine, block, 0.0)
        total = block if total is None else total + block
    return total


def start_copies(pairs, sems):
    moves = [pltpu.make_async_copy(a, b, sems.at[i]) for i, (a, b) in enumerate(pairs)]
    for move in moves:
        move.start()
    return moves


def prepare_kernel(turns, tile, mask_ref, row_ref, *refs):
    place = Place()
    block = mask_ref[...]
    strip = jnp.where(place.down, block[tile - HALO :], block[:HALO])
    row_ref[...] = strip
    for turn in range(turns):
        right = place.rightward(turn)
        for source, ref in ((block, refs[turn]), (strip, refs[turns + turn])):
            ref[...] = pack(
                jnp.where(right, source[:, tile - 2 * HALO :], source[:, : 2 * HALO]), right
            )


def own_kernel(tile, sources_count, mask_ref, *refs):
    sources, outs = (refs[:sources_count], refs[sources_count:])
    part_ref, goal_ref, *copies, target_ref, sems = outs
    moves = start_copies(zip(sources, [*copies[:3], target_ref, *copies[3:]]), sems)
    for move in moves[:2]:
        move.wait()
    part_ref[...] = dot(
        (copies[0][:, :tile], copies[1][:, :tile]), split(mask_ref[...]), product_turned
    )
    for move in moves[2:4]:
        move.wait()
    order = copies[2][...]
    goal = product_turned(order, target_ref[...].astype(F32).astype(BF16))
    goal_ref[...] = product_turned(goal.astype(BF16), order)
    for move in moves[4:]:
        move.wait()


def order_kernel(spectra_ref, order_ref, ordered_ref):
    order = order_ref[...]
    band = order.shape[0]
    for part in range(spectra_ref.shape[0]):
        for start in range(0, spectra_ref.shape[1], 2):
            group = range(start, min(start + 2, spectra_ref.shape[1]))
            high, low = split(jnp.concatenate([spectra_ref[part, k] for k in group], axis=0))
            turned = product_turned(order, high) + product_turned(order, low)
            for place_in, k in enumerate(group):
                ordered_ref[part, k] = turned[:, place_in * band : (place_in + 1) * band]


def late_kernel(sources_count, after_ref, *refs):
    sources, copies, sems = (refs[:sources_count], refs[sources_count:-1], refs[-1])
    for move in start_copies(zip(sources, copies), sems):
        move.wait()


def beside_kernel(turns, tile, band, *refs):
    part_ref, *sides = refs[: 1 + turns]
    c_high, c_low, r_high, r_low, spectrum_ref = refs[1 + turns :]
    place = Place()
    part = part_ref[...]
    if turns:
        side = merge_sides(place, sides, False)
        part = part + dot(
            (c_high[:, tile:], c_low[:, tile:]), split(side), product_turned
        )
    part = jnp.concatenate([part[:band], part[band:]], axis=1)
    spectrum_ref[...] = dot(split(part), (r_high[...], r_low[...]))


def join_kernel(turns, row_ref, *refs):
    corners, out_ref = (refs[:turns], refs[turns])
    rows = row_ref.shape[0]
    out_ref[:rows] = row_ref[...]
    for turn in range(turns):
        corner = corners[turn][...]
        half = corner.shape[0] // 2
        start = rows + turn * half
        out_ref[start : start + half] = jnp.concatenate([corner[:half], corner[half:]], axis=1)


def split_joined(joined, turns):
    half = HALO // 4
    corners = []
    for turn in range(turns):
        corner = joined[HALO + turn * half : HALO + (turn + 1) * half]
        lanes = 2 * HALO
        corners.append(jnp.concatenate([corner[:, :lanes], corner[:, lanes:]], axis=0))
    return (joined[:HALO], corners)


def forward_kernel(turns, tile, band, scale, *refs):
    spectrum_ref, joined_mine, joined_other = refs[:3]
    (c_high, c_low, m_high, m_low, lift, cosine, sine, spectra_ref) = refs[3:-2]
    row_mine, corners_mine = split_joined(joined_mine[...], turns)
    row_other, corners_other = split_joined(joined_other[...], turns)
    intensity_ref, field_ref = refs[-2:]
    place = Place()

    def margins(mine, other):
        below = jnp.where(place.has_below, jnp.where(place.down, mine, other), 0.0)
        above = jnp.where(place.has_above, jnp.where(place.down, other, mine), 0.0)
        return jnp.concatenate([below, above], axis=0)

    strips = margins(row_mine, row_other)
    if turns:
        corners = margins(
            merge_sides(place, corners_mine, False), merge_sides(place, corners_other, False)
        )
    else:
        corners = jnp.zeros((strips.shape[0], 2 * HALO), F32)
    strips = jnp.concatenate([strips, corners], axis=1)
    part = dot((c_high[...], c_low[...]), split(strips), product_turned)
    part = jnp.concatenate([part[:band], part[band:]], axis=1)
    spectrum = spectrum_ref[...] + dot(split(part), (m_high[...], m_low[...]))
    spectrum = spectrum * scale
    spec_re, spec_im = (spectrum[:, :band], spectrum[:, band:])

    middle = tile // 2
    kernels = spectra_ref.shape[1]

    def lifted(k):
        kern_re, kern_im = (spectra_ref[0, k], spectra_ref[1, k])
        shifted = jnp.concatenate(
            [spec_re * kern_re - spec_im * kern_im, spec_re * kern_im + spec_im * kern_re], axis=0
        )
        return product(as_first(shifted), lift[...])

    ahead = [lifted(k) for k in range(min(AHEAD, kernels))]
    total = None
    for k in range(kernels):
        if k + AHEAD < kernels:
            ahead.append(lifted(k + AHEAD))
        rows = ahead.pop(0)
        even_re, odd_re = (rows[:band, :middle], rows[:band, middle:])
        even_im, odd_im = (rows[band:, :middle], rows[band:, middle:])
        parts = []
        for value in (
            jnp.concatenate([even_re - odd_im, even_re + odd_im], axis=1),
            jnp.concatenate([even_im + odd_re, even_im - odd_re], axis=1),
        ):
            up, down = (value[: band // 2], value[band // 2 :])
            parts.append(product(cosine[...], as_second(up + down)))
            parts.append(product(sine[...], as_second(up - down)))
        even_re, odd_re, even_im, odd_im = parts
        near = (even_re - odd_im, even_im + odd_re)
        far = (even_re + odd_im, even_im - odd_re)
        for i, part in enumerate(near + far):
            field_ref[k, i] = part
        power = near[0] * near[0] + near[1] * near[1]
        mirrored = far[0] * far[0] + far[1] * far[1]
        total = (power, mirrored) if total is None else (total[0] + power, total[1] + mirrored)
    intensity_ref[:middle], intensity_ref[middle:] = total


def backward_kernel(tile, band, scale, *refs):
    part_mine, part_other, goal_ref, field_ref = refs[:4]
    fold_even, fold_odd, drop_even, drop_odd, spectra_ref, resist_ref, back_ref = refs[4:]
    middle = tile // 2
    intensity = part_mine[...] + part_other[...]
    resist = 1.0 / (1.0 + jnp.exp(-STEEP * (intensity - LEVEL)))
    resist_ref[...] = resist
    weight = 2.0 * (resist - goal_ref[...]) * STEEP * resist * (1.0 - resist)
    ahead_weight, mirrored_weight = (weight[:middle], weight[middle:])
    back_re = jnp.zeros((band, band), F32)
    back_im = jnp.zeros((band, band), F32)
    kernels = spectra_ref.shape[1]

    def folded(k):
        near_re, near_im = (ahead_weight * field_ref[k, i] for i in range(2))
        far_re, far_im = (mirrored_weight * field_ref[k, i] for i in range(2, 4))
        columns = []
        for even, odd in (
            (near_re + far_re, near_im - far_im),
            (near_im + far_im, far_re - near_re),
        ):
            even = product(fold_even[...], jnp.concatenate(split(even), axis=0))
            odd = product(fold_odd[...], jnp.concatenate(split(odd), axis=0))
            even = even[: band // 2] + even[band // 2 :]
            odd = odd[: band // 2] + odd[band // 2 :]
            columns += [even + odd, even - odd]
        return jnp.concatenate(columns, axis=0)

    def dropped(value, table):
        pair = product(jnp.concatenate(split(value), axis=1), table[...])
        return pair[:, :band] + pair[:, band:]

    ahead = folded(0)
    for k in range(kernels):
        rows = ahead
        if k + 1 < kernels:
            ahead = folded(k + 1)
        even = dropped(rows[:, :middle] + rows[:, middle:], drop_even)
        odd = dropped(rows[:, :middle] - rows[:, middle:], drop_odd)
        part_re = even[:band] + odd[band:]
        part_im = even[band:] - odd[:band]
        kern_re, kern_im = (spectra_ref[0, k], spectra_ref[1, k])
        back_re = back_re + (kern_re * part_re + kern_im * part_im)
        back_im = back_im + (kern_re * part_im - kern_im * part_re)
    back_ref[...] = jnp.concatenate([back_re, back_im], axis=1) * scale


def margin_kernel(turns, tile, band, *refs):
    back_mine, back_other, c_high, c_low, m_high, m_low, back_ref, row_ref = refs[:8]
    place = Place()
    back = 2.0 * (back_mine[...] + back_other[...])
    back_ref[...] = back

    def strip_rows(ref):
        picked = [
            jnp.where(place.down, ref[base : base + HALO], ref[base + HALO : base + 2 * HALO])
            for base in (0, 2 * HALO)
        ]
        return jnp.concatenate(picked, axis=0)

    lift = dot((strip_rows(m_high), strip_rows(m_low)), split(back), product_turned)
    lift = jnp.concatenate([lift[:HALO], lift[HALO:]], axis=1)
    strip = dot(split(lift), (c_high[...], c_low[...]))
    row_ref[...] = strip[:, :tile]
    for turn in range(turns):
        upper = jnp.logical_not(place.rightward(turn))
        refs[8 + turn][...] = pack(strip[:, tile:], upper)


def side_kernel(turns, tile, band, *refs):
    back_ref, c_high, c_low, r_high, r_low, lift_ref = refs[:6]
    place = Place()
    lift = dot((r_high[...], r_low[...]), split(back_ref[...]), product_turned)
    lift = jnp.concatenate([lift[:tile], lift[tile:]], axis=1)
    lift_ref[...] = lift
    if turns:
        side = dot(split(lift), (c_high[:, tile:], c_low[:, tile:]))
        for turn in range(turns):
            refs[6 + turn][...] = pack(side, jnp.logical_not(place.rightward(turn)))


def core_kernel(tile, lift_ref, c_high, c_low, core_ref):
    core_ref[...] = dot(split(lift_ref[...]), (c_high[:, :tile], c_low[:, :tile]))


def resist_kernel(resist_ref, order, out_ref):
    high, low = split(resist_ref[...])
    turned = product(high, order[...]) + product(low, order[...])
    high, low = split(turned.T)
    out_ref[...] = product(high, order[...]) + product(low, order[...])


def spread_sides(place, refs, tile):
    merged = merge_sides(place, refs, True)
    lane = lax.broadcasted_iota(jnp.int32, merged.shape, 1)
    first = jnp.where(lane < HALO, merged, 0.0)
    last = jnp.where(lane >= HALO, merged, 0.0)
    middle = jnp.zeros((merged.shape[0], tile - 2 * merged.shape[1]), F32)
    return jnp.concatenate([first, middle, last] if middle.shape[1] else [first, last], axis=1)


def add_corners_kernel(turns, row_ref, *refs):
    place = Place()
    refs[turns][...] = row_ref[...] + spread_sides(place, refs[:turns], row_ref.shape[1])


def merge_kernel(turns, tile, core_ref, row_mine, row_other, *refs):
    place = Place()
    total = core_ref[...]
    if turns:
        total = total + spread_sides(place, refs[:turns], tile)
    mine, other = (row_mine[...], row_other[...])
    out_ref = refs[turns]
    bottom = jnp.where(place.has_below, jnp.where(place.down, mine, other), 0.0)
    top = jnp.where(place.has_above, jnp.where(place.down, other, mine), 0.0)
    out_ref[:HALO] = total[:HALO] + top
    out_ref[HALO : tile - HALO] = total[HALO : tile - HALO]
    out_ref[tile - HALO :] = total[tile - HALO :] + bottom


def call(kernel, out_shape, operands, in_hbm=(), **options):
    in_vmem = pl.BlockSpec(memory_space=pltpu.VMEM)
    anywhere = pl.BlockSpec(memory_space=pltpu.HBM)
    operands = [
        pltpu.with_memory_space_constraint(operand, pltpu.HBM) if i in in_hbm else operand
        for i, operand in enumerate(operands)
    ]
    return pl.pallas_call(
        kernel,
        out_shape=out_shape,
        in_specs=[anywhere if i in in_hbm else in_vmem for i in range(len(operands))],
        out_specs=jax.tree.map(lambda _: in_vmem, out_shape),
        compiler_params=pltpu.CompilerParams(vmem_limit_bytes=VMEM_LIMIT),
        **options,
    )(*operands)


def exchange(row, sides, corners, beside, join, joined_rows):
    turns = side_turns()
    row = swap_rows(row)
    corners = [swap_rows(corners[turn], turn) for turn in range(turns)]
    sides = [swap_side(sides[turn], turn) for turn in range(turns)]
    row, corners, beside = lax.optimization_barrier((row, corners, beside))
    if turns:
        joined = pltpu.VMEM((joined_rows, row.shape[1]), F32)
        row = call(
            functools.partial(join, turns), joined, [row, *corners], cost_estimate=cost(4 << 30)
        )
    return ([row, swap_cores(row), *sides], beside)


def on_device(mask, target, spectra):
    tile = mask.shape[0]
    band = spectra.shape[-1]
    window = tile + 2 * HALO
    scale = 1.0 / (window * window)
    turns = side_turns()
    image = pltpu.VMEM((tile, tile), F32)
    row_strip = pltpu.VMEM((HALO, tile), F32)
    side_strips = [pltpu.VMEM((tile // 2, 2 * HALO), F32)] * turns
    corner_strips = [pltpu.VMEM((HALO // 2, 2 * HALO), F32)] * turns
    wide = pltpu.VMEM((band, 2 * band), F32)

    row, *packed = call(
        functools.partial(prepare_kernel, turns, tile),
        (row_strip, *side_strips, *corner_strips),
        [mask],
    )
    tables = {
        name: [jnp.asarray(t) for t in group] for name, group in make_tables(band, tile).items()
    }
    row, mask = lax.optimization_barrier((row, mask))
    sources = [*tables["window"], target, spectra, *tables["forward"]]
    kept = sources[:3] + sources[4:]
    part, goal, *shared = call(
        functools.partial(own_kernel, tile, len(sources)),
        (
            pltpu.VMEM((2 * band, tile), F32),
            image,
            *[pltpu.VMEM(source.shape, source.dtype) for source in kept],
        ),
        [mask, *sources],
        in_hbm=range(1, 1 + len(sources)),
        scratch_shapes=[
            pltpu.VMEM(target.shape, target.dtype),
            pltpu.SemaphoreType.DMA((len(sources),)),
        ],
    )
    columns, tile_order, order = (shared[0:2], shared[2], shared[4])
    own_rows, margin_rows = (shared[5:7], shared[7:9])
    (mine, other, *sides), (part, spectra) = exchange(
        row,
        packed[:turns],
        packed[turns:],
        (part, shared[3]),
        join_kernel,
        HALO + turns * HALO // 4,
    )
    ordered = call(order_kernel, pltpu.VMEM(spectra.shape, F32), [spectra, order])
    part, ordered = lax.optimization_barrier((part, ordered))
    spectrum = call(
        functools.partial(beside_kernel, turns, tile, band),
        wide,
        [part, *sides, *columns, *own_rows],
        cost_estimate=cost(3 << 30),
    )
    intensity, field = call(
        functools.partial(forward_kernel, turns, tile, band, scale),
        (image, pltpu.VMEM((spectra.shape[1], 4, tile // 2, tile), F32)),
        [
            spectrum,
            mine,
            other,
            *columns,
            *margin_rows,
            *shared[9:],
            ordered,
        ],
    )
    sources = tables["backward"]
    backward = call(
        functools.partial(late_kernel, len(sources)),
        tuple(pltpu.VMEM(source.shape, source.dtype) for source in sources),
        [intensity, *sources],
        in_hbm=range(1, 1 + len(sources)),
        scratch_shapes=[pltpu.SemaphoreType.DMA((len(sources),))],
    )
    resist, back = call(
        functools.partial(backward_kernel, tile, band, scale),
        (image, wide),
        [intensity, swap_cores(intensity), goal, field, *backward, ordered],
    )
    back, row, *corners = call(
        functools.partial(margin_kernel, turns, tile, band),
        (wide, row_strip, *corner_strips),
        [back, swap_cores(back), *columns, *margin_rows],
    )
    lift, *sides = call(
        functools.partial(side_kernel, turns, tile, band),
        (pltpu.VMEM((tile, 2 * band), F32), *side_strips),
        [back, *columns, *own_rows],
    )
    sides, resist = lax.optimization_barrier((sides, resist))
    resist = call(resist_kernel, jax.ShapeDtypeStruct((tile, tile), F32), [resist, tile_order])
    received, (lift, resist) = exchange(
        row, sides, corners, (lift, resist), add_corners_kernel, HALO
    )
    core = call(functools.partial(core_kernel, tile), image, [lift, *columns])
    grad = call(
        functools.partial(merge_kernel, turns, tile),
        jax.ShapeDtypeStruct((tile, tile), F32),
        [core, *received],
    )
    return (resist, grad)


def solution(mesh):
    return jax.shard_map(
        on_device,
        mesh=mesh,
        in_specs=(P("ty", "tx"), P("ty", "tx"), P(None, "kern", None, None)),
        out_specs=(P("ty", "tx"), P("ty", "tx")),
        check_vma=False,
    )
```

```python
import functools
import math

import jax
import jax.numpy as jnp
import ml_dtypes
import numpy as np
from jax import lax
from jax.experimental import pallas as pl
from jax.experimental.pallas import tpu as pltpu
from jax.sharding import PartitionSpec as P

HALO = 64
STEEP = 8.0
LEVEL = 1.0
F32 = jnp.float32
BF16 = jnp.bfloat16
AHEAD = 4


def cost(flops):
    return pl.CostEstimate(flops=flops, bytes_accessed=1 << 20, transcendentals=0)


VMEM_LIMIT = 24 * 1024 * 1024


def table_parts(table):
    high = table.astype(np.float32).astype(ml_dtypes.bfloat16)
    low = (table - high.astype(np.float64)).astype(np.float32).astype(ml_dtypes.bfloat16)
    return (high, low)


def signed_order(count):
    return np.concatenate([np.arange(count // 2, count), np.arange(count // 2)[::-1]])


def permutation(count):
    return np.eye(count)[signed_order(count)].astype(ml_dtypes.bfloat16)


def make_tables(band, tile):
    window = tile + 2 * HALO
    unit = 2.0 * math.pi / window
    natural = np.arange(band) - band // 2
    signed = signed_order(band) - band // 2
    places = np.concatenate([np.arange(HALO, window), np.arange(HALO)]) - (window - 1) / 2

    def blocks(frequency):
        angle = places[:, None] * frequency[None, :] * unit
        cosine, sine = (np.cos(angle), np.sin(angle))
        return np.block([[cosine, -sine], [sine, cosine]])

    rows = blocks(natural)
    own = np.r_[0:tile, window : window + tile]
    margin = np.r_[tile:window, window + tile : 2 * window]
    columns = np.ascontiguousarray(blocks(signed).T[:, :window])

    pixel = np.arange(tile // 2) + 0.5
    angle = (natural + 0.5)[:, None] * pixel[None, :] * unit
    lift = np.concatenate([np.cos(angle), np.sin(angle)], axis=1)
    drops = (np.cos(angle.T), np.sin(angle.T))
    half = pixel[:, None] * (np.arange(band // 2) + 0.5)[None, :] * unit
    cosine, sine = (np.cos(half), np.sin(half))

    def first(table):
        high, low = table_parts(table)
        return np.concatenate([high, low, high], axis=1)

    def second(table):
        high, low = table_parts(table)
        return np.concatenate([high, high, low], axis=0)

    def paired(table):
        high, low = table_parts(table)
        return np.block([[high, low], [high, np.zeros_like(low)]])

    return {
        "window": (*table_parts(columns), permutation(tile)),
        "forward": (
            permutation(band),
            *table_parts(rows[own]),
            *table_parts(rows[margin]),
            second(lift),
            first(cosine),
            first(sine),
        ),
        "backward": (
            *[np.ascontiguousarray(paired(table).T) for table in (cosine, sine)],
            *[paired(table) for table in drops],
        ),
    }


def split(value):
    high = value.astype(BF16)
    return (high, (value - high.astype(F32)).astype(BF16))


def product(a, b):
    return jnp.dot(a, b, preferred_element_type=F32)


def product_turned(a, b):
    return lax.dot_general(a, b, (((1,), (1,)), ((), ())), preferred_element_type=F32)


def dot(first, second, multiply=product):
    return multiply(first[0], second[0]) + (
        multiply(first[1], second[0]) + multiply(first[0], second[1])
    )


def as_first(value):
    high, low = split(value)
    return jnp.concatenate([high, low, high], axis=1)


def as_second(value):
    high, low = split(value)
    return jnp.concatenate([high, high, low], axis=0)


class Place:
    def __init__(self):
        core, ty, tx = (lax.axis_index(name) for name in ("kern", "ty", "tx"))
        self.down = lax.rem(ty + core, 2) == 0
        self.has_below = ty < lax.axis_size("ty") - 1
        self.has_above = ty > 0
        self.has_right = tx < lax.axis_size("tx") - 1
        self.has_left = tx > 0
        self.tx = tx

    def rightward(self, turn):
        return lax.rem(self.tx + turn, 2) == 0


def side_turns():
    count = lax.axis_size("tx")
    return 0 if count == 1 else 1 if count == 2 else 2


def partners(count, turn):
    found = [((i - turn) ^ 1) + turn for i in range(count)]
    return [j if 0 <= j < count else i for i, j in enumerate(found)]


def row_pairs(side_turn):
    rows, columns = (lax.axis_size("ty"), lax.axis_size("tx"))
    beside = partners(columns, 0)
    moved = list(range(columns)) if side_turn is None else partners(columns, side_turn)
    pairs = []
    for core in range(2):
        met = partners(rows, core)
        for ty in range(rows):
            for tx in range(columns):
                to = (met[ty], moved[tx]) if met[ty] != ty else (ty, beside[tx])
                base = core * rows * columns
                pairs.append((base + ty * columns + tx, base + to[0] * columns + to[1]))
    return pairs


def swap_cores(value):
    return lax.ppermute(value, "kern", [(0, 1), (1, 0)])


def swap_rows(value, side_turn=None):
    return lax.ppermute(value, ("kern", "ty", "tx"), row_pairs(side_turn))


def swap_side(value, turn):
    return lax.ppermute(value, "tx", list(enumerate(partners(lax.axis_size("tx"), turn))))


def half_turn(value):
    return pltpu.roll(value, HALO, 1)


def pack(block, upper):
    rows = block.shape[0] // 2
    first, last = (block[:rows], block[rows:])
    lane = lax.broadcasted_iota(jnp.int32, first.shape, 1)
    return jnp.where(
        lane < HALO,
        jnp.where(upper, half_turn(first), first),
        jnp.where(upper, last, half_turn(last)),
    )


def unpack(packed, upper):
    turned = half_turn(packed)
    return jnp.concatenate(
        [jnp.where(upper, turned, packed), jnp.where(upper, packed, turned)], axis=0
    )


def merge_sides(place, refs, right_is_upper):
    total = None
    for turn, ref in enumerate(refs):
        right = place.rightward(turn)
        there = jnp.where(right, place.has_right, place.has_left)
        upper = right if right_is_upper else jnp.logical_not(right)
        block = unpack(ref[...], upper)
        lane = lax.broadcasted_iota(jnp.int32, block.shape, 1)
        mine = jnp.logical_and((lane >= HALO) == upper, there)
        block = jnp.where(mine, block, 0.0)
        total = block if total is None else total + block
    return total


def start_copies(pairs, sems):
    moves = [pltpu.make_async_copy(a, b, sems.at[i]) for i, (a, b) in enumerate(pairs)]
    for move in moves:
        move.start()
    return moves


def prepare_kernel(turns, tile, mask_ref, row_ref, *refs):
    place = Place()
    block = mask_ref[...]
    strip = jnp.where(place.down, block[tile - HALO :], block[:HALO])
    row_ref[...] = strip
    for turn in range(turns):
        right = place.rightward(turn)
        for source, ref in ((block, refs[turn]), (strip, refs[turns + turn])):
            ref[...] = pack(
                jnp.where(right, source[:, tile - 2 * HALO :], source[:, : 2 * HALO]), right
            )


def own_kernel(tile, sources_count, mask_ref, *refs):
    sources, outs = (refs[:sources_count], refs[sources_count:])
    part_ref, goal_ref, ordered_ref, *copies, target_ref, sems = outs
    moves = start_copies(zip(sources, [*copies[:3], target_ref, *copies[3:]]), sems)
    for move in moves[:2]:
        move.wait()
    part_ref[...] = dot(
        (copies[0][:, :tile], copies[1][:, :tile]), split(mask_ref[...]), product_turned
    )
    for move in moves[2:4]:
        move.wait()
    order = copies[2][...]
    goal = product_turned(order, target_ref[...].astype(F32).astype(BF16))
    goal_ref[...] = product_turned(goal.astype(BF16), order)
    for move in moves[4:]:
        move.wait()
    turn_spectra(copies[3].at[0], copies[4][...], ordered_ref)


def turn_spectra(source_ref, order, ordered_ref):
    band = order.shape[0]
    for start in range(0, source_ref.shape[0], 2):
        group = range(start, min(start + 2, source_ref.shape[0]))
        high, low = split(jnp.concatenate([source_ref[k] for k in group], axis=0))
        turned = product_turned(order, high) + product_turned(order, low)
        for place_in, k in enumerate(group):
            ordered_ref[k] = turned[:, place_in * band : (place_in + 1) * band]


def order_kernel(spectra_ref, order_ref, ordered_ref):
    turn_spectra(spectra_ref.at[1], order_ref[...], ordered_ref)


def late_kernel(sources_count, after_ref, *refs):
    sources, copies, sems = (refs[:sources_count], refs[sources_count:-1], refs[-1])
    for move in start_copies(zip(sources, copies), sems):
        move.wait()


def beside_kernel(turns, tile, band, *refs):
    part_ref, *sides = refs[: 1 + turns]
    c_high, c_low, r_high, r_low, spectrum_ref = refs[1 + turns :]
    place = Place()
    part = part_ref[...]
    if turns:
        side = merge_sides(place, sides, False)
        part = part + dot(
            (c_high[:, tile:], c_low[:, tile:]), split(side), product_turned
        )
    part = jnp.concatenate([part[:band], part[band:]], axis=1)
    spectrum_ref[...] = dot(split(part), (r_high[...], r_low[...]))


def join_kernel(turns, row_ref, *refs):
    corners, out_ref = (refs[:turns], refs[turns])
    rows = row_ref.shape[0]
    out_ref[:rows] = row_ref[...]
    for turn in range(turns):
        corner = corners[turn][...]
        half = corner.shape[0] // 2
        start = rows + turn * half
        out_ref[start : start + half] = jnp.concatenate([corner[:half], corner[half:]], axis=1)


def split_joined(joined, turns):
    half = HALO // 4
    corners = []
    for turn in range(turns):
        corner = joined[HALO + turn * half : HALO + (turn + 1) * half]
        lanes = 2 * HALO
        corners.append(jnp.concatenate([corner[:, :lanes], corner[:, lanes:]], axis=0))
    return (joined[:HALO], corners)


def forward_kernel(turns, tile, band, scale, *refs):
    spectrum_ref, joined_mine, joined_other = refs[:3]
    (c_high, c_low, m_high, m_low, lift, cosine, sine, kern_re_ref, kern_im_ref) = refs[3:-2]
    row_mine, corners_mine = split_joined(joined_mine[...], turns)
    row_other, corners_other = split_joined(joined_other[...], turns)
    intensity_ref, field_ref = refs[-2:]
    place = Place()

    def margins(mine, other):
        below = jnp.where(place.has_below, jnp.where(place.down, mine, other), 0.0)
        above = jnp.where(place.has_above, jnp.where(place.down, other, mine), 0.0)
        return jnp.concatenate([below, above], axis=0)

    strips = margins(row_mine, row_other)
    if turns:
        corners = margins(
            merge_sides(place, corners_mine, False), merge_sides(place, corners_other, False)
        )
    else:
        corners = jnp.zeros((strips.shape[0], 2 * HALO), F32)
    strips = jnp.concatenate([strips, corners], axis=1)
    part = dot((c_high[...], c_low[...]), split(strips), product_turned)
    part = jnp.concatenate([part[:band], part[band:]], axis=1)
    spectrum = spectrum_ref[...] + dot(split(part), (m_high[...], m_low[...]))
    spectrum = spectrum * scale
    spec_re, spec_im = (spectrum[:, :band], spectrum[:, band:])

    middle = tile // 2
    kernels = kern_re_ref.shape[0]

    def lifted(k):
        kern_re, kern_im = (kern_re_ref[k], kern_im_ref[k])
        shifted = jnp.concatenate(
            [spec_re * kern_re - spec_im * kern_im, spec_re * kern_im + spec_im * kern_re], axis=0
        )
        return product(as_first(shifted), lift[...])

    ahead = [lifted(k) for k in range(min(AHEAD, kernels))]
    total = None
    for k in range(kernels):
        if k + AHEAD < kernels:
            ahead.append(lifted(k + AHEAD))
        rows = ahead.pop(0)
        even_re, odd_re = (rows[:band, :middle], rows[:band, middle:])
        even_im, odd_im = (rows[band:, :middle], rows[band:, middle:])
        parts = []
        for value in (
            jnp.concatenate([even_re - odd_im, even_re + odd_im], axis=1),
            jnp.concatenate([even_im + odd_re, even_im - odd_re], axis=1),
        ):
            up, down = (value[: band // 2], value[band // 2 :])
            parts.append(product(cosine[...], as_second(up + down)))
            parts.append(product(sine[...], as_second(up - down)))
        even_re, odd_re, even_im, odd_im = parts
        near = (even_re - odd_im, even_im + odd_re)
        far = (even_re + odd_im, even_im - odd_re)
        for i, part in enumerate(near + far):
            field_ref[k, i] = part
        power = near[0] * near[0] + near[1] * near[1]
        mirrored = far[0] * far[0] + far[1] * far[1]
        total = (power, mirrored) if total is None else (total[0] + power, total[1] + mirrored)
    intensity_ref[:middle], intensity_ref[middle:] = total


def backward_kernel(tile, band, scale, *refs):
    part_mine, part_other, goal_ref, field_ref = refs[:4]
    fold_even, fold_odd, drop_even, drop_odd, kern_re_ref, kern_im_ref = refs[4:-2]
    resist_ref, back_ref = refs[-2:]
    middle = tile // 2
    intensity = part_mine[...] + part_other[...]
    resist = 1.0 / (1.0 + jnp.exp(-STEEP * (intensity - LEVEL)))
    resist_ref[...] = resist
    weight = 2.0 * (resist - goal_ref[...]) * STEEP * resist * (1.0 - resist)
    ahead_weight, mirrored_weight = (weight[:middle], weight[middle:])
    back_re = jnp.zeros((band, band), F32)
    back_im = jnp.zeros((band, band), F32)
    kernels = kern_re_ref.shape[0]

    def folded(k):
        near_re, near_im = (ahead_weight * field_ref[k, i] for i in range(2))
        far_re, far_im = (mirrored_weight * field_ref[k, i] for i in range(2, 4))
        columns = []
        for even, odd in (
            (near_re + far_re, near_im - far_im),
            (near_im + far_im, far_re - near_re),
        ):
            even = product(fold_even[...], jnp.concatenate(split(even), axis=0))
            odd = product(fold_odd[...], jnp.concatenate(split(odd), axis=0))
            even = even[: band // 2] + even[band // 2 :]
            odd = odd[: band // 2] + odd[band // 2 :]
            columns += [even + odd, even - odd]
        return jnp.concatenate(columns, axis=0)

    def dropped(value, table):
        pair = product(jnp.concatenate(split(value), axis=1), table[...])
        return pair[:, :band] + pair[:, band:]

    ahead = folded(0)
    for k in range(kernels):
        rows = ahead
        if k + 1 < kernels:
            ahead = folded(k + 1)
        even = dropped(rows[:, :middle] + rows[:, middle:], drop_even)
        odd = dropped(rows[:, :middle] - rows[:, middle:], drop_odd)
        part_re = even[:band] + odd[band:]
        part_im = even[band:] - odd[:band]
        kern_re, kern_im = (kern_re_ref[k], kern_im_ref[k])
        back_re = back_re + (kern_re * part_re + kern_im * part_im)
        back_im = back_im + (kern_re * part_im - kern_im * part_re)
    back_ref[...] = jnp.concatenate([back_re, back_im], axis=1) * scale


def margin_kernel(turns, tile, band, *refs):
    back_mine, back_other, c_high, c_low, m_high, m_low, back_ref, row_ref = refs[:8]
    place = Place()
    back = 2.0 * (back_mine[...] + back_other[...])
    back_ref[...] = back

    def strip_rows(ref):
        picked = [
            jnp.where(place.down, ref[base : base + HALO], ref[base + HALO : base + 2 * HALO])
            for base in (0, 2 * HALO)
        ]
        return jnp.concatenate(picked, axis=0)

    lift = dot((strip_rows(m_high), strip_rows(m_low)), split(back), product_turned)
    lift = jnp.concatenate([lift[:HALO], lift[HALO:]], axis=1)
    strip = dot(split(lift), (c_high[...], c_low[...]))
    row_ref[...] = strip[:, :tile]
    for turn in range(turns):
        upper = jnp.logical_not(place.rightward(turn))
        refs[8 + turn][...] = pack(strip[:, tile:], upper)


def side_kernel(turns, tile, band, *refs):
    back_ref, c_high, c_low, r_high, r_low, lift_ref = refs[:6]
    place = Place()
    lift = dot((r_high[...], r_low[...]), split(back_ref[...]), product_turned)
    lift = jnp.concatenate([lift[:tile], lift[tile:]], axis=1)
    lift_ref[...] = lift
    if turns:
        side = dot(split(lift), (c_high[:, tile:], c_low[:, tile:]))
        for turn in range(turns):
            refs[6 + turn][...] = pack(side, jnp.logical_not(place.rightward(turn)))


def core_kernel(tile, lift_ref, c_high, c_low, core_ref):
    core_ref[...] = dot(split(lift_ref[...]), (c_high[:, :tile], c_low[:, :tile]))


def resist_kernel(resist_ref, order, out_ref):
    high, low = split(resist_ref[...])
    turned = product(high, order[...]) + product(low, order[...])
    high, low = split(turned.T)
    out_ref[...] = product(high, order[...]) + product(low, order[...])


def spread_sides(place, refs, tile):
    merged = merge_sides(place, refs, True)
    lane = lax.broadcasted_iota(jnp.int32, merged.shape, 1)
    first = jnp.where(lane < HALO, merged, 0.0)
    last = jnp.where(lane >= HALO, merged, 0.0)
    middle = jnp.zeros((merged.shape[0], tile - 2 * merged.shape[1]), F32)
    return jnp.concatenate([first, middle, last] if middle.shape[1] else [first, last], axis=1)


def add_corners_kernel(turns, row_ref, *refs):
    place = Place()
    refs[turns][...] = row_ref[...] + spread_sides(place, refs[:turns], row_ref.shape[1])


def merge_kernel(turns, tile, core_ref, row_mine, row_other, *refs):
    place = Place()
    total = core_ref[...]
    if turns:
        total = total + spread_sides(place, refs[:turns], tile)
    mine, other = (row_mine[...], row_other[...])
    out_ref = refs[turns]
    bottom = jnp.where(place.has_below, jnp.where(place.down, mine, other), 0.0)
    top = jnp.where(place.has_above, jnp.where(place.down, other, mine), 0.0)
    out_ref[:HALO] = total[:HALO] + top
    out_ref[HALO : tile - HALO] = total[HALO : tile - HALO]
    out_ref[tile - HALO :] = total[tile - HALO :] + bottom


def call(kernel, out_shape, operands, in_hbm=(), **options):
    in_vmem = pl.BlockSpec(memory_space=pltpu.VMEM)
    anywhere = pl.BlockSpec(memory_space=pltpu.HBM)
    operands = [
        pltpu.with_memory_space_constraint(operand, pltpu.HBM) if i in in_hbm else operand
        for i, operand in enumerate(operands)
    ]
    return pl.pallas_call(
        kernel,
        out_shape=out_shape,
        in_specs=[anywhere if i in in_hbm else in_vmem for i in range(len(operands))],
        out_specs=jax.tree.map(lambda _: in_vmem, out_shape),
        compiler_params=pltpu.CompilerParams(vmem_limit_bytes=VMEM_LIMIT),
        **options,
    )(*operands)


def exchange(row, sides, corners, beside, join, joined_rows):
    turns = side_turns()
    row = swap_rows(row)
    corners = [swap_rows(corners[turn], turn) for turn in range(turns)]
    sides = [swap_side(sides[turn], turn) for turn in range(turns)]
    row, corners, beside = lax.optimization_barrier((row, corners, beside))
    if turns:
        joined = pltpu.VMEM((joined_rows, row.shape[1]), F32)
        row = call(
            functools.partial(join, turns), joined, [row, *corners], cost_estimate=cost(4 << 30)
        )
    return ([row, swap_cores(row), *sides], beside)


def on_device(mask, target, spectra):
    tile = mask.shape[0]
    band = spectra.shape[-1]
    window = tile + 2 * HALO
    scale = 1.0 / (window * window)
    turns = side_turns()
    image = pltpu.VMEM((tile, tile), F32)
    row_strip = pltpu.VMEM((HALO, tile), F32)
    side_strips = [pltpu.VMEM((tile // 2, 2 * HALO), F32)] * turns
    corner_strips = [pltpu.VMEM((HALO // 2, 2 * HALO), F32)] * turns
    wide = pltpu.VMEM((band, 2 * band), F32)

    row, *packed = call(
        functools.partial(prepare_kernel, turns, tile),
        (row_strip, *side_strips, *corner_strips),
        [mask],
    )
    tables = {
        name: [jnp.asarray(t) for t in group] for name, group in make_tables(band, tile).items()
    }
    row, mask = lax.optimization_barrier((row, mask))
    sources = [*tables["window"], target, spectra, *tables["forward"]]
    kept = sources[:3] + sources[4:]
    turned = pltpu.VMEM(spectra.shape[1:], F32)
    part, goal, ordered_re, *shared = call(
        functools.partial(own_kernel, tile, len(sources)),
        (
            pltpu.VMEM((2 * band, tile), F32),
            image,
            turned,
            *[pltpu.VMEM(source.shape, source.dtype) for source in kept],
        ),
        [mask, *sources],
        in_hbm=range(1, 1 + len(sources)),
        scratch_shapes=[
            pltpu.VMEM(target.shape, target.dtype),
            pltpu.SemaphoreType.DMA((len(sources),)),
        ],
    )
    columns, tile_order, order = (shared[0:2], shared[2], shared[4])
    own_rows, margin_rows = (shared[5:7], shared[7:9])
    (mine, other, *sides), (part, spectra) = exchange(
        row,
        packed[:turns],
        packed[turns:],
        (part, shared[3]),
        join_kernel,
        HALO + turns * HALO // 4,
    )
    ordered_im = call(order_kernel, turned, [spectra, order])
    part, ordered_im = lax.optimization_barrier((part, ordered_im))
    ordered = [ordered_re, ordered_im]
    spectrum = call(
        functools.partial(beside_kernel, turns, tile, band),
        wide,
        [part, *sides, *columns, *own_rows],
        cost_estimate=cost(3 << 30),
    )
    intensity, field = call(
        functools.partial(forward_kernel, turns, tile, band, scale),
        (image, pltpu.VMEM((spectra.shape[1], 4, tile // 2, tile), F32)),
        [
            spectrum,
            mine,
            other,
            *columns,
            *margin_rows,
            *shared[9:],
            *ordered,
        ],
    )
    sources = tables["backward"]
    backward = call(
        functools.partial(late_kernel, len(sources)),
        tuple(pltpu.VMEM(source.shape, source.dtype) for source in sources),
        [intensity, *sources],
        in_hbm=range(1, 1 + len(sources)),
        scratch_shapes=[pltpu.SemaphoreType.DMA((len(sources),))],
    )
    resist, back = call(
        functools.partial(backward_kernel, tile, band, scale),
        (image, wide),
        [intensity, swap_cores(intensity), goal, field, *backward, *ordered],
    )
    back, row, *corners = call(
        functools.partial(margin_kernel, turns, tile, band),
        (wide, row_strip, *corner_strips),
        [back, swap_cores(back), *columns, *margin_rows],
    )
    lift, *sides = call(
        functools.partial(side_kernel, turns, tile, band),
        (pltpu.VMEM((tile, 2 * band), F32), *side_strips),
        [back, *columns, *own_rows],
    )
    sides, resist = lax.optimization_barrier((sides, resist))
    resist = call(resist_kernel, jax.ShapeDtypeStruct((tile, tile), F32), [resist, tile_order])
    received, (lift, resist) = exchange(
        row, sides, corners, (lift, resist), add_corners_kernel, HALO
    )
    core = call(functools.partial(core_kernel, tile), image, [lift, *columns])
    grad = call(
        functools.partial(merge_kernel, turns, tile),
        jax.ShapeDtypeStruct((tile, tile), F32),
        [core, *received],
    )
    return (resist, grad)


def solution(mesh):
    return jax.shard_map(
        on_device,
        mesh=mesh,
        in_specs=(P("ty", "tx"), P("ty", "tx"), P(None, "kern", None, None)),
        out_specs=(P("ty", "tx"), P("ty", "tx")),
        check_vma=False,
    )
```

```python
import functools
import math

import jax
import jax.numpy as jnp
import ml_dtypes
import numpy as np
from jax import lax
from jax.experimental import pallas as pl
from jax.experimental.pallas import tpu as pltpu
from jax.sharding import PartitionSpec as P

HALO = 64
STEEP = 8.0
LEVEL = 1.0
F32 = jnp.float32
BF16 = jnp.bfloat16
AHEAD = 4


def cost(flops):
    return pl.CostEstimate(flops=flops, bytes_accessed=1 << 20, transcendentals=0)


VMEM_LIMIT = 24 * 1024 * 1024


def table_parts(table):
    high = table.astype(np.float32).astype(ml_dtypes.bfloat16)
    low = (table - high.astype(np.float64)).astype(np.float32).astype(ml_dtypes.bfloat16)
    return (high, low)


def signed_order(count):
    return np.concatenate([np.arange(count // 2, count), np.arange(count // 2)[::-1]])


def permutation(count):
    return np.eye(count)[signed_order(count)].astype(ml_dtypes.bfloat16)


def make_tables(band, tile):
    window = tile + 2 * HALO
    unit = 2.0 * math.pi / window
    natural = np.arange(band) - band // 2
    signed = signed_order(band) - band // 2
    places = np.concatenate([np.arange(HALO, window), np.arange(HALO)]) - (window - 1) / 2

    def blocks(frequency):
        angle = places[:, None] * frequency[None, :] * unit
        cosine, sine = (np.cos(angle), np.sin(angle))
        return np.block([[cosine, -sine], [sine, cosine]])

    rows = blocks(natural)
    halves = np.concatenate([rows[:window, :band], rows[window:, :band]], axis=1)
    own, margin = (halves[:tile], halves[tile:])
    columns = np.ascontiguousarray(blocks(signed).T[:, :window])

    pixel = np.arange(tile // 2) + 0.5
    angle = (natural + 0.5)[:, None] * pixel[None, :] * unit
    lift = np.concatenate([np.cos(angle), np.sin(angle)], axis=1)
    drops = (np.cos(angle.T), np.sin(angle.T))
    half = pixel[:, None] * (np.arange(band // 2) + 0.5)[None, :] * unit
    cosine, sine = (np.cos(half), np.sin(half))

    def first(table):
        high, low = table_parts(table)
        return np.concatenate([high, low, high], axis=1)

    def second(table):
        high, low = table_parts(table)
        return np.concatenate([high, high, low], axis=0)

    def paired(table):
        high, low = table_parts(table)
        return np.block([[high, low], [high, np.zeros_like(low)]])

    return {
        "window": (*table_parts(columns), permutation(tile)),
        "forward": (
            permutation(band),
            *table_parts(own),
            *table_parts(margin),
            second(lift),
            first(cosine),
            first(sine),
        ),
        "backward": (
            *[np.ascontiguousarray(paired(table).T) for table in (cosine, sine)],
            *[paired(table) for table in drops],
        ),
    }


def split(value):
    high = value.astype(BF16)
    return (high, (value - high.astype(F32)).astype(BF16))


def product(a, b):
    return jnp.dot(a, b, preferred_element_type=F32)


def product_turned(a, b):
    return lax.dot_general(a, b, (((1,), (1,)), ((), ())), preferred_element_type=F32)


def dot(first, second, multiply=product):
    return multiply(first[0], second[0]) + (
        multiply(first[1], second[0]) + multiply(first[0], second[1])
    )


def as_first(value):
    high, low = split(value)
    return jnp.concatenate([high, low, high], axis=1)


def as_second(value):
    high, low = split(value)
    return jnp.concatenate([high, high, low], axis=0)


class Place:
    def __init__(self):
        core, ty, tx = (lax.axis_index(name) for name in ("kern", "ty", "tx"))
        self.down = lax.rem(ty + core, 2) == 0
        self.has_below = ty < lax.axis_size("ty") - 1
        self.has_above = ty > 0
        self.has_right = tx < lax.axis_size("tx") - 1
        self.has_left = tx > 0
        self.tx = tx

    def rightward(self, turn):
        return lax.rem(self.tx + turn, 2) == 0


def side_turns():
    count = lax.axis_size("tx")
    return 0 if count == 1 else 1 if count == 2 else 2


def partners(count, turn):
    found = [((i - turn) ^ 1) + turn for i in range(count)]
    return [j if 0 <= j < count else i for i, j in enumerate(found)]


def row_pairs(side_turn):
    rows, columns = (lax.axis_size("ty"), lax.axis_size("tx"))
    beside = partners(columns, 0)
    moved = list(range(columns)) if side_turn is None else partners(columns, side_turn)
    pairs = []
    for core in range(2):
        met = partners(rows, core)
        for ty in range(rows):
            for tx in range(columns):
                to = (met[ty], moved[tx]) if met[ty] != ty else (ty, beside[tx])
                base = core * rows * columns
                pairs.append((base + ty * columns + tx, base + to[0] * columns + to[1]))
    return pairs


def swap_cores(value):
    return lax.ppermute(value, "kern", [(0, 1), (1, 0)])


def swap_rows(value, side_turn=None):
    return lax.ppermute(value, ("kern", "ty", "tx"), row_pairs(side_turn))


def swap_side(value, turn):
    return lax.ppermute(value, "tx", list(enumerate(partners(lax.axis_size("tx"), turn))))


def half_turn(value):
    return pltpu.roll(value, HALO, 1)


def pack(block, upper):
    rows = block.shape[0] // 2
    first, last = (block[:rows], block[rows:])
    lane = lax.broadcasted_iota(jnp.int32, first.shape, 1)
    return jnp.where(
        lane < HALO,
        jnp.where(upper, half_turn(first), first),
        jnp.where(upper, last, half_turn(last)),
    )


def unpack(packed, upper):
    turned = half_turn(packed)
    return jnp.concatenate(
        [jnp.where(upper, turned, packed), jnp.where(upper, packed, turned)], axis=0
    )


def merge_sides(place, refs, right_is_upper):
    total = None
    for turn, ref in enumerate(refs):
        right = place.rightward(turn)
        there = jnp.where(right, place.has_right, place.has_left)
        upper = right if right_is_upper else jnp.logical_not(right)
        block = unpack(ref[...], upper)
        lane = lax.broadcasted_iota(jnp.int32, block.shape, 1)
        mine = jnp.logical_and((lane >= HALO) == upper, there)
        block = jnp.where(mine, block, 0.0)
        total = block if total is None else total + block
    return total


def whole(halves):
    band = halves.shape[1] // 2
    cosine, sine = (halves[:, :band], halves[:, band:])
    return jnp.concatenate(
        [jnp.concatenate([cosine, -sine], axis=1), jnp.concatenate([sine, cosine], axis=1)], axis=0
    )


def start_copies(pairs, sems):
    moves = [pltpu.make_async_copy(a, b, sems.at[i]) for i, (a, b) in enumerate(pairs)]
    for move in moves:
        move.start()
    return moves


def prepare_kernel(turns, tile, mask_ref, row_ref, *refs):
    place = Place()
    block = mask_ref[...]
    strip = jnp.where(place.down, block[tile - HALO :], block[:HALO])
    row_ref[...] = strip
    for turn in range(turns):
        right = place.rightward(turn)
        for source, ref in ((block, refs[turn]), (strip, refs[turns + turn])):
            ref[...] = pack(
                jnp.where(right, source[:, tile - 2 * HALO :], source[:, : 2 * HALO]), right
            )


def own_kernel(tile, sources_count, mask_ref, *refs):
    sources, outs = (refs[:sources_count], refs[sources_count:])
    part_ref, goal_ref, ordered_ref, *copies, target_ref, sems = outs
    moves = start_copies(zip(sources, [*copies[:3], target_ref, *copies[3:]]), sems)
    for move in moves[:2]:
        move.wait()
    part_ref[...] = dot(
        (copies[0][:, :tile], copies[1][:, :tile]), split(mask_ref[...]), product_turned
    )
    for move in moves[2:4]:
        move.wait()
    order = copies[2][...]
    goal = product_turned(order, target_ref[...].astype(F32).astype(BF16))
    goal_ref[...] = product_turned(goal.astype(BF16), order)
    for move in moves[4:]:
        move.wait()
    turn_spectra(copies[3].at[0], copies[4][...], ordered_ref)


def turn_spectra(source_ref, order, ordered_ref):
    band = order.shape[0]
    for start in range(0, source_ref.shape[0], 2):
        group = range(start, min(start + 2, source_ref.shape[0]))
        high, low = split(jnp.concatenate([source_ref[k] for k in group], axis=0))
        turned = product_turned(order, high) + product_turned(order, low)
        for place_in, k in enumerate(group):
            ordered_ref[k] = turned[:, place_in * band : (place_in + 1) * band]


def order_kernel(spectra_ref, order_ref, ordered_ref):
    turn_spectra(spectra_ref.at[1], order_ref[...], ordered_ref)


def late_kernel(sources_count, after_ref, *refs):
    sources, copies, sems = (refs[:sources_count], refs[sources_count:-1], refs[-1])
    for move in start_copies(zip(sources, copies), sems):
        move.wait()


def beside_kernel(turns, tile, band, *refs):
    part_ref, *sides = refs[: 1 + turns]
    c_high, c_low, r_high, r_low, spectrum_ref = refs[1 + turns :]
    place = Place()
    part = part_ref[...]
    if turns:
        side = merge_sides(place, sides, False)
        part = part + dot(
            (c_high[:, tile:], c_low[:, tile:]), split(side), product_turned
        )
    part = jnp.concatenate([part[:band], part[band:]], axis=1)
    spectrum_ref[...] = dot(split(part), (whole(r_high[...]), whole(r_low[...])))


def join_kernel(turns, row_ref, *refs):
    corners, out_ref = (refs[:turns], refs[turns])
    rows = row_ref.shape[0]
    out_ref[:rows] = row_ref[...]
    for turn in range(turns):
        corner = corners[turn][...]
        half = corner.shape[0] // 2
        start = rows + turn * half
        out_ref[start : start + half] = jnp.concatenate([corner[:half], corner[half:]], axis=1)


def split_joined(joined, turns):
    half = HALO // 4
    corners = []
    for turn in range(turns):
        corner = joined[HALO + turn * half : HALO + (turn + 1) * half]
        lanes = 2 * HALO
        corners.append(jnp.concatenate([corner[:, :lanes], corner[:, lanes:]], axis=0))
    return (joined[:HALO], corners)


def forward_kernel(turns, tile, band, scale, *refs):
    spectrum_ref, joined_mine, joined_other = refs[:3]
    (c_high, c_low, m_high, m_low, lift, cosine, sine, kern_re_ref, kern_im_ref) = refs[3:-2]
    row_mine, corners_mine = split_joined(joined_mine[...], turns)
    row_other, corners_other = split_joined(joined_other[...], turns)
    intensity_ref, field_ref = refs[-2:]
    place = Place()

    def margins(mine, other):
        below = jnp.where(place.has_below, jnp.where(place.down, mine, other), 0.0)
        above = jnp.where(place.has_above, jnp.where(place.down, other, mine), 0.0)
        return jnp.concatenate([below, above], axis=0)

    strips = margins(row_mine, row_other)
    if turns:
        corners = margins(
            merge_sides(place, corners_mine, False), merge_sides(place, corners_other, False)
        )
    else:
        corners = jnp.zeros((strips.shape[0], 2 * HALO), F32)
    strips = jnp.concatenate([strips, corners], axis=1)
    part = dot((c_high[...], c_low[...]), split(strips), product_turned)
    part = jnp.concatenate([part[:band], part[band:]], axis=1)
    spectrum = spectrum_ref[...] + dot(split(part), (whole(m_high[...]), whole(m_low[...])))
    spectrum = spectrum * scale
    spec_re, spec_im = (spectrum[:, :band], spectrum[:, band:])

    middle = tile // 2
    kernels = kern_re_ref.shape[0]

    def lifted(k):
        kern_re, kern_im = (kern_re_ref[k], kern_im_ref[k])
        shifted = jnp.concatenate(
            [spec_re * kern_re - spec_im * kern_im, spec_re * kern_im + spec_im * kern_re], axis=0
        )
        return product(as_first(shifted), lift[...])

    ahead = [lifted(k) for k in range(min(AHEAD, kernels))]
    total = None
    for k in range(kernels):
        if k + AHEAD < kernels:
            ahead.append(lifted(k + AHEAD))
        rows = ahead.pop(0)
        even_re, odd_re = (rows[:band, :middle], rows[:band, middle:])
        even_im, odd_im = (rows[band:, :middle], rows[band:, middle:])
        parts = []
        for value in (
            jnp.concatenate([even_re - odd_im, even_re + odd_im], axis=1),
            jnp.concatenate([even_im + odd_re, even_im - odd_re], axis=1),
        ):
            up, down = (value[: band // 2], value[band // 2 :])
            parts.append(product(cosine[...], as_second(up + down)))
            parts.append(product(sine[...], as_second(up - down)))
        even_re, odd_re, even_im, odd_im = parts
        near = (even_re - odd_im, even_im + odd_re)
        far = (even_re + odd_im, even_im - odd_re)
        for i, part in enumerate(near + far):
            field_ref[k, i] = part
        power = near[0] * near[0] + near[1] * near[1]
        mirrored = far[0] * far[0] + far[1] * far[1]
        total = (power, mirrored) if total is None else (total[0] + power, total[1] + mirrored)
    intensity_ref[:middle], intensity_ref[middle:] = total


def backward_kernel(tile, band, scale, *refs):
    part_mine, part_other, goal_ref, field_ref = refs[:4]
    fold_even, fold_odd, drop_even, drop_odd, kern_re_ref, kern_im_ref = refs[4:-2]
    resist_ref, back_ref = refs[-2:]
    middle = tile // 2
    intensity = part_mine[...] + part_other[...]
    resist = 1.0 / (1.0 + jnp.exp(-STEEP * (intensity - LEVEL)))
    resist_ref[...] = resist
    weight = 2.0 * (resist - goal_ref[...]) * STEEP * resist * (1.0 - resist)
    ahead_weight, mirrored_weight = (weight[:middle], weight[middle:])
    back_re = jnp.zeros((band, band), F32)
    back_im = jnp.zeros((band, band), F32)
    kernels = kern_re_ref.shape[0]

    def folded(k):
        near_re, near_im = (ahead_weight * field_ref[k, i] for i in range(2))
        far_re, far_im = (mirrored_weight * field_ref[k, i] for i in range(2, 4))
        columns = []
        for even, odd in (
            (near_re + far_re, near_im - far_im),
            (near_im + far_im, far_re - near_re),
        ):
            even = product(fold_even[...], jnp.concatenate(split(even), axis=0))
            odd = product(fold_odd[...], jnp.concatenate(split(odd), axis=0))
            even = even[: band // 2] + even[band // 2 :]
            odd = odd[: band // 2] + odd[band // 2 :]
            columns += [even + odd, even - odd]
        return jnp.concatenate(columns, axis=0)

    def dropped(value, table):
        pair = product(jnp.concatenate(split(value), axis=1), table[...])
        return pair[:, :band] + pair[:, band:]

    ahead = folded(0)
    for k in range(kernels):
        rows = ahead
        if k + 1 < kernels:
            ahead = folded(k + 1)
        even = dropped(rows[:, :middle] + rows[:, middle:], drop_even)
        odd = dropped(rows[:, :middle] - rows[:, middle:], drop_odd)
        part_re = even[:band] + odd[band:]
        part_im = even[band:] - odd[:band]
        kern_re, kern_im = (kern_re_ref[k], kern_im_ref[k])
        back_re = back_re + (kern_re * part_re + kern_im * part_im)
        back_im = back_im + (kern_re * part_im - kern_im * part_re)
    back_ref[...] = jnp.concatenate([back_re, back_im], axis=1) * scale


def margin_kernel(turns, tile, band, *refs):
    back_mine, back_other, c_high, c_low, m_high, m_low, back_ref, row_ref = refs[:8]
    place = Place()
    back = 2.0 * (back_mine[...] + back_other[...])
    back_ref[...] = back

    def strip_rows(ref):
        picked = [
            jnp.where(place.down, ref[base : base + HALO], ref[base + HALO : base + 2 * HALO])
            for base in (0, 2 * HALO)
        ]
        return jnp.concatenate(picked, axis=0)

    lift = dot((strip_rows(whole(m_high[...])), strip_rows(whole(m_low[...]))), split(back), product_turned)
    lift = jnp.concatenate([lift[:HALO], lift[HALO:]], axis=1)
    strip = dot(split(lift), (c_high[...], c_low[...]))
    row_ref[...] = strip[:, :tile]
    for turn in range(turns):
        upper = jnp.logical_not(place.rightward(turn))
        refs[8 + turn][...] = pack(strip[:, tile:], upper)


def side_kernel(turns, tile, band, *refs):
    back_ref, c_high, c_low, r_high, r_low, lift_ref = refs[:6]
    place = Place()
    lift = dot((whole(r_high[...]), whole(r_low[...])), split(back_ref[...]), product_turned)
    lift = jnp.concatenate([lift[:tile], lift[tile:]], axis=1)
    lift_ref[...] = lift
    if turns:
        side = dot(split(lift), (c_high[:, tile:], c_low[:, tile:]))
        for turn in range(turns):
            refs[6 + turn][...] = pack(side, jnp.logical_not(place.rightward(turn)))


def core_kernel(tile, lift_ref, c_high, c_low, core_ref):
    core_ref[...] = dot(split(lift_ref[...]), (c_high[:, :tile], c_low[:, :tile]))


def resist_kernel(resist_ref, order, out_ref):
    high, low = split(resist_ref[...])
    turned = product(high, order[...]) + product(low, order[...])
    high, low = split(turned.T)
    out_ref[...] = product(high, order[...]) + product(low, order[...])


def spread_sides(place, refs, tile):
    merged = merge_sides(place, refs, True)
    lane = lax.broadcasted_iota(jnp.int32, merged.shape, 1)
    first = jnp.where(lane < HALO, merged, 0.0)
    last = jnp.where(lane >= HALO, merged, 0.0)
    middle = jnp.zeros((merged.shape[0], tile - 2 * merged.shape[1]), F32)
    return jnp.concatenate([first, middle, last] if middle.shape[1] else [first, last], axis=1)


def add_corners_kernel(turns, row_ref, *refs):
    place = Place()
    refs[turns][...] = row_ref[...] + spread_sides(place, refs[:turns], row_ref.shape[1])


def merge_kernel(turns, tile, core_ref, row_mine, row_other, *refs):
    place = Place()
    total = core_ref[...]
    if turns:
        total = total + spread_sides(place, refs[:turns], tile)
    mine, other = (row_mine[...], row_other[...])
    out_ref = refs[turns]
    bottom = jnp.where(place.has_below, jnp.where(place.down, mine, other), 0.0)
    top = jnp.where(place.has_above, jnp.where(place.down, other, mine), 0.0)
    out_ref[:HALO] = total[:HALO] + top
    out_ref[HALO : tile - HALO] = total[HALO : tile - HALO]
    out_ref[tile - HALO :] = total[tile - HALO :] + bottom


def call(kernel, out_shape, operands, in_hbm=(), **options):
    in_vmem = pl.BlockSpec(memory_space=pltpu.VMEM)
    anywhere = pl.BlockSpec(memory_space=pltpu.HBM)
    operands = [
        pltpu.with_memory_space_constraint(operand, pltpu.HBM) if i in in_hbm else operand
        for i, operand in enumerate(operands)
    ]
    return pl.pallas_call(
        kernel,
        out_shape=out_shape,
        in_specs=[anywhere if i in in_hbm else in_vmem for i in range(len(operands))],
        out_specs=jax.tree.map(lambda _: in_vmem, out_shape),
        compiler_params=pltpu.CompilerParams(vmem_limit_bytes=VMEM_LIMIT),
        **options,
    )(*operands)


def exchange(row, sides, corners, beside, join, joined_rows):
    turns = side_turns()
    row = swap_rows(row)
    corners = [swap_rows(corners[turn], turn) for turn in range(turns)]
    sides = [swap_side(sides[turn], turn) for turn in range(turns)]
    row, corners, beside = lax.optimization_barrier((row, corners, beside))
    if turns:
        joined = pltpu.VMEM((joined_rows, row.shape[1]), F32)
        row = call(
            functools.partial(join, turns), joined, [row, *corners], cost_estimate=cost(4 << 30)
        )
    return ([row, swap_cores(row), *sides], beside)


def on_device(mask, target, spectra):
    tile = mask.shape[0]
    band = spectra.shape[-1]
    window = tile + 2 * HALO
    scale = 1.0 / (window * window)
    turns = side_turns()
    image = pltpu.VMEM((tile, tile), F32)
    row_strip = pltpu.VMEM((HALO, tile), F32)
    side_strips = [pltpu.VMEM((tile // 2, 2 * HALO), F32)] * turns
    corner_strips = [pltpu.VMEM((HALO // 2, 2 * HALO), F32)] * turns
    wide = pltpu.VMEM((band, 2 * band), F32)

    row, *packed = call(
        functools.partial(prepare_kernel, turns, tile),
        (row_strip, *side_strips, *corner_strips),
        [mask],
    )
    tables = {
        name: [jnp.asarray(t) for t in group] for name, group in make_tables(band, tile).items()
    }
    row, mask = lax.optimization_barrier((row, mask))
    sources = [*tables["window"], target, spectra, *tables["forward"]]
    kept = sources[:3] + sources[4:]
    turned = pltpu.VMEM(spectra.shape[1:], F32)
    part, goal, ordered_re, *shared = call(
        functools.partial(own_kernel, tile, len(sources)),
        (
            pltpu.VMEM((2 * band, tile), F32),
            image,
            turned,
            *[pltpu.VMEM(source.shape, source.dtype) for source in kept],
        ),
        [mask, *sources],
        in_hbm=range(1, 1 + len(sources)),
        scratch_shapes=[
            pltpu.VMEM(target.shape, target.dtype),
            pltpu.SemaphoreType.DMA((len(sources),)),
        ],
    )
    columns, tile_order, order = (shared[0:2], shared[2], shared[4])
    own_rows, margin_rows = (shared[5:7], shared[7:9])
    (mine, other, *sides), (part, spectra) = exchange(
        row,
        packed[:turns],
        packed[turns:],
        (part, shared[3]),
        join_kernel,
        HALO + turns * HALO // 4,
    )
    ordered_im = call(order_kernel, turned, [spectra, order])
    part, ordered_im = lax.optimization_barrier((part, ordered_im))
    ordered = [ordered_re, ordered_im]
    spectrum = call(
        functools.partial(beside_kernel, turns, tile, band),
        wide,
        [part, *sides, *columns, *own_rows],
        cost_estimate=cost(3 << 30),
    )
    intensity, field = call(
        functools.partial(forward_kernel, turns, tile, band, scale),
        (image, pltpu.VMEM((spectra.shape[1], 4, tile // 2, tile), F32)),
        [
            spectrum,
            mine,
            other,
            *columns,
            *margin_rows,
            *shared[9:],
            *ordered,
        ],
    )
    sources = tables["backward"]
    backward = call(
        functools.partial(late_kernel, len(sources)),
        tuple(pltpu.VMEM(source.shape, source.dtype) for source in sources),
        [intensity, *sources],
        in_hbm=range(1, 1 + len(sources)),
        scratch_shapes=[pltpu.SemaphoreType.DMA((len(sources),))],
    )
    resist, back = call(
        functools.partial(backward_kernel, tile, band, scale),
        (image, wide),
        [intensity, swap_cores(intensity), goal, field, *backward, *ordered],
    )
    back, row, *corners = call(
        functools.partial(margin_kernel, turns, tile, band),
        (wide, row_strip, *corner_strips),
        [back, swap_cores(back), *columns, *margin_rows],
    )
    lift, *sides = call(
        functools.partial(side_kernel, turns, tile, band),
        (pltpu.VMEM((tile, 2 * band), F32), *side_strips),
        [back, *columns, *own_rows],
    )
    sides, resist = lax.optimization_barrier((sides, resist))
    resist = call(resist_kernel, jax.ShapeDtypeStruct((tile, tile), F32), [resist, tile_order])
    received, (lift, resist) = exchange(
        row, sides, corners, (lift, resist), add_corners_kernel, HALO
    )
    core = call(functools.partial(core_kernel, tile), image, [lift, *columns])
    grad = call(
        functools.partial(merge_kernel, turns, tile),
        jax.ShapeDtypeStruct((tile, tile), F32),
        [core, *received],
    )
    return (resist, grad)


def solution(mesh):
    return jax.shard_map(
        on_device,
        mesh=mesh,
        in_specs=(P("ty", "tx"), P("ty", "tx"), P(None, "kern", None, None)),
        out_specs=(P("ty", "tx"), P("ty", "tx")),
        check_vma=False,
    )
```

```python
import functools
import math

import jax
import jax.numpy as jnp
import ml_dtypes
import numpy as np
from jax import lax
from jax.experimental import pallas as pl
from jax.experimental.pallas import tpu as pltpu
from jax.sharding import PartitionSpec as P

HALO = 64
STEEP = 8.0
LEVEL = 1.0
F32 = jnp.float32
BF16 = jnp.bfloat16
AHEAD = 4


def cost(flops):
    return pl.CostEstimate(flops=flops, bytes_accessed=1 << 20, transcendentals=0)


VMEM_LIMIT = 24 * 1024 * 1024


def table_parts(table):
    high = table.astype(np.float32).astype(ml_dtypes.bfloat16)
    low = (table - high.astype(np.float64)).astype(np.float32).astype(ml_dtypes.bfloat16)
    return (high, low)


def signed_order(count):
    return np.concatenate([np.arange(count // 2, count), np.arange(count // 2)[::-1]])


def permutation(count):
    return np.eye(count)[signed_order(count)].astype(ml_dtypes.bfloat16)


def make_tables(band, tile):
    window = tile + 2 * HALO
    unit = 2.0 * math.pi / window
    natural = np.arange(band) - band // 2
    signed = signed_order(band) - band // 2
    places = np.concatenate([np.arange(HALO, window), np.arange(HALO)]) - (window - 1) / 2

    def blocks(frequency):
        angle = places[:, None] * frequency[None, :] * unit
        cosine, sine = (np.cos(angle), np.sin(angle))
        return np.block([[cosine, -sine], [sine, cosine]])

    rows = blocks(natural)
    halves = np.concatenate([rows[:window, :band], rows[window:, :band]], axis=1)
    own, margin = (halves[:tile], halves[tile:])
    columns = np.ascontiguousarray(blocks(signed).T[:, :window])

    pixel = np.arange(tile // 2) + 0.5
    angle = (natural + 0.5)[:, None] * pixel[None, :] * unit
    lift = np.concatenate([np.cos(angle), np.sin(angle)], axis=1)
    drops = (np.cos(angle.T), np.sin(angle.T))
    half = pixel[:, None] * (np.arange(band // 2) + 0.5)[None, :] * unit
    cosine, sine = (np.cos(half), np.sin(half))

    def first(table):
        high, low = table_parts(table)
        return np.concatenate([high, low, high], axis=1)

    def paired(table):
        high, low = table_parts(table)
        return np.block([[high, low], [high, np.zeros_like(low)]])

    return {
        "window": (*table_parts(columns), permutation(tile)),
        "forward": (
            permutation(band),
            *table_parts(own),
            *table_parts(margin),
            np.concatenate(table_parts(lift), axis=0),
            first(cosine),
            first(sine),
        ),
        "backward": (
            *[np.ascontiguousarray(paired(table).T) for table in (cosine, sine)],
            *[paired(table) for table in drops],
        ),
    }


def split(value):
    high = value.astype(BF16)
    return (high, (value - high.astype(F32)).astype(BF16))


def product(a, b):
    return jnp.dot(a, b, preferred_element_type=F32)


def product_turned(a, b):
    return lax.dot_general(a, b, (((1,), (1,)), ((), ())), preferred_element_type=F32)


def dot(first, second, multiply=product):
    return multiply(first[0], second[0]) + (
        multiply(first[1], second[0]) + multiply(first[0], second[1])
    )


def as_first(value):
    high, low = split(value)
    return jnp.concatenate([high, low, high], axis=1)


def as_second(value):
    high, low = split(value)
    return jnp.concatenate([high, high, low], axis=0)


class Place:
    def __init__(self):
        core, ty, tx = (lax.axis_index(name) for name in ("kern", "ty", "tx"))
        self.down = lax.rem(ty + core, 2) == 0
        self.has_below = ty < lax.axis_size("ty") - 1
        self.has_above = ty > 0
        self.has_right = tx < lax.axis_size("tx") - 1
        self.has_left = tx > 0
        self.tx = tx

    def rightward(self, turn):
        return lax.rem(self.tx + turn, 2) == 0


def side_turns():
    count = lax.axis_size("tx")
    return 0 if count == 1 else 1 if count == 2 else 2


def partners(count, turn):
    found = [((i - turn) ^ 1) + turn for i in range(count)]
    return [j if 0 <= j < count else i for i, j in enumerate(found)]


def row_pairs(side_turn):
    rows, columns = (lax.axis_size("ty"), lax.axis_size("tx"))
    beside = partners(columns, 0)
    moved = list(range(columns)) if side_turn is None else partners(columns, side_turn)
    pairs = []
    for core in range(2):
        met = partners(rows, core)
        for ty in range(rows):
            for tx in range(columns):
                to = (met[ty], moved[tx]) if met[ty] != ty else (ty, beside[tx])
                base = core * rows * columns
                pairs.append((base + ty * columns + tx, base + to[0] * columns + to[1]))
    return pairs


def swap_cores(value):
    return lax.ppermute(value, "kern", [(0, 1), (1, 0)])


def swap_rows(value, side_turn=None):
    return lax.ppermute(value, ("kern", "ty", "tx"), row_pairs(side_turn))


def swap_side(value, turn):
    return lax.ppermute(value, "tx", list(enumerate(partners(lax.axis_size("tx"), turn))))


def half_turn(value):
    return pltpu.roll(value, HALO, 1)


def pack(block, upper):
    rows = block.shape[0] // 2
    first, last = (block[:rows], block[rows:])
    lane = lax.broadcasted_iota(jnp.int32, first.shape, 1)
    return jnp.where(
        lane < HALO,
        jnp.where(upper, half_turn(first), first),
        jnp.where(upper, last, half_turn(last)),
    )


def unpack(packed, upper):
    turned = half_turn(packed)
    return jnp.concatenate(
        [jnp.where(upper, turned, packed), jnp.where(upper, packed, turned)], axis=0
    )


def merge_sides(place, refs, right_is_upper):
    total = None
    for turn, ref in enumerate(refs):
        right = place.rightward(turn)
        there = jnp.where(right, place.has_right, place.has_left)
        upper = right if right_is_upper else jnp.logical_not(right)
        block = unpack(ref[...], upper)
        lane = lax.broadcasted_iota(jnp.int32, block.shape, 1)
        mine = jnp.logical_and((lane >= HALO) == upper, there)
        block = jnp.where(mine, block, 0.0)
        total = block if total is None else total + block
    return total


def whole(halves):
    band = halves.shape[1] // 2
    cosine, sine = (halves[:, :band], halves[:, band:])
    return jnp.concatenate(
        [jnp.concatenate([cosine, -sine], axis=1), jnp.concatenate([sine, cosine], axis=1)], axis=0
    )


def start_copies(pairs, sems):
    moves = [pltpu.make_async_copy(a, b, sems.at[i]) for i, (a, b) in enumerate(pairs)]
    for move in moves:
        move.start()
    return moves


def prepare_kernel(turns, tile, mask_ref, row_ref, *refs):
    place = Place()
    block = mask_ref[...]
    strip = jnp.where(place.down, block[tile - HALO :], block[:HALO])
    row_ref[...] = strip
    for turn in range(turns):
        right = place.rightward(turn)
        for source, ref in ((block, refs[turn]), (strip, refs[turns + turn])):
            ref[...] = pack(
                jnp.where(right, source[:, tile - 2 * HALO :], source[:, : 2 * HALO]), right
            )


def own_kernel(tile, sources_count, mask_ref, *refs):
    sources, outs = (refs[:sources_count], refs[sources_count:])
    part_ref, goal_ref, ordered_ref, *copies, target_ref, sems = outs
    moves = start_copies(zip(sources, [*copies[:3], target_ref, *copies[3:]]), sems)
    for move in moves[:2]:
        move.wait()
    part_ref[...] = dot(
        (copies[0][:, :tile], copies[1][:, :tile]), split(mask_ref[...]), product_turned
    )
    for move in moves[2:4]:
        move.wait()
    order = copies[2][...]
    goal = product_turned(order, target_ref[...].astype(F32).astype(BF16))
    goal_ref[...] = product_turned(goal.astype(BF16), order)
    for move in moves[4:]:
        move.wait()
    turn_spectra(copies[3].at[0], copies[4][...], ordered_ref)


def turn_spectra(source_ref, order, ordered_ref):
    band = order.shape[0]
    for start in range(0, source_ref.shape[0], 2):
        group = range(start, min(start + 2, source_ref.shape[0]))
        high, low = split(jnp.concatenate([source_ref[k] for k in group], axis=0))
        turned = product_turned(order, high) + product_turned(order, low)
        for place_in, k in enumerate(group):
            ordered_ref[k] = turned[:, place_in * band : (place_in + 1) * band]


def order_kernel(spectra_ref, order_ref, ordered_ref):
    turn_spectra(spectra_ref.at[1], order_ref[...], ordered_ref)


def late_kernel(sources_count, after_ref, *refs):
    sources, copies, sems = (refs[:sources_count], refs[sources_count:-1], refs[-1])
    for move in start_copies(zip(sources, copies), sems):
        move.wait()


def beside_kernel(turns, tile, band, *refs):
    part_ref, *sides = refs[: 1 + turns]
    c_high, c_low, r_high, r_low, spectrum_ref = refs[1 + turns :]
    place = Place()
    part = part_ref[...]
    if turns:
        side = merge_sides(place, sides, False)
        part = part + dot(
            (c_high[:, tile:], c_low[:, tile:]), split(side), product_turned
        )
    part = jnp.concatenate([part[:band], part[band:]], axis=1)
    spectrum_ref[...] = dot(split(part), (whole(r_high[...]), whole(r_low[...])))


def join_kernel(turns, row_ref, *refs):
    corners, out_ref = (refs[:turns], refs[turns])
    rows = row_ref.shape[0]
    out_ref[:rows] = row_ref[...]
    for turn in range(turns):
        corner = corners[turn][...]
        half = corner.shape[0] // 2
        start = rows + turn * half
        out_ref[start : start + half] = jnp.concatenate([corner[:half], corner[half:]], axis=1)


def split_joined(joined, turns):
    half = HALO // 4
    corners = []
    for turn in range(turns):
        corner = joined[HALO + turn * half : HALO + (turn + 1) * half]
        lanes = 2 * HALO
        corners.append(jnp.concatenate([corner[:, :lanes], corner[:, lanes:]], axis=0))
    return (joined[:HALO], corners)


def forward_kernel(turns, tile, band, scale, *refs):
    spectrum_ref, joined_mine, joined_other = refs[:3]
    (c_high, c_low, m_high, m_low, lift, cosine, sine, kern_re_ref, kern_im_ref) = refs[3:-2]
    row_mine, corners_mine = split_joined(joined_mine[...], turns)
    row_other, corners_other = split_joined(joined_other[...], turns)
    intensity_ref, field_ref = refs[-2:]
    place = Place()

    def margins(mine, other):
        below = jnp.where(place.has_below, jnp.where(place.down, mine, other), 0.0)
        above = jnp.where(place.has_above, jnp.where(place.down, other, mine), 0.0)
        return jnp.concatenate([below, above], axis=0)

    strips = margins(row_mine, row_other)
    if turns:
        corners = margins(
            merge_sides(place, corners_mine, False), merge_sides(place, corners_other, False)
        )
    else:
        corners = jnp.zeros((strips.shape[0], 2 * HALO), F32)
    strips = jnp.concatenate([strips, corners], axis=1)
    part = dot((c_high[...], c_low[...]), split(strips), product_turned)
    part = jnp.concatenate([part[:band], part[band:]], axis=1)
    spectrum = spectrum_ref[...] + dot(split(part), (whole(m_high[...]), whole(m_low[...])))
    spectrum = spectrum * scale
    spec_re, spec_im = (spectrum[:, :band], spectrum[:, band:])

    middle = tile // 2
    kernels = kern_re_ref.shape[0]
    lift_table = jnp.concatenate([lift[:band], lift[...]], axis=0)

    def lifted(k):
        kern_re, kern_im = (kern_re_ref[k], kern_im_ref[k])
        shifted = jnp.concatenate(
            [spec_re * kern_re - spec_im * kern_im, spec_re * kern_im + spec_im * kern_re], axis=0
        )
        return product(as_first(shifted), lift_table)

    ahead = [lifted(k) for k in range(min(AHEAD, kernels))]
    total = None
    for k in range(kernels):
        if k + AHEAD < kernels:
            ahead.append(lifted(k + AHEAD))
        rows = ahead.pop(0)
        even_re, odd_re = (rows[:band, :middle], rows[:band, middle:])
        even_im, odd_im = (rows[band:, :middle], rows[band:, middle:])
        parts = []
        for value in (
            jnp.concatenate([even_re - odd_im, even_re + odd_im], axis=1),
            jnp.concatenate([even_im + odd_re, even_im - odd_re], axis=1),
        ):
            up, down = (value[: band // 2], value[band // 2 :])
            parts.append(product(cosine[...], as_second(up + down)))
            parts.append(product(sine[...], as_second(up - down)))
        even_re, odd_re, even_im, odd_im = parts
        near = (even_re - odd_im, even_im + odd_re)
        far = (even_re + odd_im, even_im - odd_re)
        for i, part in enumerate(near + far):
            field_ref[k, i] = part
        power = near[0] * near[0] + near[1] * near[1]
        mirrored = far[0] * far[0] + far[1] * far[1]
        total = (power, mirrored) if total is None else (total[0] + power, total[1] + mirrored)
    intensity_ref[:middle], intensity_ref[middle:] = total


def backward_kernel(tile, band, scale, *refs):
    part_mine, part_other, goal_ref, field_ref = refs[:4]
    fold_even, fold_odd, drop_even, drop_odd, kern_re_ref, kern_im_ref = refs[4:-2]
    resist_ref, back_ref = refs[-2:]
    middle = tile // 2
    intensity = part_mine[...] + part_other[...]
    resist = 1.0 / (1.0 + jnp.exp(-STEEP * (intensity - LEVEL)))
    resist_ref[...] = resist
    weight = 2.0 * (resist - goal_ref[...]) * STEEP * resist * (1.0 - resist)
    ahead_weight, mirrored_weight = (weight[:middle], weight[middle:])
    back_re = jnp.zeros((band, band), F32)
    back_im = jnp.zeros((band, band), F32)
    kernels = kern_re_ref.shape[0]

    def folded(k):
        near_re, near_im = (ahead_weight * field_ref[k, i] for i in range(2))
        far_re, far_im = (mirrored_weight * field_ref[k, i] for i in range(2, 4))
        columns = []
        for even, odd in (
            (near_re + far_re, near_im - far_im),
            (near_im + far_im, far_re - near_re),
        ):
            even = product(fold_even[...], jnp.concatenate(split(even), axis=0))
            odd = product(fold_odd[...], jnp.concatenate(split(odd), axis=0))
            even = even[: band // 2] + even[band // 2 :]
            odd = odd[: band // 2] + odd[band // 2 :]
            columns += [even + odd, even - odd]
        return jnp.concatenate(columns, axis=0)

    def dropped(value, table):
        pair = product(jnp.concatenate(split(value), axis=1), table[...])
        return pair[:, :band] + pair[:, band:]

    ahead = folded(0)
    for k in range(kernels):
        rows = ahead
        if k + 1 < kernels:
            ahead = folded(k + 1)
        even = dropped(rows[:, :middle] + rows[:, middle:], drop_even)
        odd = dropped(rows[:, :middle] - rows[:, middle:], drop_odd)
        part_re = even[:band] + odd[band:]
        part_im = even[band:] - odd[:band]
        kern_re, kern_im = (kern_re_ref[k], kern_im_ref[k])
        back_re = back_re + (kern_re * part_re + kern_im * part_im)
        back_im = back_im + (kern_re * part_im - kern_im * part_re)
    back_ref[...] = jnp.concatenate([back_re, back_im], axis=1) * scale


def margin_kernel(turns, tile, band, *refs):
    back_mine, back_other, c_high, c_low, m_high, m_low, back_ref, row_ref = refs[:8]
    place = Place()
    back = 2.0 * (back_mine[...] + back_other[...])
    back_ref[...] = back

    def strip_rows(ref):
        picked = [
            jnp.where(place.down, ref[base : base + HALO], ref[base + HALO : base + 2 * HALO])
            for base in (0, 2 * HALO)
        ]
        return jnp.concatenate(picked, axis=0)

    lift = dot((strip_rows(whole(m_high[...])), strip_rows(whole(m_low[...]))), split(back), product_turned)
    lift = jnp.concatenate([lift[:HALO], lift[HALO:]], axis=1)
    strip = dot(split(lift), (c_high[...], c_low[...]))
    row_ref[...] = strip[:, :tile]
    for turn in range(turns):
        upper = jnp.logical_not(place.rightward(turn))
        refs[8 + turn][...] = pack(strip[:, tile:], upper)


def side_kernel(turns, tile, band, *refs):
    back_ref, c_high, c_low, r_high, r_low, lift_ref = refs[:6]
    place = Place()
    lift = dot((whole(r_high[...]), whole(r_low[...])), split(back_ref[...]), product_turned)
    lift = jnp.concatenate([lift[:tile], lift[tile:]], axis=1)
    lift_ref[...] = lift
    if turns:
        side = dot(split(lift), (c_high[:, tile:], c_low[:, tile:]))
        for turn in range(turns):
            refs[6 + turn][...] = pack(side, jnp.logical_not(place.rightward(turn)))


def core_kernel(tile, lift_ref, c_high, c_low, core_ref):
    core_ref[...] = dot(split(lift_ref[...]), (c_high[:, :tile], c_low[:, :tile]))


def resist_kernel(resist_ref, order, out_ref):
    high, low = split(resist_ref[...])
    turned = product(high, order[...]) + product(low, order[...])
    high, low = split(turned.T)
    out_ref[...] = product(high, order[...]) + product(low, order[...])


def spread_sides(place, refs, tile):
    merged = merge_sides(place, refs, True)
    lane = lax.broadcasted_iota(jnp.int32, merged.shape, 1)
    first = jnp.where(lane < HALO, merged, 0.0)
    last = jnp.where(lane >= HALO, merged, 0.0)
    middle = jnp.zeros((merged.shape[0], tile - 2 * merged.shape[1]), F32)
    return jnp.concatenate([first, middle, last] if middle.shape[1] else [first, last], axis=1)


def add_corners_kernel(turns, row_ref, *refs):
    place = Place()
    refs[turns][...] = row_ref[...] + spread_sides(place, refs[:turns], row_ref.shape[1])


def merge_kernel(turns, tile, core_ref, row_mine, row_other, *refs):
    place = Place()
    total = core_ref[...]
    if turns:
        total = total + spread_sides(place, refs[:turns], tile)
    mine, other = (row_mine[...], row_other[...])
    out_ref = refs[turns]
    bottom = jnp.where(place.has_below, jnp.where(place.down, mine, other), 0.0)
    top = jnp.where(place.has_above, jnp.where(place.down, other, mine), 0.0)
    out_ref[:HALO] = total[:HALO] + top
    out_ref[HALO : tile - HALO] = total[HALO : tile - HALO]
    out_ref[tile - HALO :] = total[tile - HALO :] + bottom


def call(kernel, out_shape, operands, in_hbm=(), **options):
    in_vmem = pl.BlockSpec(memory_space=pltpu.VMEM)
    anywhere = pl.BlockSpec(memory_space=pltpu.HBM)
    operands = [
        pltpu.with_memory_space_constraint(operand, pltpu.HBM) if i in in_hbm else operand
        for i, operand in enumerate(operands)
    ]
    return pl.pallas_call(
        kernel,
        out_shape=out_shape,
        in_specs=[anywhere if i in in_hbm else in_vmem for i in range(len(operands))],
        out_specs=jax.tree.map(lambda _: in_vmem, out_shape),
        compiler_params=pltpu.CompilerParams(vmem_limit_bytes=VMEM_LIMIT),
        **options,
    )(*operands)


def exchange(row, sides, corners, beside, join, joined_rows):
    turns = side_turns()
    row = swap_rows(row)
    corners = [swap_rows(corners[turn], turn) for turn in range(turns)]
    sides = [swap_side(sides[turn], turn) for turn in range(turns)]
    row, corners, beside = lax.optimization_barrier((row, corners, beside))
    if turns:
        joined = pltpu.VMEM((joined_rows, row.shape[1]), F32)
        row = call(
            functools.partial(join, turns), joined, [row, *corners], cost_estimate=cost(4 << 30)
        )
    return ([row, swap_cores(row), *sides], beside)


def on_device(mask, target, spectra):
    tile = mask.shape[0]
    band = spectra.shape[-1]
    window = tile + 2 * HALO
    scale = 1.0 / (window * window)
    turns = side_turns()
    image = pltpu.VMEM((tile, tile), F32)
    row_strip = pltpu.VMEM((HALO, tile), F32)
    side_strips = [pltpu.VMEM((tile // 2, 2 * HALO), F32)] * turns
    corner_strips = [pltpu.VMEM((HALO // 2, 2 * HALO), F32)] * turns
    wide = pltpu.VMEM((band, 2 * band), F32)

    row, *packed = call(
        functools.partial(prepare_kernel, turns, tile),
        (row_strip, *side_strips, *corner_strips),
        [mask],
    )
    tables = {
        name: [jnp.asarray(t) for t in group] for name, group in make_tables(band, tile).items()
    }
    row, mask = lax.optimization_barrier((row, mask))
    sources = [*tables["window"], target, spectra, *tables["forward"]]
    kept = sources[:3] + sources[4:]
    turned = pltpu.VMEM(spectra.shape[1:], F32)
    part, goal, ordered_re, *shared = call(
        functools.partial(own_kernel, tile, len(sources)),
        (
            pltpu.VMEM((2 * band, tile), F32),
            image,
            turned,
            *[pltpu.VMEM(source.shape, source.dtype) for source in kept],
        ),
        [mask, *sources],
        in_hbm=range(1, 1 + len(sources)),
        scratch_shapes=[
            pltpu.VMEM(target.shape, target.dtype),
            pltpu.SemaphoreType.DMA((len(sources),)),
        ],
    )
    columns, tile_order, order = (shared[0:2], shared[2], shared[4])
    own_rows, margin_rows = (shared[5:7], shared[7:9])
    (mine, other, *sides), (part, spectra) = exchange(
        row,
        packed[:turns],
        packed[turns:],
        (part, shared[3]),
        join_kernel,
        HALO + turns * HALO // 4,
    )
    ordered_im = call(order_kernel, turned, [spectra, order])
    part, ordered_im = lax.optimization_barrier((part, ordered_im))
    ordered = [ordered_re, ordered_im]
    spectrum = call(
        functools.partial(beside_kernel, turns, tile, band),
        wide,
        [part, *sides, *columns, *own_rows],
        cost_estimate=cost(3 << 30),
    )
    intensity, field = call(
        functools.partial(forward_kernel, turns, tile, band, scale),
        (image, pltpu.VMEM((spectra.shape[1], 4, tile // 2, tile), F32)),
        [
            spectrum,
            mine,
            other,
            *columns,
            *margin_rows,
            *shared[9:],
            *ordered,
        ],
    )
    sources = tables["backward"]
    backward = call(
        functools.partial(late_kernel, len(sources)),
        tuple(pltpu.VMEM(source.shape, source.dtype) for source in sources),
        [intensity, *sources],
        in_hbm=range(1, 1 + len(sources)),
        scratch_shapes=[pltpu.SemaphoreType.DMA((len(sources),))],
    )
    resist, back = call(
        functools.partial(backward_kernel, tile, band, scale),
        (image, wide),
        [intensity, swap_cores(intensity), goal, field, *backward, *ordered],
    )
    back, row, *corners = call(
        functools.partial(margin_kernel, turns, tile, band),
        (wide, row_strip, *corner_strips),
        [back, swap_cores(back), *columns, *margin_rows],
    )
    lift, *sides = call(
        functools.partial(side_kernel, turns, tile, band),
        (pltpu.VMEM((tile, 2 * band), F32), *side_strips),
        [back, *columns, *own_rows],
    )
    sides, resist = lax.optimization_barrier((sides, resist))
    resist = call(resist_kernel, jax.ShapeDtypeStruct((tile, tile), F32), [resist, tile_order])
    received, (lift, resist) = exchange(
        row, sides, corners, (lift, resist), add_corners_kernel, HALO
    )
    core = call(functools.partial(core_kernel, tile), image, [lift, *columns])
    grad = call(
        functools.partial(merge_kernel, turns, tile),
        jax.ShapeDtypeStruct((tile, tile), F32),
        [core, *received],
    )
    return (resist, grad)


def solution(mesh):
    return jax.shard_map(
        on_device,
        mesh=mesh,
        in_specs=(P("ty", "tx"), P("ty", "tx"), P(None, "kern", None, None)),
        out_specs=(P("ty", "tx"), P("ty", "tx")),
        check_vma=False,
    )
```
